32 devices in a mesh: rows: 16 (over z, x, core), mlp: 2 (over y).
Axes of the slice: x: 2, y: 2, z: 4, core: 2. Of those that a mesh axis runs over, the one named last changes fastest.
Arguments:
- tokens: bfloat16 [65536, 512], P(('rows', 'mlp')), may hold values from -6 to 6
- segment_ids: int32 [512, 128], P(('rows', 'mlp')), may hold values from 0 to 7, never falling along the last dimension, each value on 1 to 64 neighbouring positions
- ln1_gain: bfloat16 [512], replicated, may hold values from 0.099609375 to 1.8984375
- ln1_bias: bfloat16 [512], replicated, may hold values from -3 to 3
- qkv_weight: bfloat16 [512, 1536], replicated, may hold values from -0.25 to 0.25
- qv_bias: bfloat16 [2, 512], replicated, may hold values from -3 to 3
- out_weight: bfloat16 [512, 512], replicated, may hold values from -1 to 1
- out_bias: bfloat16 [512], replicated, may hold values from -3 to 3
- ln2_gain: bfloat16 [512], replicated, may hold values from 0.099609375 to 1.8984375
- ln2_bias: bfloat16 [512], replicated, may hold values from -3 to 3
- up_weight: bfloat16 [512, 2048], P(None, 'mlp'), may hold values from -0.25 to 0.25
- up_bias: bfloat16 [2048], P('mlp'), may hold values from -3 to 3
- down_weight: bfloat16 [2048, 512], P('mlp'), may hold values from -0.125 to 0.125
- down_bias: bfloat16 [512], replicated, may hold values from -3 to 3
- out_grad: bfloat16 [65536, 512], P(('rows', 'mlp')), may hold values from -6 to 6
Outputs:
- layer_out: bfloat16 [65536, 512], P(('rows', 'mlp'))
- in_grad: bfloat16 [65536, 512], P(('rows', 'mlp'))
- grad_ln1_gain: float32 [512], replicated
- grad_ln1_bias: float32 [512], replicated
- grad_qkv_weight: float32 [512, 1536], replicated
- grad_qv_bias: float32 [2, 512], replicated
- grad_out_weight: float32 [512, 512], replicated
- grad_out_bias: float32 [512], replicated
- grad_ln2_gain: float32 [512], replicated
- grad_ln2_bias: float32 [512], replicated
- grad_up_weight: float32 [512, 2048], P(None, 'mlp')
- grad_up_bias: float32 [2048], P('mlp')
- grad_down_weight: float32 [2048, 512], P('mlp')
- grad_down_bias: float32 [512], replicated
The draws below stay inside these ranges and needn't reach their ends.
Inputs may be any that keep to these rules, and one draw needn't show every extreme that they name: `segment_ids`: within each packed row the ids never fall; each episode fragment holds 1 to 64 tokens, and some fragment holds exactly 64.
All inputs are finite; a program needn't handle non-finite values.
Results may differ from the reference program's by a relative error of at most 0.011.
Values may be sent and summed in bfloat16 or wider, within the bound.
No kernel may reach another device: no remote copies, remote signals or barrier semaphores. Data moves between devices by JAX's collectives and lax.ppermute only.
A program may use at most 192 MiB of HBM per device.

```python
import math
import jax
import jax.numpy as jnp
import numpy as np
from jax import lax

D = 512
HEADS = 8
HEAD_DIM = 64
FF = 2048
SEQ = 128
FRAME = 4
MOSTSEG = 64
TOKENS = 65536
NSEQ = 512


def steps_of(own_key, extent, pieces, smallest, top_value):
    loudness, own = 1.0, jax.random.fold_in(own_key, 6)
    for position, shards_of in pieces:
        draws = jnp.exp(jax.random.uniform(jax.random.fold_in(own, position), (shards_of,), jnp.float32, smallest / len(pieces), top_value / len(pieces)))
        loudness = loudness * jnp.repeat(draws, extent[position] // shards_of).reshape([-1 if axis == position else 1 for axis in range(len(extent))])
    return loudness


def length_profile(amount, total, bound, skew):
    portions = [(1 << 20) // math.isqrt(grade ** skew) + 1 for grade in range(2, amount + 1)]
    rest, holding = total - bound - (amount - 1), [1] * (amount - 1)
    while rest > 0:
        candidates = [i for i in range(amount - 1) if holding[i] < bound]
        mass, budget = sum([portions[i] for i in candidates]), rest
        for i in candidates:
            addition = min(bound - holding[i], max(1, budget * portions[i] // mass), rest)
            holding[i] = holding[i] + addition
            rest = rest - addition
    return np.array([bound] + holding)


def uneven_parts(stream_key, amount, total, most, skew):
    if amount == 2:
        one = jax.random.randint(stream_key, (), max(1, total - most), min(most, total - 1) + 1)
        return jnp.stack([one, total - one])
    lengths = jnp.asarray(length_profile(amount, total, most, skew), jnp.int32)
    couples = (amount - 1) // 2
    donor, receiver = lengths[1:1 + 2 * couples:2], lengths[2:2 + 2 * couples:2]
    room = jnp.minimum(donor - 1, most - receiver)
    passed = jax.random.randint(jax.random.fold_in(stream_key, 1), (couples,), 0, 1 << 20) % (room + 1)
    lengths = lengths.at[1:1 + 2 * couples:2].set(donor - passed).at[2:2 + 2 * couples:2].set(receiver + passed)
    return lengths[jax.random.permutation(jax.random.fold_in(stream_key, 2), amount)]


def noise(key, extent, width, bound, pieces=(), kind=jnp.bfloat16):
    entries = jax.random.normal(key, extent, jnp.float32) * width
    if len(pieces) > 0:
        entries = steps_of(key, extent, pieces, -0.22, 0.18) * entries
    return jnp.clip(entries, min=-bound, max=bound).astype(kind)


def setup_inputs(seed: int = 0) -> dict:
    splits = jax.random.split(jax.random.key(seed), 16)
    tokens = noise(splits[0], (TOKENS, D), 1.0, 6.0, ((0, 32),))
    segment_ids = jax.vmap(lambda own: jnp.searchsorted(jnp.cumsum(uneven_parts(own, 8, SEQ, MOSTSEG, 0)), jnp.arange(SEQ), side="right"))(jax.random.split(splits[1], NSEQ)).reshape((NSEQ, SEQ)).astype(jnp.int32)
    ln1_gain = jnp.clip(1.0 + 0.18 * jax.random.normal(splits[2], (D,), jnp.float32), 0.099609375, 1.8984375).astype(jnp.bfloat16)
    ln1_bias = noise(splits[3], (D,), 0.3, 3.0)
    qkv_weight = noise(splits[4], (D, 3 * D), D ** -0.5, 0.25)
    qv_bias = noise(splits[5], (2, D), 0.5, 3.0)
    out_weight = noise(splits[6], (D, D), (D // 16) ** -0.5, 1.0)
    out_bias = noise(splits[7], (D,), 0.5, 3.0)
    ln2_gain = jnp.clip(1.0 + 0.18 * jax.random.normal(splits[8], (D,), jnp.float32), 0.099609375, 1.8984375).astype(jnp.bfloat16)
    ln2_bias = noise(splits[9], (D,), 0.3, 3.0)
    up_weight = noise(splits[10], (D, FF), D ** -0.5, 0.25, ((1, 2),))
    up_bias = noise(splits[11], (FF,), 0.5, 3.0, ((0, 2),))
    down_weight = noise(splits[12], (FF, D), FF ** -0.5, 0.125, ((0, 2),))
    down_bias = noise(splits[13], (D,), 0.5, 3.0)
    out_grad = noise(splits[14], (TOKENS, D), 1.0, 6.0, ((0, 32),))
    return dict(tokens=tokens, segment_ids=segment_ids, ln1_gain=ln1_gain, ln1_bias=ln1_bias, qkv_weight=qkv_weight, qv_bias=qv_bias, out_weight=out_weight, out_bias=out_bias, ln2_gain=ln2_gain, ln2_bias=ln2_bias, up_weight=up_weight, up_bias=up_bias, down_weight=down_weight, down_bias=down_bias, out_grad=out_grad)


norm_eps = 1e-05

@jax.custom_vjp
def low(v):
    return lax.optimization_barrier(v.astype(jnp.bfloat16)).astype(jnp.float32)

@jax.custom_vjp
def low_back(v):
    return v

def low_keep(v):
    return (low(v), None)

def low_pass(kept, grad):
    return (grad,)

def back_keep(v):
    return (v, None)

def back_low(kept, grad):
    return (low(grad),)
low.defvjp(low_keep, low_pass)
low_back.defvjp(back_keep, back_low)

def smooth_gate(value):
    return jax.nn.gelu(value, approximate=True)

def layer_norm(value, gain, shift):
    center = value - lax.optimization_barrier(jnp.mean(value, axis=-1, keepdims=True))
    spread = lax.optimization_barrier(jnp.mean(center * center, axis=-1, keepdims=True))
    return center * lax.rsqrt(spread + norm_eps) * gain + shift

def forward(params, block, segments):
    gain_one, shift_one, qkv_w, qv_shift, out_w, out_shift, gain_two, shift_two, up_w, up_shift, down_w, down_shift = params
    exact = lax.Precision.HIGHEST
    count = block.shape[0]
    nrows_blk = count // SEQ
    scale = 1.0 / math.sqrt(HEAD_DIM)
    normed = low(layer_norm(block, gain_one, shift_one))
    joined = jnp.dot(normed, qkv_w, precision=exact)
    query = low(low_back(joined[:, :D] + qv_shift[0]))
    keys = low(low_back(joined[:, D:2 * D]))
    values = low(low_back(joined[:, 2 * D:] + qv_shift[1]))
    shape_four = (nrows_blk, SEQ, HEADS, HEAD_DIM)
    scores = jnp.einsum('gqhd,gkhd->ghqk', query.reshape(shape_four), keys.reshape(shape_four), precision=exact) * scale
    frames = jnp.arange(SEQ) // FRAME
    allow = (segments[:, :, None] == segments[:, None, :]) & (frames[:, None] >= frames[None, :])[None]
    scores = low_back(jnp.where(allow[:, None], scores, -1000000000.0))
    probs = jax.nn.softmax(scores, axis=-1)
    context = jnp.einsum('ghqk,gkhd->gqhd', low(probs), values.reshape(shape_four), precision=exact).reshape(count, D)
    context = low(low_back(context))
    attended = low_back(jnp.dot(context, out_w, precision=exact) + out_shift)
    resid = block + attended
    normed_two = low(layer_norm(resid, gain_two, shift_two))
    hidden = low_back(jnp.dot(normed_two, up_w, precision=exact) + up_shift)
    gated = low(smooth_gate(hidden))
    return resid + jnp.dot(gated, down_w, precision=exact) + down_shift

def reference(tokens, segment_ids, ln1_gain, ln1_bias, qkv_weight, qv_bias, out_weight, out_bias, ln2_gain, ln2_bias, up_weight, up_bias, down_weight, down_bias, out_grad):
    params = tuple((a.astype(jnp.float32) for a in (ln1_gain, ln1_bias, qkv_weight, qv_bias, out_weight, out_bias, ln2_gain, ln2_bias, up_weight, up_bias, down_weight, down_bias)))
    block_len = math.gcd(TOKENS, 4096)
    nblocks = TOKENS // block_len
    inputs = tokens.astype(jnp.float32).reshape(nblocks, block_len, D)
    segs = segment_ids.reshape(nblocks, block_len // SEQ, SEQ)
    cotans = out_grad.astype(jnp.float32).reshape(nblocks, block_len, D)

    def step(acc, items):
        block, seg_blk, cotan = items
        result, pull = jax.vjp(lambda prm, inp: forward(prm, inp, seg_blk), params, block)
        grad_params, grad_in = pull(cotan)
        acc = jax.tree.map(lambda a, b: a + b, acc, grad_params)
        return (acc, (result.astype(jnp.bfloat16), grad_in.astype(jnp.bfloat16)))
    zeros = jax.tree.map(jnp.zeros_like, params)
    sums, (outputs, in_grads) = lax.scan(step, zeros, (inputs, segs, cotans))
    return (outputs.reshape(TOKENS, D), in_grads.reshape(TOKENS, D), sums[0], sums[1], sums[2], sums[3], sums[4], sums[5], sums[6], sums[7], sums[8], sums[9], sums[10], sums[11])
```

```python
import functools
import math

import jax
import jax.numpy as jnp
from jax import lax
from jax.experimental import pallas as pl
from jax.experimental.pallas import tpu as pltpu
from jax.sharding import PartitionSpec as P

BF, F32 = jnp.bfloat16, jnp.float32
SEQ, HD, FRAME = 128, 64, 4
EPS = 1e-5
C0 = math.sqrt(2.0 / math.pi)
C1 = C0 * 0.044715
LIMIT = 56 * 1024 * 1024
BOTH = ("rows", "mlp")


def mm(a, b, ca=1, cb=0):
    return lax.dot_general(a, b, (((ca,), (cb,)), ((), ())), preferred_element_type=F32)


def layer_norm(x):
    c = x - jnp.mean(x, axis=-1, keepdims=True)
    inv = lax.rsqrt(jnp.mean(c * c, axis=-1, keepdims=True) + EPS)
    return c * inv, inv


def norm_back(grad, normed, inv, gain):
    s = grad * gain
    return inv * (
        s
        - jnp.mean(s, axis=-1, keepdims=True)
        - normed * jnp.mean(s * normed, axis=-1, keepdims=True)
    )


def fold(v):
    return jnp.sum(v.reshape(-1, 8, v.shape[-1]), axis=0)


def stack_heads(v):
    low = lax.broadcasted_iota(jnp.int32, v.shape, 1) < HD
    zero = jnp.zeros_like(v)
    return jnp.concatenate([jnp.where(low, v, zero), jnp.where(low, zero, v)], axis=0)


def allowed_of(seg_row, transposed):
    wide = jnp.broadcast_to(seg_row.astype(F32), (SEQ, SEQ))
    same = wide == wide.T
    a = lax.broadcasted_iota(jnp.int32, (SEQ, SEQ), 1 if transposed else 0)
    b = lax.broadcasted_iota(jnp.int32, (SEQ, SEQ), 0 if transposed else 1)
    return same & (a // FRAME >= b // FRAME)


def whole(a):
    zeros = (0,) * len(a.shape)
    return pl.BlockSpec(a.shape, lambda i, *_: zeros)


def rows_spec(r, w):
    return pl.BlockSpec((r, w), lambda i, *_: (i, 0))


def shape(s, dtype):
    return jax.ShapeDtypeStruct(s, dtype)


def cost(macs, nbytes=0):
    return pl.CostEstimate(flops=2 * macs, bytes_accessed=nbytes, transcendentals=0)


def attn_fwd_body(tok, seg, g1, b1, wqkv, bqkv, wo, bo, g2, b2, joined_o, ctx_o, resid_o, h2_o):
    rows, width = tok.shape
    x = tok[...].astype(F32)
    n1, _ = layer_norm(x)
    h1 = (n1 * g1[...].astype(F32) + b1[...].astype(F32)).astype(BF)
    joined = (mm(h1, wqkv[...]) + bqkv[...].astype(F32)).astype(BF)
    joined_o[...] = joined
    parts = []
    for s in range(rows // SEQ):
        ok = allowed_of(seg[0, s : s + 1, :], False)
        r = slice(s * SEQ, (s + 1) * SEQ)
        outs = []
        for p in range(width // 128):
            q = joined[r, p * 128 : (p + 1) * 128] * BF(0.125)
            k = joined[r, width + p * 128 : width + (p + 1) * 128]
            v = joined[r, 2 * width + p * 128 : 2 * width + (p + 1) * 128]
            sc = mm(q, stack_heads(k), 1, 1)
            pr = []
            for h in range(2):
                t = jnp.where(ok, sc[:, h * 128 : (h + 1) * 128], -1e9)
                e = jnp.exp(t - jnp.max(t, axis=1, keepdims=True))
                pr.append((e * (1.0 / jnp.sum(e, axis=1, keepdims=True))).astype(BF))
            outs.append(mm(jnp.concatenate(pr, axis=1), stack_heads(v)).astype(BF))
        parts.append(jnp.concatenate(outs, axis=1))
    ctx = jnp.concatenate(parts, axis=0)
    ctx_o[...] = ctx
    resid = x + mm(ctx, wo[...]) + bo[...].astype(F32)
    resid_o[...] = resid
    n2, _ = layer_norm(resid)
    h2_o[...] = (n2 * g2[...].astype(F32) + b2[...].astype(F32)).astype(BF)


def attn_fwd(tok, seg, g1, b1, wqkv, bqkv, wo, bo, g2, b2, rows):
    t, d = tok.shape
    small = (g1, b1, wqkv, bqkv, wo, bo, g2, b2)
    return pl.pallas_call(
        attn_fwd_body,
        grid=(t // rows,),
        in_specs=[rows_spec(rows, d), pl.BlockSpec((1, rows // SEQ, SEQ), lambda i: (i, 0, 0))]
        + [whole(a) for a in small],
        out_specs=[rows_spec(rows, w) for w in (3 * d, d, d, d)],
        out_shape=[shape((t, 3 * d), BF), shape((t, d), BF), shape((t, d), F32), shape((t, d), BF)],
        compiler_params=pltpu.CompilerParams(vmem_limit_bytes=LIMIT),
        cost_estimate=cost(2 * t * d * 4 * d),
        name="attn_fwd",
    )(tok, seg.reshape(t // rows, rows // SEQ, SEQ), *small)


def ffn_chunk(hv, gv, h2t, gt, up, ub, dn):
    v = mm(hv, up) + ub
    v2 = v * v
    a = 0.5 + 0.5 * jnp.tanh(v * (C0 + C1 * v2))
    act = v * a
    slope = a + 2.0 * act * (1.0 - a) * (C0 + 3.0 * C1 * v2)
    gated = act.astype(BF)
    dhid = (mm(gv, dn, 1, 1) * slope).astype(BF)
    return mm(gated, dn), mm(dhid, up, 1, 1), mm(h2t, dhid), mm(gt, gated), fold(dhid.astype(F32))


def ffn_own_body(core, h2, g, up, ub, down, out_o, dh2_o, keep_o, send_o, gub_o, gup, gdn, gub):
    i = pl.program_id(0)
    d, f = up.shape
    half = f // 2

    @pl.when(i == 0)
    def _():
        gup[...] = jnp.zeros_like(gup)
        gdn[...] = jnp.zeros_like(gdn)
        gub[...] = jnp.zeros_like(gub)

    hv, gv = h2[...], g[...]
    h2t, gt = hv.T, gv.T
    out = dh2 = 0.0
    for c in range(2):
        s = slice(c * half, (c + 1) * half)
        o, dh, u, w, b = ffn_chunk(hv, gv, h2t, gt, up[:, s], ub[:, s].astype(F32), down[s, :])
        out, dh2 = out + o, dh2 + dh
        gup[c] += u
        gdn[c] += w
        gub[c] += b
    out_o[...] = out
    dh2_o[...] = dh2

    @pl.when(i == pl.num_programs(0) - 1)
    def _():
        c = core[0]
        keep_o[0] = gup[c].astype(BF)
        keep_o[1] = gdn[c].astype(BF)
        send_o[0] = gup[1 - c].astype(BF)
        send_o[1] = gdn[1 - c].astype(BF)
        gub_o[0:1] = jnp.sum(gub[0], axis=0, keepdims=True)
        gub_o[1:2] = jnp.sum(gub[1], axis=0, keepdims=True)


def ffn_own(core, h2, g, up, ub, down, rows):
    t, d = h2.shape
    f = up.shape[1]
    half = f // 2
    outs = [shape((t, d), F32), shape((t, d), F32), shape((2, d, half), BF), shape((2, d, half), BF), shape((2, half), F32)]
    return pl.pallas_call(
        ffn_own_body,
        grid_spec=pltpu.PrefetchScalarGridSpec(
            num_scalar_prefetch=1,
            grid=(t // rows,),
            in_specs=[rows_spec(rows, d), rows_spec(rows, d), whole(up), whole(ub), whole(down)],
            out_specs=[rows_spec(rows, d), rows_spec(rows, d)] + [whole(o) for o in outs[2:]],
            scratch_shapes=[pltpu.VMEM((2, d, half), F32), pltpu.VMEM((2, d, half), F32), pltpu.VMEM((2, 8, half), F32)],
        ),
        out_shape=outs,
        compiler_params=pltpu.CompilerParams(vmem_limit_bytes=LIMIT),
        cost_estimate=cost(2 * 6 * t * d * f),
        name="ffn_own",
    )(core, h2, g, up, ub, down)


def ffn_other_body(
    h2, g, w_send, w_keep, out_p, dh2_p, resid, ctx, wo, g2, b2,
    layer_o, dattn_o, dctx_o, keep_o, send_o, gub_o, gout_o, vec_o, gup, gdn, gub, gout, vec,
):
    i = pl.program_id(0)
    d = h2.shape[1]

    @pl.when(i == 0)
    def _():
        for a in (gup, gdn, gub, gout, vec):
            a[...] = jnp.zeros_like(a)

    hv, gv = h2[...], g[...]
    h2t, gt = hv.T, gv.T
    out, dh2 = out_p[...], dh2_p[...]
    for c, w in enumerate((w_send, w_keep)):
        ub = w[2 * d : 2 * d + 8, :].astype(F32)[0:1]
        o, dh, u, wd, b = ffn_chunk(hv, gv, h2t, gt, w[0:d, :], ub, w[d : 2 * d, :])
        out, dh2 = out + o, dh2 + dh
        gup[c] += u
        gdn[c] += wd
        gub[c] += b
    res = resid[...]
    layer_o[...] = (res + out + b2[...].astype(F32)).astype(BF)
    n2, inv2 = layer_norm(res)
    gf = gv.astype(F32)
    dattn = (gf + norm_back(dh2, n2, inv2, g2[...].astype(F32))).astype(BF)
    dattn_o[...] = dattn
    dctx_o[...] = mm(dattn, wo[...], 1, 1).astype(BF)
    gout[...] += mm(ctx[...].T, dattn)
    vec[0] += fold(dattn.astype(F32))
    vec[1] += fold(dh2 * n2)
    vec[2] += fold(dh2)
    vec[3] += fold(gf)

    @pl.when(i == pl.num_programs(0) - 1)
    def _():
        send_o[0] = gup[0].astype(BF)
        send_o[1] = gdn[0].astype(BF)
        keep_o[0] = gup[1].astype(BF)
        keep_o[1] = gdn[1].astype(BF)
        for c in range(2):
            gub_o[c : c + 1] = jnp.sum(gub[c], axis=0, keepdims=True)
        gout_o[...] = gout[...].astype(BF)
        for c in range(4):
            vec_o[c : c + 1] = jnp.sum(vec[c], axis=0, keepdims=True)


def ffn_other(h2, g, w_send, w_keep, out_p, dh2_p, resid, ctx, wo, g2, b2, rows):
    t, d = h2.shape
    half = d
    outs = [shape((t, d), BF)] * 3 + [
        shape((2, d, half), BF), shape((2, d, half), BF), shape((2, half), F32), shape((d, d), BF), shape((4, d), F32),
    ]
    return pl.pallas_call(
        ffn_other_body,
        grid=(t // rows,),
        in_specs=[rows_spec(rows, d), rows_spec(rows, d), whole(w_send), whole(w_keep)]
        + [rows_spec(rows, d)] * 4
        + [whole(wo), whole(g2), whole(b2)],
        out_specs=[rows_spec(rows, d)] * 3 + [whole(o) for o in outs[3:]],
        out_shape=outs,
        scratch_shapes=[
            pltpu.VMEM((2, d, half), F32), pltpu.VMEM((2, d, half), F32), pltpu.VMEM((2, 8, half), F32),
            pltpu.VMEM((d, d), F32), pltpu.VMEM((4, 8, d), F32),
        ],
        compiler_params=pltpu.CompilerParams(vmem_limit_bytes=LIMIT),
        cost_estimate=cost(2 * (6 * t * d * 2 * half + 2 * t * d * d)),
        name="ffn_other",
    )(h2, g, w_send, w_keep, out_p, dh2_p, resid, ctx, wo, g2, b2)


def attn_bwd_body(place, joined, dctx, seg, tok, wqkv, gout, gub_own, gub_other, vec, dj_o, pay_o, acc, cs, small):
    i = pl.program_id(0)
    rows, width = tok.shape

    @pl.when(i == 0)
    def _():
        acc[...] = jnp.zeros_like(acc)
        cs[...] = jnp.zeros_like(cs)

    n1, _ = layer_norm(tok[...].astype(F32))
    n1t = n1.astype(BF).T
    seqs = []
    for s in range(rows // SEQ):
        ok = allowed_of(seg[0, s : s + 1, :], True)
        r = slice(s * SEQ, (s + 1) * SEQ)
        dq, dk, dv = [], [], []
        for p in range(width // 128):
            q = joined[r, p * 128 : (p + 1) * 128] * BF(0.125)
            k = joined[r, width + p * 128 : width + (p + 1) * 128]
            v = joined[r, 2 * width + p * 128 : 2 * width + (p + 1) * 128]
            qs = stack_heads(q)
            dc = stack_heads(dctx[r, p * 128 : (p + 1) * 128])
            sc = mm(k, qs, 1, 1)
            dp = mm(v, dc, 1, 1)
            pb, ds = [], []
            for h in range(2):
                hs = slice(h * 128, (h + 1) * 128)
                t = jnp.where(ok, sc[:, hs], -1e9)
                e = jnp.exp(t - jnp.max(t, axis=0, keepdims=True))
                pr = e * (1.0 / jnp.sum(e, axis=0, keepdims=True))
                dph = dp[:, hs]
                ds.append((pr * (dph - jnp.sum(pr * dph, axis=0, keepdims=True))).astype(BF))
                pb.append(pr.astype(BF))
            dv.append(mm(jnp.concatenate(pb, axis=1), dc).astype(BF))
            dk.append(mm(jnp.concatenate(ds, axis=1), qs).astype(BF))
            dq.append((mm(jnp.concatenate(ds, axis=0), stack_heads(k), 0, 0) * 0.125).astype(BF))
        seqs.append(jnp.concatenate(dq + dk + dv, axis=1))
    dj = jnp.concatenate(seqs, axis=0)
    dj_o[...] = dj
    acc[...] += mm(n1t, dj)
    cs[...] += fold(dj.astype(F32))

    @pl.when(i == pl.num_programs(0) - 1)
    def _():
        w = wqkv[...]
        weighted = (acc[...] * w.astype(F32)).astype(BF)
        ones = jnp.ones((8, 3 * width), BF)
        total = jnp.sum(cs[...], axis=0, keepdims=True)
        part = cs[...]
        hi = part.astype(BF)
        lo = (part - hi.astype(F32)).astype(BF)
        small[...] = jnp.zeros_like(small)
        small[0:1] = mm(ones, weighted, 1, 1)[0:1]
        small[1:2] = jnp.sum(mm(hi, w, 1, 1) + mm(lo, w, 1, 1), axis=0, keepdims=True)
        for j in range(3):
            small[2 + j : 3 + j] = total[:, j * width : (j + 1) * width]
        for j in range(4):
            small[5 + j : 6 + j] = vec[j : j + 1, :]
        y, c = place[0], place[1]
        for j in range(2):
            small[pl.ds(16 + 2 * y + j, 1)] = gub_own[j : j + 1, :]
        small[pl.ds(16 + 2 * (1 - y) + 1 - c, 1)] = gub_other[0:1, :]
        small[pl.ds(16 + 2 * (1 - y) + c, 1)] = gub_other[1:2, :]
        pay_o[0, 0:width] = acc[:, 0:width].astype(BF)
        pay_o[0, width : 2 * width] = acc[:, width : 2 * width].astype(BF)
        pay_o[0, 2 * width :] = small[...].astype(BF)
        pay_o[1, 0:width] = acc[:, 2 * width :].astype(BF)
        pay_o[1, width : 2 * width] = gout[...]
        pay_o[1, 2 * width :] = jnp.zeros((32, width), BF)


def attn_bwd(place, joined, dctx, seg, tok, wqkv, gout, gub_own, gub_other, vec, rows):
    t, d = tok.shape
    outs = [shape((t, 3 * d), BF), shape((2, 2 * d + 32, d), BF)]
    rest = (wqkv, gout, gub_own, gub_other, vec)
    return pl.pallas_call(
        attn_bwd_body,
        grid_spec=pltpu.PrefetchScalarGridSpec(
            num_scalar_prefetch=1,
            grid=(t // rows,),
            in_specs=[
                rows_spec(rows, 3 * d),
                rows_spec(rows, d),
                pl.BlockSpec((1, rows // SEQ, SEQ), lambda i, *_: (i, 0, 0)),
                rows_spec(rows, d),
            ]
            + [whole(a) for a in rest],
            out_specs=[rows_spec(rows, 3 * d), whole(outs[1])],
            scratch_shapes=[pltpu.VMEM((d, 3 * d), F32), pltpu.VMEM((8, 3 * d), F32), pltpu.VMEM((32, d), F32)],
        ),
        out_shape=outs,
        compiler_params=pltpu.CompilerParams(vmem_limit_bytes=LIMIT),
        cost_estimate=cost(2 * t * d * 5 * d),
        name="attn_bwd",
    )(place, joined, dctx, seg.reshape(t // rows, rows // SEQ, SEQ), tok, *rest)


def in_grad_body(dj, tok, dattn, wqkv, g1, out_o):
    dh1 = mm(dj[...], wqkv[...], 1, 1)
    n1, inv1 = layer_norm(tok[...].astype(F32))
    out_o[...] = (dattn[...].astype(F32) + norm_back(dh1, n1, inv1, g1[...].astype(F32))).astype(BF)


def in_grad_of(dj, tok, dattn, wqkv, g1, rows):
    t, d = tok.shape
    return pl.pallas_call(
        in_grad_body,
        grid=(t // rows,),
        in_specs=[rows_spec(rows, 3 * d), rows_spec(rows, d), rows_spec(rows, d), whole(wqkv), whole(g1)],
        out_specs=rows_spec(rows, d),
        out_shape=shape((t, d), BF),
        compiler_params=pltpu.CompilerParams(vmem_limit_bytes=LIMIT),
        cost_estimate=cost(2 * t * d * 3 * d),
        name="in_grad",
    )(dj, tok, dattn, wqkv, g1)


def gray(u):
    return u ^ (u >> 1)


def gray_back(g):
    u = 0
    while g:
        u, g = u ^ g, g >> 1
    return u


def local(
    n_rows,
    tokens,
    segment_ids,
    ln1_gain,
    ln1_bias,
    qkv_weight,
    qv_bias,
    out_weight,
    out_bias,
    ln2_gain,
    ln2_bias,
    up_weight,
    up_bias,
    down_weight,
    down_bias,
    out_grad,
):
    t, d = tokens.shape
    half = up_weight.shape[1] // 2
    r, y = lax.axis_index("rows"), lax.axis_index("mlp")
    core = r & 1
    up_dims = n_rows.bit_length() - 2

    def flip(dim, row, m):
        if dim == "core":
            return row ^ 1, m
        if dim == "y":
            return row, m ^ 1
        if dim == 0:
            return row ^ 2, m
        return (gray_back(gray(row >> 2) ^ (1 << (dim - 1))) << 2) | (row & 3), m

    def bit(dim):
        if dim == "y":
            return y
        if dim == 0:
            return (r >> 1) & 1
        return (gray(r >> 2) >> (dim - 1)) & 1

    def swap(value, *dims):
        pairs = []
        for row in range(n_rows):
            for m in range(2):
                row2, m2 = flip(dims[0] if row & 1 == 0 else dims[-1], row, m)
                pairs.append((row * 2 + m, row2 * 2 + m2))
        return lax.ppermute(value, BOTH, pairs)

    def by_core(first, second):
        return jnp.where(core == 0, first, second)

    def pick(value, index):
        return lax.dynamic_index_in_dim(value, index, 0, keepdims=False)

    def add(a, b):
        return (a.astype(F32) + b.astype(F32)).astype(BF)

    def in_order(mine, other, v):
        return jnp.stack([jnp.where(v == 0, mine, other), jnp.where(v == 0, other, mine)])

    first = 1 - core
    bias_rows = jnp.broadcast_to(lax.dynamic_slice(up_bias, (first * half,), (half,))[None], (16, half))
    w_mine = jnp.concatenate(
        [
            lax.dynamic_slice(up_weight, (0, first * half), (d, half)),
            lax.dynamic_slice(down_weight, (first * half, 0), (half, d)),
            bias_rows,
        ],
        axis=0,
    )
    w_send = swap(w_mine, "y")
    w_keep = swap(w_send, "core")

    row = lambda a: a.reshape(1, -1)
    bqkv = jnp.concatenate([qv_bias[0], jnp.zeros((d,), BF), qv_bias[1]]).reshape(1, -1)
    joined, ctx, resid, h2 = attn_fwd(
        tokens, segment_ids, row(ln1_gain), row(ln1_bias), qkv_weight, bqkv, out_weight, row(out_bias),
        row(ln2_gain), row(ln2_bias), rows=512,
    )
    core_s = core.reshape(1).astype(jnp.int32)
    out_p, dh2_p, own_keep, own_send, gub_own = ffn_own(
        core_s, h2, out_grad, up_weight, row(up_bias), down_weight, rows=512
    )
    own = add(own_keep, swap(own_send, "core"))
    layer_out, dattn, dctx, oth_keep, oth_send, gub_oth, gout, vec = ffn_other(
        h2, out_grad, w_send, w_keep, out_p, dh2_p, resid, ctx, out_weight, row(ln2_gain), row(down_bias), rows=512
    )
    oth = add(oth_keep, swap(oth_send, "core"))
    place = jnp.stack([y, core]).astype(jnp.int32)
    dj, pay = attn_bwd(place, joined, dctx, segment_ids, tokens, qkv_weight, gout, gub_own, gub_oth, vec, rows=512)

    order0 = [0, "y"] + list(range(1, up_dims))
    order1 = ["y"] + list(range(1, up_dims)) + [0]
    v0 = bit(0)
    four = jnp.concatenate([own, oth], axis=0)
    k0, k1 = by_core(v0, 0), by_core(2 + v0, 1)
    s0, s1 = by_core(1 - v0, 2), by_core(3 - v0, 3)
    two = jnp.stack([pick(four, k0), pick(four, k1)])
    two = add(two, swap(jnp.stack([pick(four, s0), pick(four, s1)]), order0[0], order1[0]))
    v1 = by_core(0, bit(order1[1]))
    one = add(pick(two, v1), swap(pick(two, 1 - v1), order0[1], order1[1]))
    for a, b in zip(order0[2:], order1[2:]):
        one = add(one, swap(one, a, b))
    v2 = by_core(v0, bit(order1[1]))
    mine = in_order(one, swap(one, order0[0], order1[1]), v2)
    theirs = swap(mine, "core")
    both = in_order(mine, theirs, core)
    grad_up = jnp.concatenate([both[0, 0], both[1, 0]], axis=1).astype(F32)
    grad_down = jnp.concatenate([both[0, 1].T, both[1, 1].T], axis=0).astype(F32)

    part = add(pick(pay, core), swap(pick(pay, 1 - core), "core"))
    hr = part.shape[0] // 2
    part = part.reshape(2, hr, d)
    va = by_core(bit(order0[0]), bit(order1[0]))
    piece = add(pick(part, va), swap(pick(part, 1 - va), order0[0], order1[0]))
    for a, b in zip(order0[1:], order1[1:]):
        piece = add(piece, swap(piece, a, b))
    part = in_order(piece, swap(piece, order0[0], order1[0]), va).reshape(2 * hr, d)
    full = in_order(part, swap(part, "core"), core).astype(F32)

    in_grad = in_grad_of(dj, tokens, dattn, qkv_weight, row(ln1_gain), rows=512)

    small = full[0, 2 * d :]
    raw = jnp.concatenate([full[0, :d], full[0, d : 2 * d], full[1, :d]], axis=1)
    csum = small[2:5].reshape(1, 3 * d)
    grad_qkv = raw * ln1_gain.astype(F32)[:, None] + ln1_bias.astype(F32)[:, None] * csum
    gub = lax.dynamic_slice(small, (16 + 2 * y, 0), (2, d)).reshape(-1)
    return (
        layer_out,
        in_grad,
        small[0],
        small[1],
        grad_qkv,
        jnp.stack([small[2], small[4]]),
        full[1, d : 2 * d],
        small[5],
        small[6],
        small[7],
        grad_up,
        gub,
        grad_down,
        small[8],
    )


def solution(mesh):
    placed = (
        P(BOTH, None), P(BOTH, None), P(), P(), P(), P(), P(), P(), P(), P(),
        P(None, "mlp"), P("mlp"), P("mlp", None), P(), P(BOTH, None),
    )
    return jax.shard_map(
        functools.partial(local, mesh.shape["rows"]),
        mesh=mesh,
        in_specs=placed,
        out_specs=(
            P(BOTH, None), P(BOTH, None), P(), P(), P(), P(), P(), P(), P(), P(),
            P(None, "mlp"), P("mlp"), P("mlp", None), P(),
        ),
        check_vma=False,
    )
```

```python
import functools
import math

import jax
import jax.numpy as jnp
from jax import lax
from jax.experimental import pallas as pl
from jax.experimental.pallas import tpu as pltpu
from jax.sharding import PartitionSpec as P

BF, F32 = jnp.bfloat16, jnp.float32
SEQ, HD, FRAME = 128, 64, 4
EPS = 1e-5
C0 = math.sqrt(2.0 / math.pi)
C1 = C0 * 0.044715
LIMIT = 20 * 1024 * 1024
BOTH = ("rows", "mlp")
SCALE = 8


def mm(a, b, ca=1, cb=0):
    return lax.dot_general(a, b, (((ca,), (cb,)), ((), ())), preferred_element_type=F32)


def layer_norm(x):
    c = x - jnp.mean(x, axis=-1, keepdims=True)
    inv = lax.rsqrt(jnp.mean(c * c, axis=-1, keepdims=True) + EPS)
    return c * inv, inv


def norm_back(grad, normed, inv, gain):
    s = grad * gain
    return inv * (
        s
        - jnp.mean(s, axis=-1, keepdims=True)
        - normed * jnp.mean(s * normed, axis=-1, keepdims=True)
    )


def fold(v):
    return jnp.sum(v.reshape(-1, 8, v.shape[-1]), axis=0)


def stack_heads(v):
    low = lax.broadcasted_iota(jnp.int32, v.shape, 1) < HD
    zero = jnp.zeros_like(v)
    return jnp.concatenate([jnp.where(low, v, zero), jnp.where(low, zero, v)], axis=0)


def allowed_of(seg_row, transposed):
    wide = jnp.broadcast_to(seg_row.astype(F32), (SEQ, SEQ))
    same = wide == wide.T
    a = lax.broadcasted_iota(jnp.int32, (SEQ, SEQ), 1 if transposed else 0)
    b = lax.broadcasted_iota(jnp.int32, (SEQ, SEQ), 0 if transposed else 1)
    return same & (a // FRAME >= b // FRAME)


def whole(a):
    zeros = (0,) * len(a.shape)
    return pl.BlockSpec(a.shape, lambda i, *_: zeros)


def rows_spec(r, w):
    return pl.BlockSpec((r, w), lambda i, *_: (i, 0))


def shape(s, dtype):
    return jax.ShapeDtypeStruct(s, dtype)


def in_hbm(s, dtype):
    return pltpu.HBM(s, dtype)


def cost(macs, nbytes=0):
    return pl.CostEstimate(flops=macs // SCALE, bytes_accessed=nbytes // SCALE, transcendentals=0)


def slab(ref, r, c):
    return ref[r, c * 128 : (c + 1) * 128]


def attn_fwd_body(tok, seg, vecs, wqkv, wo, joined_o, ctx_o, resid_o, h2_o, n1t_o):
    rows, width = tok.shape
    pairs = width // 128
    vec = vecs[...].astype(F32)
    g1, b1, bo, g2, b2, bq, bv = (vec[j : j + 1] for j in range(7))
    x = tok[...].astype(F32)
    n1, _ = layer_norm(x)
    n1t_o[...] = n1.astype(BF).T
    h1 = (n1 * g1 + b1).astype(BF)
    bias = jnp.concatenate([bq, jnp.zeros_like(bq), bv], axis=1)
    joined = (mm(h1, wqkv[...]) + bias).astype(BF)
    joined_o[...] = joined
    group = 2
    done = []
    for s0 in range(0, rows // SEQ, group):
        items = [(s, p) for s in range(s0, s0 + group) for p in range(pairs)]
        allow = {s: allowed_of(seg[0, s : s + 1, :], True) for s in range(s0, s0 + group)}

        def part(s, o, p):
            return joined[s * SEQ : (s + 1) * SEQ, o * width + p * 128 : o * width + (p + 1) * 128]

        scores = [mm(part(s, 1, p), stack_heads(part(s, 0, p) * BF(0.125)), 1, 1) for s, p in items]
        probs = []
        for (s, p), sc in zip(items, scores):
            two = []
            for h in range(2):
                v = jnp.where(allow[s], sc[:, h * SEQ : (h + 1) * SEQ], -1e9)
                e = jnp.exp(v - jnp.max(v, axis=0, keepdims=True))
                two.append((e * (1.0 / jnp.sum(e, axis=0, keepdims=True))).astype(BF))
            probs.append(jnp.concatenate(two, axis=0))
        outs = [mm(pr, stack_heads(part(s, 2, p)), 0, 0).astype(BF) for (s, p), pr in zip(items, probs)]
        for j in range(group):
            done.append(jnp.concatenate(outs[j * pairs : (j + 1) * pairs], axis=1))
    ctx = jnp.concatenate(done, axis=0)
    ctx_o[...] = ctx
    resid = x + mm(ctx, wo[...]) + bo
    resid_o[...] = resid
    n2, _ = layer_norm(resid)
    h2_o[...] = (n2 * g2 + b2).astype(BF)


def attn_fwd(tok, seg, vecs, wqkv, wo, rows):
    t, d = tok.shape
    return pl.pallas_call(
        attn_fwd_body,
        grid=(t // rows,),
        in_specs=[rows_spec(rows, d), pl.BlockSpec((1, rows // SEQ, SEQ), lambda i: (i, 0, 0))]
        + [whole(a) for a in (vecs, wqkv, wo)],
        out_specs=[rows_spec(rows, w) for w in (3 * d, d, d, d)] + [pl.BlockSpec((d, rows), lambda i: (0, i))],
        out_shape=[in_hbm((t, 3 * d), BF), in_hbm((t, d), BF), in_hbm((t, d), F32), shape((t, d), BF), in_hbm((d, t), BF)],
        compiler_params=pltpu.CompilerParams(vmem_limit_bytes=LIMIT),
        cost_estimate=cost(3 * t * d * 4 * d),
        name="attn_fwd",
    )(tok, seg.reshape(t // rows, rows // SEQ, SEQ), vecs, wqkv, wo)


def ffn_block(hv, gv, up, ub, down, chunk, gated_o, gup, gdn, gub):
    d, f = up.shape
    cuts = [slice(c * chunk, (c + 1) * chunk) for c in range(f // chunk)]
    ahead = [(mm(hv, up[:, s]), mm(gv, down[s, :], 1, 1)) for s in cuts]
    gates, slopes = [], []
    for s, (v, dg) in zip(cuts, ahead):
        v = v + ub[:, s]
        v2 = v * v
        a = 0.5 + 0.5 * jnp.tanh(v * (C0 + C1 * v2))
        act = v * a
        slope = a + act * (1.0 - a) * (2.0 * C0 + 6.0 * C1 * v2)
        dh = (dg * slope).astype(BF)
        gates.append(act.astype(BF))
        slopes.append(dh)
        gub[:, s] += fold(dh.astype(F32))
    gated, dhid = jnp.concatenate(gates, axis=1), jnp.concatenate(slopes, axis=1)
    gated_o[...] = gated
    gup[...] += mm(hv.T, dhid)
    gdn[...] += mm(gv.T, gated)
    return mm(dhid, up[...], 1, 1)


def ffn_own_body(core, h2, g, up, ub, down, gated_o, dh2_o, keep_o, send_o, gub_o, gup, gdn, gub):
    i = pl.program_id(0)
    half = up.shape[1] // 2

    @pl.when(i == 0)
    def _():
        for a in (gup, gdn, gub):
            a[...] = jnp.zeros_like(a)

    bias = jnp.concatenate([ub[j : j + 1] for j in range(2)], axis=1).astype(F32)
    dh2_o[...] = ffn_block(h2[...], g[...], up, bias, down, 256, gated_o, gup, gdn, gub)

    @pl.when(i == pl.num_programs(0) - 1)
    def _():
        mine = pl.ds(pl.multiple_of(core[0] * half, 128), half)
        theirs = pl.ds(pl.multiple_of((1 - core[0]) * half, 128), half)
        keep_o[0] = gup[:, mine].astype(BF)
        keep_o[1] = gdn[:, mine].astype(BF)
        send_o[0] = gup[:, theirs].astype(BF)
        send_o[1] = gdn[:, theirs].astype(BF)
        total = jnp.sum(gub[...], axis=0, keepdims=True)
        for j in range(2):
            gub_o[j : j + 1] = total[:, j * half : (j + 1) * half]


def ffn_outs(t, d, f):
    half = f // 2
    return [in_hbm((t, f), BF), pltpu.VMEM((t, d), F32), shape((2, d, half), BF), shape((2, d, half), BF), shape((2, half), F32)]


def ffn_scratch(d, f):
    return [pltpu.VMEM((d, f), F32), pltpu.VMEM((d, f), F32), pltpu.VMEM((8, f), F32)]


def ffn_own(core, h2, g, up, ub, down, rows):
    t, d = h2.shape
    f = up.shape[1]
    outs = ffn_outs(t, d, f)
    return pl.pallas_call(
        ffn_own_body,
        grid_spec=pltpu.PrefetchScalarGridSpec(
            num_scalar_prefetch=1,
            grid=(t // rows,),
            in_specs=[rows_spec(rows, d), rows_spec(rows, d), whole(up), whole(ub), whole(down)],
            out_specs=[rows_spec(rows, f), rows_spec(rows, d)] + [whole(o) for o in outs[2:]],
            scratch_shapes=ffn_scratch(d, f),
        ),
        out_shape=outs,
        compiler_params=pltpu.CompilerParams(vmem_limit_bytes=LIMIT),
        cost_estimate=cost(2 * 5 * t * d * f),
        name="ffn_own",
    )(core, h2, g, up, ub, down)


def ffn_other_body(h2, g, w_send, w_keep, dh2_p, gated_o, dh2_o, keep_o, send_o, gub_o, gup, gdn, gub, up, down, ub):
    i = pl.program_id(0)
    d = h2.shape[1]
    half = w_send.shape[1]

    @pl.when(i == 0)
    def _():
        for a in (gup, gdn, gub):
            a[...] = jnp.zeros_like(a)
        for c, w in enumerate((w_send, w_keep)):
            up[:, c * half : (c + 1) * half] = w[0:d, :]
            down[c * half : (c + 1) * half, :] = w[d : d + half, :]
            ub[:, c * half : (c + 1) * half] = w[d + half : d + half + 16, :].astype(F32)[0:8]

    dh2_o[...] = dh2_p[...] + ffn_block(h2[...], g[...], up, ub[0:1], down, 256, gated_o, gup, gdn, gub)

    @pl.when(i == pl.num_programs(0) - 1)
    def _():
        send_o[0] = gup[:, 0:half].astype(BF)
        send_o[1] = gdn[:, 0:half].astype(BF)
        keep_o[0] = gup[:, half:].astype(BF)
        keep_o[1] = gdn[:, half:].astype(BF)
        total = jnp.sum(gub[...], axis=0, keepdims=True)
        for j in range(2):
            gub_o[j : j + 1] = total[:, j * half : (j + 1) * half]


def ffn_other(h2, g, w_send, w_keep, dh2_p, rows):
    t, d = h2.shape
    f = 2 * w_send.shape[1]
    outs = ffn_outs(t, d, f)
    return pl.pallas_call(
        ffn_other_body,
        grid=(t // rows,),
        in_specs=[rows_spec(rows, d), rows_spec(rows, d), whole(w_send), whole(w_keep), rows_spec(rows, d)],
        out_specs=[rows_spec(rows, f), rows_spec(rows, d)] + [whole(o) for o in outs[2:]],
        out_shape=outs,
        scratch_shapes=ffn_scratch(d, f) + [pltpu.VMEM((d, f), BF), pltpu.VMEM((f, d), BF), pltpu.VMEM((8, f), F32)],
        compiler_params=pltpu.CompilerParams(vmem_limit_bytes=LIMIT),
        cost_estimate=cost(2 * 5 * t * d * f),
        name="ffn_other",
    )(h2, g, w_send, w_keep, dh2_p)


def mid_body(dh2, resid, g, ctx, wo, vecs, dattn_o, dctx_o, gout_o, vec_o, gout, vec):
    i = pl.program_id(0)

    @pl.when(i == 0)
    def _():
        gout[...] = jnp.zeros_like(gout)
        vec[...] = jnp.zeros_like(vec)

    dh = dh2[...]
    n2, inv2 = layer_norm(resid[...])
    gf = g[...].astype(F32)
    dattn = (gf + norm_back(dh, n2, inv2, vecs[...].astype(F32)[3:4])).astype(BF)
    dattn_o[...] = dattn
    dctx_o[...] = mm(dattn, wo[...], 1, 1).astype(BF)
    gout[...] += mm(ctx[...].T, dattn)
    for j, v in enumerate((dattn.astype(F32), dh * n2, dh, gf)):
        vec[j] += fold(v)

    @pl.when(i == pl.num_programs(0) - 1)
    def _():
        gout_o[...] = gout[...].astype(BF)
        for j in range(4):
            vec_o[j : j + 1] = jnp.sum(vec[j], axis=0, keepdims=True)


def mid(dh2, resid, g, ctx, wo, vecs, rows):
    t, d = dh2.shape
    outs = [pltpu.VMEM((t, d), BF), pltpu.VMEM((t, d), BF), shape((d, d), BF), shape((4, d), F32)]
    return pl.pallas_call(
        mid_body,
        grid=(t // rows,),
        in_specs=[rows_spec(rows, d)] * 4 + [whole(wo), whole(vecs)],
        out_specs=[rows_spec(rows, d)] * 2 + [whole(o) for o in outs[2:]],
        out_shape=outs,
        scratch_shapes=[pltpu.VMEM((d, d), F32), pltpu.VMEM((4, 8, d), F32)],
        compiler_params=pltpu.CompilerParams(vmem_limit_bytes=LIMIT),
        cost_estimate=cost(3 * 2 * t * d * d),
        name="mid",
    )(dh2, resid, g, ctx, wo, vecs)


def attn_bwd_block(q, k, v, dc, seg, dj_o):
    rows, width = q.shape
    pairs = width // 128
    group = 2
    for s0 in range(0, rows // SEQ, group):
        items = [(slice(s * SEQ, (s + 1) * SEQ), p) for s in range(s0, s0 + group) for p in range(pairs)]
        allow = [allowed_of(seg[0, s : s + 1, :], True) for s in range(s0, s0 + group) for p in range(pairs)]
        qs = [stack_heads(slab(q, r, p) * BF(0.125)) for r, p in items]
        dcs = [stack_heads(slab(dc, r, p)) for r, p in items]
        scores = [mm(slab(k, r, p), a, 1, 1) for (r, p), a in zip(items, qs)]
        dprobs = [mm(slab(v, r, p), a, 1, 1) for (r, p), a in zip(items, dcs)]
        probs, dscores = [], []
        for ok, sc, dp in zip(allow, scores, dprobs):
            pb, ds = [], []
            for h in range(2):
                cols = slice(h * SEQ, (h + 1) * SEQ)
                w = jnp.where(ok, sc[:, cols], -1e9)
                e = jnp.exp(w - jnp.max(w, axis=0, keepdims=True))
                pr = e * (1.0 / jnp.sum(e, axis=0, keepdims=True))
                ds.append((pr * (dp[:, cols] - jnp.sum(pr * dp[:, cols], axis=0, keepdims=True))).astype(BF))
                pb.append(pr.astype(BF))
            probs.append(pb)
            dscores.append(ds)
        for (r, p), pb, a in zip(items, probs, dcs):
            dj_o[r, 2 * width + p * 128 : 2 * width + (p + 1) * 128] = mm(jnp.concatenate(pb, axis=1), a).astype(BF)
        for (r, p), ds, a in zip(items, dscores, qs):
            dj_o[r, width + p * 128 : width + (p + 1) * 128] = mm(jnp.concatenate(ds, axis=1), a).astype(BF)
        for (r, p), ds in zip(items, dscores):
            dq = mm(jnp.concatenate(ds, axis=0), stack_heads(slab(k, r, p)), 0, 0) * 0.125
            dj_o[r, p * 128 : (p + 1) * 128] = dq.astype(BF)


def ln1_parts(acc, cs, w):
    ones = jnp.ones((8, w.shape[1]), BF)
    gain = mm(ones, (acc * w.astype(F32)).astype(BF), 1, 1)[0:1]
    hi = cs.astype(BF)
    lo = (cs - hi.astype(F32)).astype(BF)
    return gain, jnp.sum(mm(hi, w, 1, 1) + mm(lo, w, 1, 1), axis=0, keepdims=True)


def attn_bwd_body(place, joined, dc, seg, n1t, wqkv, gout, gub_own, gub_oth, vec, dj_o, keep_o, send_o, acc, cs, small):
    i = pl.program_id(0)
    d = n1t.shape[0]
    step = d // 16

    @pl.when(i == 0)
    def _():
        acc[...] = jnp.zeros_like(acc)
        cs[...] = jnp.zeros_like(cs)

    q, k, v = (joined.at[:, j * d : (j + 1) * d] for j in range(3))
    attn_bwd_block(q, k, v, dc, seg, dj_o)
    dj = dj_o[...]
    acc[...] += mm(n1t[...], dj)
    cs[...] += fold(dj.astype(F32))

    @pl.when(i == pl.num_programs(0) - 1)
    def _():
        gain, bias = ln1_parts(acc[...], cs[...], wqkv[...])
        csum = jnp.sum(cs[...], axis=0, keepdims=True)
        y, c = place[0], place[1]
        small[...] = jnp.zeros_like(small)

        def put(at, row):
            n = row.shape[1] // 128
            for j in range(n):
                small[pl.ds(at + j, 1)] = row[:, j * 128 : (j + 1) * 128]

        n = d // 128
        for j in range(4):
            put(j * n, vec[j : j + 1, :])
        for j in range(2):
            put(4 * n + (2 * y + j) * n, gub_own[j : j + 1, :])
        put(4 * n + (2 * (1 - y) + 1 - c) * n, gub_oth[0:1, :])
        put(4 * n + (2 * (1 - y) + c) * n, gub_oth[1:2, :])
        put(8 * n, csum)
        put(11 * n, gain)
        put(12 * n, bias)
        for o, core in ((keep_o, c), (send_o, 1 - c)):
            for b in range(8):
                where = pl.ds(pl.multiple_of((8 * core + b) * step, step), step)
                o[b, :, 0 : 3 * d] = acc[where, :].astype(BF)
                o[b, :, 3 * d : 4 * d] = gout[where, :]
                o[b, :, 4 * d :] = jnp.zeros((step, 128), BF)

        @pl.when(c == 0)
        def _():
            for b in range(2):
                keep_o[b, :, 4 * d :] = small[b * step : (b + 1) * step].astype(BF)

        @pl.when(c == 1)
        def _():
            for b in range(2):
                send_o[b, :, 4 * d :] = small[b * step : (b + 1) * step].astype(BF)


def attn_bwd(place, joined, dctx, seg, n1t, wqkv, gout, gub_own, gub_oth, vec, rows):
    d, t = n1t.shape
    outs = [pltpu.VMEM((t, 3 * d), BF)] + [shape((8, d // 16, 4 * d + 128), BF)] * 2
    rest = (wqkv, gout, gub_own, gub_oth, vec)
    return pl.pallas_call(
        attn_bwd_body,
        grid_spec=pltpu.PrefetchScalarGridSpec(
            num_scalar_prefetch=1,
            grid=(t // rows,),
            in_specs=[
                rows_spec(rows, 3 * d),
                rows_spec(rows, d),
                pl.BlockSpec((1, rows // SEQ, SEQ), lambda i, *_: (i, 0, 0)),
                pl.BlockSpec((d, rows), lambda i, *_: (0, i)),
            ]
            + [whole(a) for a in rest],
            out_specs=[rows_spec(rows, 3 * d)] + [whole(o) for o in outs[1:]],
            scratch_shapes=[pltpu.VMEM((d, 3 * d), F32), pltpu.VMEM((8, 3 * d), F32), pltpu.VMEM((64, 128), F32)],
        ),
        out_shape=outs,
        compiler_params=pltpu.CompilerParams(vmem_limit_bytes=LIMIT + 8 * 1024 * 1024),
        cost_estimate=cost(8 * t * d * 3 * d),
        name="attn_bwd",
    )(place, joined, dctx, seg.reshape(t // rows, rows // SEQ, SEQ), n1t, *rest)


def in_grad_body(dj, tok, dattn, wqkv, vecs, out_o):
    dh1 = mm(dj[...], wqkv[...], 1, 1)
    n1, inv1 = layer_norm(tok[...].astype(F32))
    gain = vecs[...].astype(F32)[0:1]
    out_o[...] = (dattn[...].astype(F32) + norm_back(dh1, n1, inv1, gain)).astype(BF)


def in_grad_of(dj, tok, dattn, wqkv, vecs, rows):
    t, d = tok.shape
    return pl.pallas_call(
        in_grad_body,
        grid=(t // rows,),
        in_specs=[rows_spec(rows, 3 * d), rows_spec(rows, d), rows_spec(rows, d), whole(wqkv), whole(vecs)],
        out_specs=rows_spec(rows, d),
        out_shape=shape((t, d), BF),
        compiler_params=pltpu.CompilerParams(vmem_limit_bytes=LIMIT),
        cost_estimate=cost(2 * t * d * 3 * d),
        name="in_grad",
    )(dj, tok, dattn, wqkv, vecs)


def layer_out_body(own, oth, resid, down, w_send, w_keep, vecs, out_o):
    d = resid.shape[1]
    half = w_send.shape[1]
    out = mm(own[...], down[...])
    out += mm(oth[:, 0:half], w_send[d : d + half, :]) + mm(oth[:, half:], w_keep[d : d + half, :])
    out_o[...] = (resid[...] + out + vecs[...].astype(F32)[7:8]).astype(BF)


def layer_out_of(own, oth, resid, down, w_send, w_keep, vecs, rows):
    t, d = resid.shape
    f = own.shape[1]
    return pl.pallas_call(
        layer_out_body,
        grid=(t // rows,),
        in_specs=[rows_spec(rows, f)] * 2 + [rows_spec(rows, d)] + [whole(a) for a in (down, w_send, w_keep, vecs)],
        out_specs=rows_spec(rows, d),
        out_shape=shape((t, d), BF),
        compiler_params=pltpu.CompilerParams(vmem_limit_bytes=LIMIT),
        cost_estimate=cost(2 * t * d * 2 * f),
        name="layer_out",
    )(own, oth, resid, down, w_send, w_keep, vecs)


def on_chip(body, outs, at, *args, name):
    return pl.pallas_call(
        body,
        in_specs=[pl.BlockSpec(memory_space=pltpu.SMEM)] + [pl.BlockSpec(memory_space=pltpu.VMEM)] * len(args),
        out_specs=[pl.BlockSpec(memory_space=pltpu.VMEM)] * len(outs),
        out_shape=outs,
        compiler_params=pltpu.CompilerParams(vmem_limit_bytes=24 * 1024 * 1024),
        cost_estimate=cost(0, 4 * 1024 * 1024),
        name=name,
    )(at, *args)


def plus(a, b):
    return (a.astype(F32) + b.astype(F32)).astype(BF)


def split_body(at, own_a, own_b, oth_a, oth_b, keep_o, send_o):
    def total(o, h):
        a, b = (own_a, own_b) if o == 0 else (oth_a, oth_b)
        return plus(a[h], b[h])

    @pl.when(at[0] == 0)
    def _():
        v = at[1]
        for o in range(2):
            keep_o[o] = total(o, v)
            send_o[o] = total(o, 1 - v)

    @pl.when(at[0] == 1)
    def _():
        for h in range(2):
            keep_o[h] = total(0, h)
            send_o[h] = total(1, h)


def halve(at, which, a, b):
    n = a.shape[0] // 2

    def body(at, a, b, keep_o, send_o):
        v = at[which]
        for j in range(n):
            keep_o[j] = plus(a[v * n + j], b[v * n + j])
            send_o[j] = plus(a[(1 - v) * n + j], b[(1 - v) * n + j])

    return on_chip(body, [shape((n, *a.shape[1:]), BF)] * 2, at, a, b, name="halve")


def finish_ffn_body(at, *refs):
    up_o, down_o = refs[4:]
    for c in range(2):
        chunk = at[0] if c == 0 else 1 - at[0]
        quarter, half = refs[0].shape[1:]
        units = pl.ds(pl.multiple_of(chunk * half, 128), half)
        for j in range(2):
            pair = refs[2 * c + j]
            which = at[3 + 2 * c] if j == 0 else 1 - at[3 + 2 * c]
            for i in range(2):
                part = at[4 + 2 * c] if i == 0 else 1 - at[4 + 2 * c]
                cols = pl.ds(pl.multiple_of(part * quarter, 128), quarter)

                @pl.when(which == 0)
                def _(pair=pair, i=i, cols=cols, units=units):
                    up_o[cols, units] = pair[i].astype(F32)

                @pl.when(which == 1)
                def _(pair=pair, i=i, cols=cols, units=units):
                    down_o[units, cols] = pair[i].astype(F32).T


def finish_rest_body(at, columns, *refs):
    qkv_o, qv_o, gout_o, gain1_o, bias1_o, bo_o, gain2_o, bias2_o, gub_o, b2_o, small = refs[4:]
    d = gout_o.shape[0]
    step, n = d // 16, d // 128
    pieces = []
    for c in range(2):
        core = at[0] if c == 0 else 1 - at[0]
        a0, b0, c0 = (at[7 + j] if c == 0 else at[11 + j] for j in range(3))
        for j in range(2):
            for i in range(4):
                bits = (a0 if j == 0 else 1 - a0, b0 if i < 2 else 1 - b0, c0 if i % 2 == 0 else 1 - c0)
                pieces.append((refs[2 * c + j], i, 8 * core + 4 * bits[0] + 2 * bits[1] + bits[2]))
    for ref, i, at_ in pieces:

        @pl.when(at_ < 2)
        def _(ref=ref, i=i, at_=at_):
            small[pl.ds(pl.multiple_of(at_ * step, step), step)] = ref[i, :, 4 * d :].astype(F32)

    def row(first, count):
        return jnp.concatenate([small[first + j : first + j + 1] for j in range(count)], axis=1)

    csum = row(8 * n, 3 * n)
    for ref, i, at_ in pieces:
        rows = pl.ds(pl.multiple_of(at_ * step, step), step)
        gain, bias = columns[rows, 0:1], columns[rows, 1:2]
        qkv_o[rows, :] = ref[i, :, 0 : 3 * d].astype(F32) * gain + bias * csum
        gout_o[rows, :] = ref[i, :, 3 * d : 4 * d].astype(F32)
    qv_o[0:1] = csum[:, 0:d]
    qv_o[1:2] = csum[:, 2 * d :]
    for o, j in ((bo_o, 0), (gain2_o, 1), (bias2_o, 2), (b2_o, 3)):
        o[...] = row(j * n, n)
    gain1_o[...] = row(11 * n, n)
    bias1_o[...] = row(12 * n, n)
    first = 4 * n + 2 * n * at[10]
    for j in range(2 * n):
        gub_o[:, j * 128 : (j + 1) * 128] = small[pl.ds(first + j, 1)]


def finish_rest(at, columns, *pieces):
    d = columns.shape[0]
    one = shape((1, d), F32)
    outs = [shape((d, 3 * d), F32), shape((2, d), F32), shape((d, d), F32)] + [one] * 5 + [shape((1, 2 * d), F32), one]
    args = (columns, *pieces)
    return pl.pallas_call(
        finish_rest_body,
        in_specs=[pl.BlockSpec(memory_space=pltpu.SMEM)] + [pl.BlockSpec(memory_space=pltpu.VMEM)] * len(args),
        out_specs=[pl.BlockSpec(memory_space=pltpu.VMEM)] * len(outs),
        out_shape=outs,
        scratch_shapes=[pltpu.VMEM((64, 128), F32)],
        compiler_params=pltpu.CompilerParams(vmem_limit_bytes=24 * 1024 * 1024),
        cost_estimate=cost(0, 8 * 1024 * 1024),
        name="finish_rest",
    )(at, *args)


def local(
    n_rows,
    tokens,
    segment_ids,
    ln1_gain,
    ln1_bias,
    qkv_weight,
    qv_bias,
    out_weight,
    out_bias,
    ln2_gain,
    ln2_bias,
    up_weight,
    up_bias,
    down_weight,
    down_bias,
    out_grad,
):
    t, d = tokens.shape
    half = up_weight.shape[1] // 2
    r, y = lax.axis_index("rows"), lax.axis_index("mlp")
    core = r & 1
    up_dims = n_rows.bit_length() - 2

    def flip(dim, row, m):
        if dim == "core":
            return row ^ 1, m
        if dim == "y":
            return row, m ^ 1
        return row ^ (2 << dim), m

    def bit(dim):
        return y if dim == "y" else (r >> (dim + 1)) & 1

    def swap(value, *dims):
        pairs = []
        for row in range(n_rows):
            for m in range(2):
                row2, m2 = flip(dims[0] if row & 1 == 0 else dims[-1], row, m)
                pairs.append((row * 2 + m, row2 * 2 + m2))
        return lax.ppermute(value, BOTH, pairs)

    def by_core(first, second):
        return jnp.where(core == 0, first, second)

    def after(value, *done):
        return lax.optimization_barrier((value, *done))[0]

    u0 = [0, "y"] + list(range(1, up_dims))
    u1 = ["y"] + list(range(1, up_dims)) + [0]
    q0 = [0, "y", 1, 2] + list(range(3, up_dims))
    q1 = ["y", 0, 2, 1] + list(range(3, up_dims))
    big, small = (by_core(bit(u0[0]), bit(u1[1])), by_core(bit(u1[1]), bit(u0[0]))), (
        by_core(bit(u0[2]), bit(u1[2])), by_core(bit(u1[2]), bit(u0[2])),
    )
    at = jnp.stack(
        [core, bit(0), by_core(0, bit(u1[1])), big[0], small[0], big[1], small[1]]
        + [by_core(bit(a), bit(b)) for a, b in zip(q0[:3], q1[:3])]
        + [y]
        + [by_core(bit(b), bit(a)) for a, b in zip(q0[:3], q1[:3])]
    ).astype(jnp.int32)
    place = jnp.stack([y, core]).astype(jnp.int32)
    core_s = core.reshape(1).astype(jnp.int32)
    vmem = lambda v: pltpu.with_memory_space_constraint(v, pltpu.VMEM)
    hbm = lambda v: pltpu.with_memory_space_constraint(v, pltpu.HBM)
    tokens, out_grad = hbm(tokens), hbm(out_grad)

    first = 1 - core
    bias_rows = jnp.broadcast_to(lax.dynamic_slice(up_bias, (first * half,), (half,))[None], (16, half))
    w_mine = jnp.concatenate(
        [
            lax.dynamic_slice(up_weight, (0, first * half), (d, half)),
            lax.dynamic_slice(down_weight, (first * half, 0), (half, d)),
            bias_rows,
        ],
        axis=0,
    )
    w_send = swap(w_mine, "y")
    vecs = jnp.concatenate(
        [
            jnp.stack([ln1_gain, ln1_bias, out_bias, ln2_gain, ln2_bias, qv_bias[0], qv_bias[1], down_bias]),
            up_bias.reshape(2, half),
            jnp.zeros((6, d), BF),
        ]
    )
    columns = jnp.stack([ln1_gain, ln1_bias], axis=1).astype(F32)
    joined, ctx, resid, h2, n1t = attn_fwd(tokens, segment_ids, vecs, qkv_weight, out_weight, rows=512)
    gated_own, dh2_own, own_keep, own_send, gub_own = ffn_own(
        core_s, h2, out_grad, up_weight, vecs[8:10], down_weight, rows=512
    )
    w_send = after(w_send, own_send)
    w_keep = swap(w_send, "core")
    own_recv = swap(own_send, "core")
    gated_oth, dh2, oth_keep, oth_send, gub_oth = ffn_other(h2, out_grad, w_send, w_keep, vmem(dh2_own), rows=512)
    oth_recv = swap(oth_send, "core")
    dattn, dctx, gout, vec = mid(vmem(dh2), hbm(resid), out_grad, hbm(ctx), out_weight, vecs, rows=512)

    block = shape((2, d, half), BF)
    oth_recv = after(oth_recv, vec)
    u_keep, u_send = on_chip(split_body, [block] * 2, at, own_keep, own_recv, oth_keep, oth_recv, name="split")
    u_recv = swap(u_send, u0[0], u1[0])
    dj, q_keep, q_send = attn_bwd(
        place, hbm(joined), after(dctx, u_keep), segment_ids, hbm(n1t), qkv_weight, gout, gub_own, gub_oth, vec, rows=512
    )
    q_recv = swap(q_send, "core")
    cut = lambda v: v.reshape(2, d // 2, half)
    u_keep, u_send = halve(at, 2, u_keep, after(u_recv, q_send))
    u_recv = swap(cut(u_send), u0[1], u1[1])
    in_grad = in_grad_of(dj, tokens, after(dattn, u_keep), qkv_weight, vecs, rows=512)
    q_keep, q_send = halve(at, 7, q_keep, after(q_recv, in_grad))
    q_recv = swap(q_send, q0[0], q1[0])
    layer_out = layer_out_of(
        hbm(gated_own), hbm(gated_oth), hbm(after(resid, q_keep)), down_weight, w_send, w_keep, vecs, rows=512
    )
    u_keep, u_send = halve(at, 4, cut(u_keep), after(u_recv, layer_out))
    u_recv = swap(u_send, u0[2], u1[2])
    q_keep, q_send = halve(at, 8, q_keep, after(q_recv, u_keep))
    q_recv = swap(q_send, q0[1], q1[1])
    u_one = plus(u_keep, after(u_recv, q_keep))
    for k in range(3, len(u0)):
        u_recv = swap(u_one, u0[k], u1[k])
        if k == 3:
            q_keep, q_send = halve(at, 9, q_keep, after(q_recv, u_one))
            q_recv = swap(q_send, q0[2], q1[2])
            u_recv = after(u_recv, q_keep)
        u_one = plus(u_one, u_recv)
    u_ag = swap(u_one, u0[2], u1[2])
    q_one = plus(q_keep, after(q_recv, u_one))
    for k in range(3, len(q0)):
        q_recv = swap(q_one, q0[k], q1[k])
        if k == 3:
            u_pair = jnp.concatenate([u_one, after(u_ag, q_one)], axis=0)
            u_far = swap(u_pair, u0[0], u1[1])
            u_pair_c = swap(u_pair, "core")
            q_recv = after(q_recv, u_pair)
        q_one = plus(q_one, q_recv)
    q_ag = swap(q_one, q0[2], q1[2])
    u_far = after(u_far, q_one)
    u_far_c = swap(u_far, "core")
    q_pair = jnp.concatenate([q_one, after(q_ag, u_far)], axis=0)
    q_ag = swap(q_pair, q0[1], q1[1])
    grad_up, grad_down = on_chip(
        finish_ffn_body, [shape((d, 2 * half), F32), shape((2 * half, d), F32)], at,
        u_pair, u_far, u_pair_c, after(u_far_c, q_pair), name="finish_ffn",
    )
    q_four = jnp.concatenate([q_pair, after(q_ag, grad_up)], axis=0)
    q_far = swap(q_four, q0[0], q1[0])
    grad_qkv, grad_qv, grad_wo, g1, c1, bo, g2, c2, gub, b2 = finish_rest(
        at, columns, q_four, q_far, swap(q_four, "core"), swap(q_far, "core")
    )
    flat = lambda v: v.reshape(-1)
    return (
        layer_out, in_grad, flat(g1), flat(c1), grad_qkv, grad_qv, grad_wo, flat(bo), flat(g2), flat(c2),
        grad_up, flat(gub), grad_down, flat(b2),
    )


def solution(mesh):
    placed = (
        P(BOTH, None), P(BOTH, None), P(), P(), P(), P(), P(), P(), P(), P(),
        P(None, "mlp"), P("mlp"), P("mlp", None), P(), P(BOTH, None),
    )
    return jax.shard_map(
        functools.partial(local, mesh.shape["rows"]),
        mesh=mesh,
        in_specs=placed,
        out_specs=(
            P(BOTH, None), P(BOTH, None), P(), P(), P(), P(), P(), P(), P(), P(),
            P(None, "mlp"), P("mlp"), P("mlp", None), P(),
        ),
        check_vma=False,
    )
```

```python
import functools
import math

import jax
import jax.numpy as jnp
from jax import lax
from jax.experimental import pallas as pl
from jax.experimental.pallas import tpu as pltpu
from jax.sharding import PartitionSpec as P

BF, F32 = jnp.bfloat16, jnp.float32
SEQ, HD, FRAME = 128, 64, 4
EPS = 1e-5
C0 = math.sqrt(2.0 / math.pi)
C1 = C0 * 0.044715
LIMIT = 20 * 1024 * 1024
BOTH = ("rows", "mlp")
OWN_LIMIT = 24 * 1024 * 1024
OTHER_LIMIT = 32 * 1024 * 1024


def mm(a, b, ca=1, cb=0):
    return lax.dot_general(a, b, (((ca,), (cb,)), ((), ())), preferred_element_type=F32)


def layer_norm(x):
    c = x - jnp.mean(x, axis=-1, keepdims=True)
    inv = lax.rsqrt(jnp.mean(c * c, axis=-1, keepdims=True) + EPS)
    return c * inv, inv


def norm_back(grad, normed, inv, gain):
    s = grad * gain
    return inv * (
        s
        - jnp.mean(s, axis=-1, keepdims=True)
        - normed * jnp.mean(s * normed, axis=-1, keepdims=True)
    )


def fold(v):
    return jnp.sum(v.reshape(-1, 8, v.shape[-1]), axis=0)


def stack_heads(v):
    low = lax.broadcasted_iota(jnp.int32, v.shape, 1) < HD
    zero = jnp.zeros_like(v)
    return jnp.concatenate([jnp.where(low, v, zero), jnp.where(low, zero, v)], axis=0)


def allowed_of(seg_row, transposed):
    wide = jnp.broadcast_to(seg_row.astype(F32), (SEQ, SEQ))
    same = wide == wide.T
    a = lax.broadcasted_iota(jnp.int32, (SEQ, SEQ), 1 if transposed else 0)
    b = lax.broadcasted_iota(jnp.int32, (SEQ, SEQ), 0 if transposed else 1)
    return same & (a // FRAME >= b // FRAME)


def whole(a):
    zeros = (0,) * len(a.shape)
    return pl.BlockSpec(a.shape, lambda i, *_: zeros)


def once(a):
    zeros = (0,) * len(a.shape)
    return pl.BlockSpec(a.shape, lambda i, *_: zeros, pipeline_mode=pl.Buffered(buffer_count=1))


def rows_spec(r, w):
    return pl.BlockSpec((r, w), lambda i, *_: (i, 0))


def shape(s, dtype):
    return jax.ShapeDtypeStruct(s, dtype)


def in_hbm(s, dtype):
    return pltpu.HBM(s, dtype)


def cost(macs, nbytes=0):
    return pl.CostEstimate(flops=8 * macs, bytes_accessed=1, transcendentals=0)


def slab(ref, r, c):
    return ref[r, c * 128 : (c + 1) * 128]


def attn_fwd_body(tok, seg, vecs, wqkv, wo, joined_o, ctx_o, resid_o, h2_o, n1t_o):
    rows, width = tok.shape
    pairs = width // 128
    vec = vecs[...].astype(F32)
    g1, b1, bo, g2, b2, bq, bv = (vec[j : j + 1] for j in range(7))
    x = tok[...].astype(F32)
    n1, _ = layer_norm(x)
    n1t_o[...] = n1.astype(BF).T
    h1 = (n1 * g1 + b1).astype(BF)
    bias = jnp.concatenate([bq, jnp.zeros_like(bq), bv], axis=1)
    joined = (mm(h1, wqkv[...]) + bias).astype(BF)
    joined_o[...] = joined
    group = 4
    done = []
    for s0 in range(0, rows // SEQ, group):
        items = [(s, p) for s in range(s0, s0 + group) for p in range(pairs)]
        allow = {s: allowed_of(seg[0, s : s + 1, :], True) for s in range(s0, s0 + group)}

        def part(s, o, p):
            return joined[s * SEQ : (s + 1) * SEQ, o * width + p * 128 : o * width + (p + 1) * 128]

        scores = [mm(part(s, 1, p), stack_heads(part(s, 0, p) * BF(0.125)), 1, 1) for s, p in items]
        probs = []
        for (s, p), sc in zip(items, scores):
            two = []
            for h in range(2):
                v = jnp.where(allow[s], sc[:, h * SEQ : (h + 1) * SEQ], -1e9)
                e = jnp.exp(v - jnp.max(v, axis=0, keepdims=True))
                two.append((e * (1.0 / jnp.sum(e, axis=0, keepdims=True))).astype(BF))
            probs.append(jnp.concatenate(two, axis=0))
        outs = [mm(pr, stack_heads(part(s, 2, p)), 0, 0).astype(BF) for (s, p), pr in zip(items, probs)]
        for j in range(group):
            done.append(jnp.concatenate(outs[j * pairs : (j + 1) * pairs], axis=1))
    ctx = jnp.concatenate(done, axis=0)
    ctx_o[...] = ctx
    resid = x + mm(ctx, wo[...]) + bo
    resid_o[...] = resid
    n2, _ = layer_norm(resid)
    h2_o[...] = (n2 * g2 + b2).astype(BF)


def attn_fwd(tok, seg, vecs, wqkv, wo, rows):
    t, d = tok.shape
    return pl.pallas_call(
        attn_fwd_body,
        grid=(t // rows,),
        in_specs=[rows_spec(rows, d), pl.BlockSpec((1, rows // SEQ, SEQ), lambda i: (i, 0, 0))]
        + [once(a) for a in (vecs, wqkv, wo)],
        out_specs=[rows_spec(rows, w) for w in (3 * d, d, d, d)] + [pl.BlockSpec((d, rows), lambda i: (0, i))],
        out_shape=[in_hbm((t, 3 * d), BF), in_hbm((t, d), BF), in_hbm((t, d), F32), in_hbm((t, d), BF), in_hbm((d, t), BF)],
        compiler_params=pltpu.CompilerParams(vmem_limit_bytes=LIMIT),
        cost_estimate=cost(3 * t * d * 4 * d),
        name="attn_fwd",
    )(tok, seg.reshape(t // rows, rows // SEQ, SEQ), vecs, wqkv, wo)


def fetch_body(first, up, down, bias, out_o):
    d, half = up.shape
    out_o[0:d] = up[...]
    out_o[d : d + half] = down[...]
    bias = bias[...].astype(F32)
    bias = jnp.where(first[0] == 0, bias[0:1], bias[1:2])
    out_o[d + half :] = jnp.broadcast_to(bias, (16, half)).astype(BF)


def fetch(first, up, down, bias):
    d, f = up.shape
    half = f // 2
    return pl.pallas_call(
        fetch_body,
        grid_spec=pltpu.PrefetchScalarGridSpec(
            num_scalar_prefetch=1,
            grid=(1,),
            in_specs=[
                pl.BlockSpec((d, half), lambda i, at: (0, at[0])),
                pl.BlockSpec((half, d), lambda i, at: (at[0], 0)),
                whole(bias),
            ],
            out_specs=pl.BlockSpec((d + half + 16, half), lambda i, at: (0, 0)),
        ),
        out_shape=shape((d + half + 16, half), BF),
        compiler_params=pltpu.CompilerParams(vmem_limit_bytes=LIMIT),
        cost_estimate=cost(0, 1024 * 1024),
        name="fetch",
    )(first, up, down, bias)


def gate(v, dg, bias):
    v = v + bias
    v2 = v * v
    a = 0.5 + 0.5 * jnp.tanh(v * (C0 + C1 * v2))
    act = v * a
    slope = a + act * (1.0 - a) * (2.0 * C0 + 6.0 * C1 * v2)
    return act.astype(BF), (dg * slope).astype(BF)


def ffn_block(h2, g, up, ub, down, gated_o, dhid, gup, gdn, gub):
    f = up.shape[1]
    side, tile = 256, 64
    units = [(r, c) for r in range(0, h2.shape[0], side) for c in range(0, f, side)]

    def products(r, c):
        return mm(h2[r : r + side, :], up[:, c : c + side]), mm(g[r : r + side, :], down[c : c + side, :], 1, 1)

    ahead = products(*units[0])
    for k, (r, c) in enumerate(units):
        v, dg = ahead
        if k + 1 < len(units):
            ahead = products(*units[k + 1])
        for t in range(0, side, tile):
            act, dh = gate(v[t : t + tile], dg[t : t + tile], ub[:, c : c + side])
            gated_o[r + t : r + t + tile, c : c + side] = act
            dhid[r + t : r + t + tile, c : c + side] = dh
    dh = dhid[...]
    gup[...] += mm(h2[...].T, dh)
    gdn[...] += mm(g[...].T, gated_o[...])
    gub[...] += fold(dh.astype(F32))
    return mm(dh, up[...], 1, 1)


def put_grads(o, gup, gdn, cols):
    n = gup.shape[0] // 2
    for j in range(2):
        o[j] = gup[j * n : (j + 1) * n, cols].astype(BF)
        o[2 + j] = gdn[j * n : (j + 1) * n, cols].astype(BF)


def put_bias(o, gub):
    half = o.shape[1]
    total = jnp.sum(gub[...], axis=0, keepdims=True)
    for j in range(2):
        o[j : j + 1] = total[:, j * half : (j + 1) * half]


def ffn_own_body(core, h2, g, up, vecs, down, gated_o, dh2_o, keep_o, send_o, gub_o, gup, gdn, gub, dhid):
    i = pl.program_id(0)
    half = up.shape[1] // 2

    @pl.when(i == 0)
    def _():
        for a in (gup, gdn, gub):
            a[...] = jnp.zeros_like(a)

    bias = vecs[...].astype(F32)
    bias = jnp.concatenate([bias[8:9], bias[9:10]], axis=1)
    dh2_o[...] = ffn_block(h2, g, up, bias, down, gated_o, dhid, gup, gdn, gub)

    @pl.when(i == pl.num_programs(0) - 1)
    def _():
        put_grads(keep_o, gup, gdn, pl.ds(pl.multiple_of(core[0] * half, 128), half))
        put_grads(send_o, gup, gdn, pl.ds(pl.multiple_of((1 - core[0]) * half, 128), half))
        put_bias(gub_o, gub)


def ffn_scratch(rows, d, f):
    return [pltpu.VMEM((d, f), F32), pltpu.VMEM((d, f), F32), pltpu.VMEM((8, f), F32), pltpu.VMEM((rows, f), BF)]


def ffn_own(core, h2, g, up, vecs, down, rows):
    t, d = h2.shape
    f = up.shape[1]
    half = f // 2
    outs = [in_hbm((t, f), BF), in_hbm((t, d), F32)] + [shape((4, d // 2, half), BF)] * 2 + [shape((2, half), F32)]
    return pl.pallas_call(
        ffn_own_body,
        grid_spec=pltpu.PrefetchScalarGridSpec(
            num_scalar_prefetch=1,
            grid=(t // rows,),
            in_specs=[rows_spec(rows, d), rows_spec(rows, d), once(up), whole(vecs), once(down)],
            out_specs=[rows_spec(rows, f), rows_spec(rows, d)] + [whole(o) for o in outs[2:]],
            scratch_shapes=ffn_scratch(rows, d, f),
        ),
        out_shape=outs,
        compiler_params=pltpu.CompilerParams(vmem_limit_bytes=OWN_LIMIT),
        cost_estimate=cost(2 * 5 * t * d * f),
        name="ffn_own",
    )(core, h2, g, up, vecs, down)


def ffn_other_body(
    h2, g, w_send, w_keep, dh2_p, resid, ctx, wo, vecs,
    gated_o, dattn_o, dctx_o, keep_o, send_o, gub_o, gout_o, vec_o,
    gup, gdn, gub, dhid, up, down, ub, gout, vec,
):
    i = pl.program_id(0)
    d = h2.shape[1]
    half = w_send.shape[1]

    @pl.when(i == 0)
    def _():
        for a in (gup, gdn, gub, gout, vec):
            a[...] = jnp.zeros_like(a)
        for c, w in enumerate((w_send, w_keep)):
            up[:, c * half : (c + 1) * half] = w[0:d, :]
            down[c * half : (c + 1) * half, :] = w[d : d + half, :]
            ub[:, c * half : (c + 1) * half] = w[d + half : d + half + 16, :].astype(F32)[0:8]

    dh = dh2_p[...] + ffn_block(h2, g, up, ub[0:1], down, gated_o, dhid, gup, gdn, gub)
    n2, inv2 = layer_norm(resid[...])
    gf = g[...].astype(F32)
    dattn = (gf + norm_back(dh, n2, inv2, vecs[...].astype(F32)[3:4])).astype(BF)
    dattn_o[...] = dattn
    dctx_o[...] = mm(dattn, wo[...], 1, 1).astype(BF)
    gout[...] += mm(ctx[...].T, dattn)
    for j, v in enumerate((dattn.astype(F32), dh * n2, dh, gf)):
        vec[j] += fold(v)

    @pl.when(i == pl.num_programs(0) - 1)
    def _():
        put_grads(send_o, gup, gdn, slice(0, half))
        put_grads(keep_o, gup, gdn, slice(half, 2 * half))
        gout_o[...] = gout[...].astype(BF)
        put_bias(gub_o, gub)
        for j in range(4):
            vec_o[j : j + 1] = jnp.sum(vec[j], axis=0, keepdims=True)


def ffn_other(h2, g, w_send, w_keep, dh2_p, resid, ctx, wo, vecs, rows):
    t, d = h2.shape
    half = w_send.shape[1]
    f = 2 * half
    outs = [in_hbm((t, f), BF), in_hbm((t, d), BF), in_hbm((t, d), BF)]
    outs += [shape((4, d // 2, half), BF)] * 2 + [shape((2, half), F32), in_hbm((d, d), BF), shape((4, d), F32)]
    return pl.pallas_call(
        ffn_other_body,
        grid_spec=pltpu.PrefetchScalarGridSpec(
            num_scalar_prefetch=0,
            grid=(t // rows,),
            in_specs=[rows_spec(rows, d), rows_spec(rows, d), once(w_send), once(w_keep)]
            + [rows_spec(rows, d)] * 3
            + [once(wo), whole(vecs)],
            out_specs=[rows_spec(rows, f), rows_spec(rows, d), rows_spec(rows, d)] + [whole(o) for o in outs[3:]],
            scratch_shapes=ffn_scratch(rows, d, f)
            + [pltpu.VMEM((d, f), BF), pltpu.VMEM((f, d), BF), pltpu.VMEM((8, f), F32)]
            + [pltpu.VMEM((d, d), F32), pltpu.VMEM((4, 8, d), F32)],
        ),
        out_shape=outs,
        compiler_params=pltpu.CompilerParams(vmem_limit_bytes=OTHER_LIMIT),
        cost_estimate=cost(2 * (5 * t * d * f + 2 * t * d * d)),
        name="ffn_other",
    )(h2, g, w_send, w_keep, dh2_p, resid, ctx, wo, vecs)


def attn_bwd_block(q, k, v, dc, seg, dj_o):
    rows, width = q.shape
    pairs = width // 128
    group = 2
    for s0 in range(0, rows // SEQ, group):
        items = [(slice(s * SEQ, (s + 1) * SEQ), p) for s in range(s0, s0 + group) for p in range(pairs)]
        allow = [allowed_of(seg[0, s : s + 1, :], True) for s in range(s0, s0 + group) for p in range(pairs)]
        qs = [stack_heads(slab(q, r, p) * BF(0.125)) for r, p in items]
        dcs = [stack_heads(slab(dc, r, p)) for r, p in items]
        scores = [mm(slab(k, r, p), a, 1, 1) for (r, p), a in zip(items, qs)]
        dprobs = [mm(slab(v, r, p), a, 1, 1) for (r, p), a in zip(items, dcs)]
        probs, dscores = [], []
        for ok, sc, dp in zip(allow, scores, dprobs):
            pb, ds = [], []
            for h in range(2):
                cols = slice(h * SEQ, (h + 1) * SEQ)
                w = jnp.where(ok, sc[:, cols], -1e9)
                e = jnp.exp(w - jnp.max(w, axis=0, keepdims=True))
                pr = e * (1.0 / jnp.sum(e, axis=0, keepdims=True))
                ds.append((pr * (dp[:, cols] - jnp.sum(pr * dp[:, cols], axis=0, keepdims=True))).astype(BF))
                pb.append(pr.astype(BF))
            probs.append(pb)
            dscores.append(ds)
        for (r, p), pb, a in zip(items, probs, dcs):
            dj_o[r, 2 * width + p * 128 : 2 * width + (p + 1) * 128] = mm(jnp.concatenate(pb, axis=1), a).astype(BF)
        for (r, p), ds, a in zip(items, dscores, qs):
            dj_o[r, width + p * 128 : width + (p + 1) * 128] = mm(jnp.concatenate(ds, axis=1), a).astype(BF)
        for (r, p), ds in zip(items, dscores):
            dq = mm(jnp.concatenate(ds, axis=0), stack_heads(slab(k, r, p)), 0, 0) * 0.125
            dj_o[r, p * 128 : (p + 1) * 128] = dq.astype(BF)


def ln1_parts(acc, cs, w):
    ones = jnp.ones((8, w.shape[1]), BF)
    gain = mm(ones, (acc * w.astype(F32)).astype(BF), 1, 1)[0:1]
    hi = cs.astype(BF)
    lo = (cs - hi.astype(F32)).astype(BF)
    return gain, jnp.sum(mm(hi, w, 1, 1) + mm(lo, w, 1, 1), axis=0, keepdims=True)


def attn_bwd_body(place, joined, dc, seg, n1t, wqkv, gout, gub_own, gub_oth, vec, dj_o, keep_o, send_o, acc, cs, small):
    i = pl.program_id(0)
    d = n1t.shape[0]
    step = d // 16

    @pl.when(i == 0)
    def _():
        acc[...] = jnp.zeros_like(acc)
        cs[...] = jnp.zeros_like(cs)

    q, k, v = (joined.at[:, j * d : (j + 1) * d] for j in range(3))
    attn_bwd_block(q, k, v, dc, seg, dj_o)
    dj = dj_o[...]
    acc[...] += mm(n1t[...], dj)
    cs[...] += fold(dj.astype(F32))

    @pl.when(i == pl.num_programs(0) - 1)
    def _():
        gain, bias = ln1_parts(acc[...], cs[...], wqkv[...])
        csum = jnp.sum(cs[...], axis=0, keepdims=True)
        y, c = place[0], place[1]
        small[...] = jnp.zeros_like(small)

        def put(at, row):
            n = row.shape[1] // 128
            for j in range(n):
                small[pl.ds(at + j, 1)] = row[:, j * 128 : (j + 1) * 128]

        n = d // 128
        for j in range(4):
            put(j * n, vec[j : j + 1, :])
        for j in range(2):
            put(4 * n + (2 * y + j) * n, gub_own[j : j + 1, :])
        put(4 * n + (2 * (1 - y) + 1 - c) * n, gub_oth[0:1, :])
        put(4 * n + (2 * (1 - y) + c) * n, gub_oth[1:2, :])
        put(8 * n, csum)
        put(11 * n, gain)
        put(12 * n, bias)
        for o, core in ((keep_o, c), (send_o, 1 - c)):
            for b in range(8):
                where = pl.ds(pl.multiple_of((8 * core + b) * step, step), step)
                o[b, :, 0 : 3 * d] = acc[where, :].astype(BF)
                o[b, :, 3 * d : 4 * d] = gout[where, :]
                o[b, :, 4 * d :] = jnp.zeros((step, 128), BF)

        @pl.when(c == 0)
        def _():
            for b in range(2):
                keep_o[b, :, 4 * d :] = small[b * step : (b + 1) * step].astype(BF)

        @pl.when(c == 1)
        def _():
            for b in range(2):
                send_o[b, :, 4 * d :] = small[b * step : (b + 1) * step].astype(BF)


def attn_bwd(place, joined, dctx, seg, n1t, wqkv, gout, gub_own, gub_oth, vec, rows):
    d, t = n1t.shape
    outs = [pltpu.VMEM((t, 3 * d), BF)] + [shape((8, d // 16, 4 * d + 128), BF)] * 2
    rest = (wqkv, gout, gub_own, gub_oth, vec)
    return pl.pallas_call(
        attn_bwd_body,
        grid_spec=pltpu.PrefetchScalarGridSpec(
            num_scalar_prefetch=1,
            grid=(t // rows,),
            in_specs=[
                rows_spec(rows, 3 * d),
                rows_spec(rows, d),
                pl.BlockSpec((1, rows // SEQ, SEQ), lambda i, *_: (i, 0, 0)),
                pl.BlockSpec((d, rows), lambda i, *_: (0, i)),
            ]
            + [once(a) for a in rest],
            out_specs=[rows_spec(rows, 3 * d)] + [whole(o) for o in outs[1:]],
            scratch_shapes=[pltpu.VMEM((d, 3 * d), F32), pltpu.VMEM((8, 3 * d), F32), pltpu.VMEM((64, 128), F32)],
        ),
        out_shape=outs,
        compiler_params=pltpu.CompilerParams(vmem_limit_bytes=LIMIT + 8 * 1024 * 1024),
        cost_estimate=cost(8 * t * d * 3 * d),
        name="attn_bwd",
    )(place, joined, dctx, seg.reshape(t // rows, rows // SEQ, SEQ), n1t, *rest)


def in_grad_body(dj, tok, dattn, wqkv, vecs, *refs):
    dh1 = mm(dj[...], wqkv[...], 1, 1)
    n1, inv1 = layer_norm(tok[...].astype(F32))
    gain = vecs[...].astype(F32)[0:1]
    refs[-1][...] = (dattn[...].astype(F32) + norm_back(dh1, n1, inv1, gain)).astype(BF)


def in_part(body, rows, first, count, streams, fixed, before, macs, name):
    t, d = streams[1].shape
    spec = lambda w: pl.BlockSpec((rows, w), lambda i: (i + first, 0))
    args = (*streams, *fixed) + (() if before is None else (before,))
    return pl.pallas_call(
        body,
        grid=(count,),
        in_specs=[spec(a.shape[1]) for a in streams]
        + [once(a) for a in fixed]
        + ([] if before is None else [pl.BlockSpec(memory_space=pl.ANY)]),
        out_specs=spec(d),
        out_shape=in_hbm((t, d), BF),
        input_output_aliases={} if before is None else {len(args) - 1: 0},
        compiler_params=pltpu.CompilerParams(vmem_limit_bytes=LIMIT),
        cost_estimate=cost(2 * rows * count * macs),
        name=name,
    )(*args)


def layer_out_body(own, resid, oth, down, w_send, w_keep, vecs, *refs):
    d = resid.shape[1]
    half = w_send.shape[1]
    out = mm(own[...], down[...])
    out += mm(oth[:, 0:half], w_send[d : d + half, :]) + mm(oth[:, half:], w_keep[d : d + half, :])
    refs[-1][...] = (resid[...] + out + vecs[...].astype(F32)[7:8]).astype(BF)


def on_chip(body, outs, at, *args, name):
    return pl.pallas_call(
        body,
        in_specs=[pl.BlockSpec(memory_space=pltpu.SMEM)] + [pl.BlockSpec(memory_space=pltpu.VMEM)] * len(args),
        out_specs=[pl.BlockSpec(memory_space=pltpu.VMEM)] * len(outs),
        out_shape=outs,
        compiler_params=pltpu.CompilerParams(vmem_limit_bytes=24 * 1024 * 1024),
        cost_estimate=cost(0, 4 * 1024 * 1024),
        name=name,
    )(at, *args)


def plus(a, b):
    return (a.astype(F32) + b.astype(F32)).astype(BF)


def split_body(at, own_a, own_b, oth_a, oth_b, keep_o, send_o):
    def total(o, j):
        a, b = (own_a, own_b) if o == 0 else (oth_a, oth_b)
        return plus(a[j], b[j])

    @pl.when(at[0] == 0)
    def _():
        v = at[1]
        for o in range(2):
            for p in range(2):
                keep_o[2 * o + p] = total(o, 2 * v + p)
                send_o[2 * o + p] = total(o, 2 * (1 - v) + p)

    @pl.when(at[0] == 1)
    def _():
        for j in range(4):
            keep_o[j] = total(0, j)
            send_o[j] = total(1, j)


def halve(at, which, a, b):
    n = a.shape[0] // 2

    def body(at, a, b, keep_o, send_o):
        v = at[which]
        for j in range(n):
            keep_o[j] = plus(a[v * n + j], b[v * n + j])
            send_o[j] = plus(a[(1 - v) * n + j], b[(1 - v) * n + j])

    return on_chip(body, [shape((n, *a.shape[1:]), BF)] * 2, at, a, b, name="halve")


def finish_ffn_body(at, *refs):
    up_o, down_o = refs[4:]
    for c in range(2):
        chunk = at[0] if c == 0 else 1 - at[0]
        quarter, half = refs[0].shape[1:]
        units = pl.ds(pl.multiple_of(chunk * half, 128), half)
        for j in range(2):
            pair = refs[2 * c + j]
            which = at[3 + 2 * c] if j == 0 else 1 - at[3 + 2 * c]
            for i in range(2):
                part = at[4 + 2 * c] if i == 0 else 1 - at[4 + 2 * c]
                cols = pl.ds(pl.multiple_of(part * quarter, 128), quarter)

                @pl.when(which == 0)
                def _(pair=pair, i=i, cols=cols, units=units):
                    up_o[cols, units] = pair[i].astype(F32)

                @pl.when(which == 1)
                def _(pair=pair, i=i, cols=cols, units=units):
                    down_o[units, cols] = pair[i].astype(F32).T


def finish_rest_body(at, columns, *refs):
    qkv_o, qv_o, gout_o, gain1_o, bias1_o, bo_o, gain2_o, bias2_o, gub_o, b2_o, small = refs[4:]
    d = qkv_o.shape[0]
    step, n = d // 16, d // 128
    pieces = []
    for c in range(2):
        core = at[0] if c == 0 else 1 - at[0]
        a0, b0, c0 = (at[7 + j] if c == 0 else at[11 + j] for j in range(3))
        for j in range(2):
            for i in range(4):
                bits = (a0 if j == 0 else 1 - a0, b0 if i < 2 else 1 - b0, c0 if i % 2 == 0 else 1 - c0)
                pieces.append((refs[2 * c + j], i, 8 * core + 4 * bits[0] + 2 * bits[1] + bits[2]))
    for ref, i, at_ in pieces:

        @pl.when(at_ < 2)
        def _(ref=ref, i=i, at_=at_):
            small[pl.ds(pl.multiple_of(at_ * step, step), step)] = ref[i, :, 4 * d :].astype(F32)

    def row(first, count):
        return jnp.concatenate([small[first + j : first + j + 1] for j in range(count)], axis=1)

    csum = row(8 * n, 3 * n)
    for ref, i, at_ in pieces:
        rows = pl.ds(pl.multiple_of(at_ * step, step), step)
        gain, bias = columns[rows, 0:1], columns[rows, 1:2]
        qkv_o[rows, :] = ref[i, :, 0 : 3 * d].astype(F32) * gain + bias * csum
        gout_o[rows, :] = ref[i, :, 3 * d : 4 * d].astype(F32)
    qv_o[0:1] = csum[:, 0:d]
    qv_o[1:2] = csum[:, 2 * d :]
    for o, j in ((bo_o, 0), (gain2_o, 1), (bias2_o, 2), (b2_o, 3)):
        o[...] = row(j * n, n)
    gain1_o[...] = row(11 * n, n)
    bias1_o[...] = row(12 * n, n)
    first = 4 * n + 2 * n * at[10]
    for j in range(2 * n):
        gub_o[:, j * 128 : (j + 1) * 128] = small[pl.ds(first + j, 1)]


def finish_rest(at, columns, *pieces):
    d = columns.shape[0]
    one = shape((1, d), F32)
    outs = [shape((d, 3 * d), F32), shape((2, d), F32), shape((d, d), F32)] + [one] * 5 + [shape((1, 2 * d), F32), one]
    args = (columns, *pieces)
    return pl.pallas_call(
        finish_rest_body,
        in_specs=[pl.BlockSpec(memory_space=pltpu.SMEM)] + [pl.BlockSpec(memory_space=pltpu.VMEM)] * len(args),
        out_specs=[pl.BlockSpec(memory_space=pltpu.VMEM)] * len(outs),
        out_shape=outs,
        scratch_shapes=[pltpu.VMEM((64, 128), F32)],
        compiler_params=pltpu.CompilerParams(vmem_limit_bytes=24 * 1024 * 1024),
        cost_estimate=cost(0, 8 * 1024 * 1024),
        name="finish_rest",
    )(at, *args)


def local(
    n_rows,
    tokens,
    segment_ids,
    ln1_gain,
    ln1_bias,
    qkv_weight,
    qv_bias,
    out_weight,
    out_bias,
    ln2_gain,
    ln2_bias,
    up_weight,
    up_bias,
    down_weight,
    down_bias,
    out_grad,
):
    t, d = tokens.shape
    half = up_weight.shape[1] // 2
    r, y = lax.axis_index("rows"), lax.axis_index("mlp")
    core = r & 1
    up_dims = n_rows.bit_length() - 2

    def flip(dim, row, m):
        if dim == "core":
            return row ^ 1, m
        if dim == "y":
            return row, m ^ 1
        return row ^ (2 << dim), m

    def bit(dim):
        return y if dim == "y" else (r >> (dim + 1)) & 1

    def swap(value, *dims):
        pairs = []
        for row in range(n_rows):
            for m in range(2):
                row2, m2 = flip(dims[0] if row & 1 == 0 else dims[-1], row, m)
                pairs.append((row * 2 + m, row2 * 2 + m2))
        return lax.ppermute(value, BOTH, pairs)

    def by_core(first, second):
        return jnp.where(core == 0, first, second)

    def after(value, *done):
        return lax.optimization_barrier((value, *done))[0]

    u0 = [0, "y"] + list(range(1, up_dims))
    u1 = ["y", 1, 0] + list(range(2, up_dims))
    q0 = [0, "y", 1, 2] + list(range(3, up_dims))
    q1 = ["y", 0, 2, 1] + list(range(3, up_dims))
    at = jnp.stack(
        [core, bit(0), by_core(0, bit(u1[1]))]
        + [by_core(bit(u0[0]), bit(u1[1])), by_core(bit(u0[2]), bit(u1[2]))]
        + [by_core(bit(u1[1]), bit(u0[0])), by_core(bit(u1[2]), bit(u0[2]))]
        + [by_core(bit(a), bit(b)) for a, b in zip(q0[:3], q1[:3])]
        + [y]
        + [by_core(bit(b), bit(a)) for a, b in zip(q0[:3], q1[:3])]
    ).astype(jnp.int32)
    place = jnp.stack([y, core]).astype(jnp.int32)
    core_s = core.reshape(1).astype(jnp.int32)
    hbm = lambda v: pltpu.with_memory_space_constraint(v, pltpu.HBM)
    qkv_free, down_free = qkv_weight, down_weight
    tokens, out_grad, qkv_weight, out_weight, up_weight, down_weight = map(
        hbm, (tokens, out_grad, qkv_weight, out_weight, up_weight, down_weight)
    )

    bias = up_bias.reshape(2, half)
    vecs = jnp.concatenate(
        [
            jnp.stack([ln1_gain, ln1_bias, out_bias, ln2_gain, ln2_bias, qv_bias[0], qv_bias[1], down_bias]),
            bias,
            jnp.zeros((6, d), BF),
        ]
    )
    columns = jnp.stack([ln1_gain, ln1_bias], axis=1).astype(F32)

    w_send = swap(fetch(1 - core_s, up_weight, down_weight, bias), "y")
    joined, ctx, resid, h2, n1t = attn_fwd(tokens, segment_ids, vecs, qkv_weight, out_weight, rows=512)
    gated_own, dh2_own, own_keep, own_send, gub_own = ffn_own(
        core_s, hbm(h2), out_grad, up_weight, vecs, down_weight, rows=512
    )
    w_send = hbm(after(w_send, own_send))
    w_keep = swap(w_send, "core")
    own_recv = swap(own_send, "core")
    gated_oth, dattn, dctx, oth_keep, oth_send, gub_oth, gout, vec = ffn_other(
        hbm(h2), out_grad, w_send, w_keep, hbm(dh2_own), hbm(resid), hbm(ctx), out_weight, vecs, rows=512
    )
    oth_recv = swap(oth_send, "core")
    blocks = t // 512

    def layer_out_part(first, count, before, *ready):
        return in_part(
            layer_out_body, 512, first, count, (hbm(gated_own), hbm(after(resid, *ready)), hbm(gated_oth)),
            (down_weight, w_send, hbm(w_keep), vecs), before, 4 * half * d, "layer_out",
        )

    def in_grad_part(first, count, before, *ready):
        return in_part(
            in_grad_body, 512, first, count, (dj, tokens, hbm(after(dattn, *ready))), (qkv_free, vecs), before,
            3 * d * d, "in_grad",
        )

    block = shape((4, d // 2, half), BF)
    u_keep, u_send = on_chip(split_body, [block] * 2, at, own_keep, own_recv, oth_keep, oth_recv, name="split")
    u_recv = swap(u_send, u0[0], u1[0])
    dj, q_keep, q_send = attn_bwd(
        place, hbm(joined), hbm(after(dctx, u_keep)), segment_ids, hbm(n1t), qkv_weight, hbm(gout), gub_own, gub_oth, vec,
        rows=512,
    )
    q_recv = swap(q_send, "core")
    u_keep, u_send = halve(at, 2, u_keep, after(u_recv, q_send))
    u_recv = swap(u_send, u0[1], u1[1])
    in_grad = in_grad_part(0, blocks // 2, None, u_keep)
    q_keep, q_send = halve(at, 7, q_keep, after(q_recv, in_grad))
    q_recv = swap(q_send, q0[0], q1[0])
    in_grad = in_grad_part(blocks // 2, blocks // 2, in_grad, q_keep)
    u_keep, u_send = halve(at, 4, u_keep, after(u_recv, in_grad))
    u_recv = swap(u_send, u0[2], u1[2])
    q_keep, q_send = halve(at, 8, q_keep, after(q_recv, u_keep))
    q_recv = swap(q_send, q0[1], q1[1])
    u_one = plus(u_keep, after(u_recv, q_keep))
    u_recv = swap(u_one, u0[3], u1[3])
    q_keep, q_send = halve(at, 9, q_keep, after(q_recv, u_one))
    q_recv = swap(q_send, q0[2], q1[2])
    layer_out = layer_out_part(0, blocks // 2, None, q_keep)
    q_one = plus(q_keep, after(q_recv, layer_out))
    for k in range(3, len(u0)):
        q_recv = swap(q_one, q0[k], q1[k])
        u_one = plus(u_one, after(u_recv, q_one))
        if k + 1 < len(u0):
            u_recv = swap(u_one, u0[k + 1], u1[k + 1])
            q_one = plus(q_one, after(q_recv, u_one))
    u_ag = swap(u_one, u0[2], u1[2])
    q_one = plus(q_one, after(q_recv, u_one))
    q_ag = swap(q_one, q0[2], q1[2])
    u_pair = jnp.concatenate([u_one, after(u_ag, q_one)], axis=0)
    u_far = swap(u_pair, u0[0], u1[1])
    u_pair_c = swap(u_pair, "core")
    q_pair = jnp.concatenate([q_one, after(q_ag, u_pair)], axis=0)
    q_ag = swap(q_pair, q0[1], q1[1])
    q_four = jnp.concatenate([q_pair, after(q_ag, u_pair)], axis=0)
    q_far = swap(q_four, q0[0], q1[0])
    q_four_c = swap(q_four, "core")
    layer_out = layer_out_part(blocks // 2, blocks // 2, layer_out, q_four)
    u_far = after(u_far, layer_out)
    u_far_c = swap(u_far, "core")
    grad_up, grad_down = on_chip(
        finish_ffn_body, [shape((d, 2 * half), F32), shape((2 * half, d), F32)], at,
        u_pair, u_far, u_pair_c, u_far_c, name="finish_ffn",
    )
    q_far = after(q_far, grad_up)
    grad_qkv, grad_qv, grad_wo, g1, c1, bo, g2, c2, gub, b2 = finish_rest(
        at, columns, q_four, q_far, q_four_c, swap(q_far, "core")
    )
    flat = lambda v: v.reshape(-1)
    return (
        layer_out, in_grad, flat(g1), flat(c1), grad_qkv, grad_qv, grad_wo, flat(bo), flat(g2), flat(c2),
        grad_up, flat(gub), grad_down, flat(b2),
    )


def solution(mesh):
    placed = (
        P(BOTH, None), P(BOTH, None), P(), P(), P(), P(), P(), P(), P(), P(),
        P(None, "mlp"), P("mlp"), P("mlp", None), P(), P(BOTH, None),
    )
    return jax.shard_map(
        functools.partial(local, mesh.shape["rows"]),
        mesh=mesh,
        in_specs=placed,
        out_specs=(
            P(BOTH, None), P(BOTH, None), P(), P(), P(), P(), P(), P(), P(), P(),
            P(None, "mlp"), P("mlp"), P("mlp", None), P(),
        ),
        check_vma=False,
    )
```

```python
import functools
import math

import jax
import jax.numpy as jnp
from jax import lax
from jax.experimental import pallas as pl
from jax.experimental.pallas import tpu as pltpu
from jax.sharding import PartitionSpec as P

BF, F32 = jnp.bfloat16, jnp.float32
SEQ, HD, FRAME = 128, 64, 4
EPS = 1e-5
C0 = math.sqrt(2.0 / math.pi)
C1 = C0 * 0.044715
LIMIT = 20 * 1024 * 1024
BOTH = ("rows", "mlp")
OWN_LIMIT = 24 * 1024 * 1024
OTHER_LIMIT = 32 * 1024 * 1024


def mm(a, b, ca=1, cb=0):
    return lax.dot_general(a, b, (((ca,), (cb,)), ((), ())), preferred_element_type=F32)


def layer_norm(x):
    c = x - jnp.mean(x, axis=-1, keepdims=True)
    inv = lax.rsqrt(jnp.mean(c * c, axis=-1, keepdims=True) + EPS)
    return c * inv, inv


def norm_back(grad, normed, inv, gain):
    s = grad * gain
    return inv * (
        s
        - jnp.mean(s, axis=-1, keepdims=True)
        - normed * jnp.mean(s * normed, axis=-1, keepdims=True)
    )


def fold(v):
    return jnp.sum(v.reshape(-1, 8, v.shape[-1]), axis=0)


def stack_heads(v):
    low = lax.broadcasted_iota(jnp.int32, v.shape, 1) < HD
    zero = jnp.zeros_like(v)
    return jnp.concatenate([jnp.where(low, v, zero), jnp.where(low, zero, v)], axis=0)


def allowed_of(seg_row, transposed):
    wide = jnp.broadcast_to(seg_row.astype(F32), (SEQ, SEQ))
    same = wide == wide.T
    a = lax.broadcasted_iota(jnp.int32, (SEQ, SEQ), 1 if transposed else 0)
    b = lax.broadcasted_iota(jnp.int32, (SEQ, SEQ), 0 if transposed else 1)
    return same & (a // FRAME >= b // FRAME)


def whole(a):
    zeros = (0,) * len(a.shape)
    return pl.BlockSpec(a.shape, lambda i, *_: zeros)


def once(a):
    zeros = (0,) * len(a.shape)
    return pl.BlockSpec(a.shape, lambda i, *_: zeros, pipeline_mode=pl.Buffered(buffer_count=1))


def rows_spec(r, w):
    return pl.BlockSpec((r, w), lambda i, *_: (i, 0))


def shape(s, dtype):
    return jax.ShapeDtypeStruct(s, dtype)


def in_hbm(s, dtype):
    return pltpu.HBM(s, dtype)


def cost(macs, nbytes=0):
    return pl.CostEstimate(flops=8 * macs, bytes_accessed=1, transcendentals=0)


def slab(ref, r, c):
    return ref[r, c * 128 : (c + 1) * 128]


def attn_fwd_body(tok, seg, vecs, wqkv, wo, joined_o, ctx_o, resid_o, h2_o, n1t_o, probs_o):
    rows, width = tok.shape
    pairs = width // 128
    vec = vecs[...].astype(F32)
    g1, b1, bo, g2, b2, bq, bv = (vec[j : j + 1] for j in range(7))
    x = tok[...].astype(F32)
    n1, _ = layer_norm(x)
    n1t_o[...] = n1.astype(BF).T
    h1 = (n1 * g1 + b1).astype(BF)
    bias = jnp.concatenate([bq, jnp.zeros_like(bq), bv], axis=1)
    joined = (mm(h1, wqkv[...]) + bias).astype(BF)
    joined_o[...] = joined
    group = 4
    done = []
    for s0 in range(0, rows // SEQ, group):
        items = [(s, p) for s in range(s0, s0 + group) for p in range(pairs)]
        allow = {s: allowed_of(seg[0, s : s + 1, :], True) for s in range(s0, s0 + group)}

        def part(s, o, p):
            return joined[s * SEQ : (s + 1) * SEQ, o * width + p * 128 : o * width + (p + 1) * 128]

        scores = [mm(part(s, 1, p), stack_heads(part(s, 0, p) * BF(0.125)), 1, 1) for s, p in items]
        probs = []
        for (s, p), sc in zip(items, scores):
            two = []
            for h in range(2):
                v = jnp.where(allow[s], sc[:, h * SEQ : (h + 1) * SEQ], -1e9)
                e = jnp.exp(v - jnp.max(v, axis=0, keepdims=True))
                two.append((e * (1.0 / jnp.sum(e, axis=0, keepdims=True))).astype(BF))
            probs.append(jnp.concatenate(two, axis=0))
            for h in range(2):
                at = (2 * p + h) * SEQ
                probs_o[s * SEQ : (s + 1) * SEQ, at : at + SEQ] = two[h]
        outs = [mm(pr, stack_heads(part(s, 2, p)), 0, 0).astype(BF) for (s, p), pr in zip(items, probs)]
        for j in range(group):
            done.append(jnp.concatenate(outs[j * pairs : (j + 1) * pairs], axis=1))
    ctx = jnp.concatenate(done, axis=0)
    ctx_o[...] = ctx
    resid = x + mm(ctx, wo[...]) + bo
    resid_o[...] = resid
    n2, _ = layer_norm(resid)
    h2_o[...] = (n2 * g2 + b2).astype(BF)


def attn_fwd(tok, seg, vecs, wqkv, wo, rows):
    t, d = tok.shape
    return pl.pallas_call(
        attn_fwd_body,
        grid=(t // rows,),
        in_specs=[rows_spec(rows, d), pl.BlockSpec((1, rows // SEQ, SEQ), lambda i: (i, 0, 0))]
        + [once(a) for a in (vecs, wqkv, wo)],
        out_specs=[rows_spec(rows, w) for w in (3 * d, d, d, d)] + [pl.BlockSpec((d, rows), lambda i: (0, i)), rows_spec(rows, 2 * d)],
        out_shape=[in_hbm((t, 3 * d), BF), in_hbm((t, d), BF), in_hbm((t, d), F32), in_hbm((t, d), BF), in_hbm((d, t), BF), in_hbm((t, 2 * d), BF)],
        compiler_params=pltpu.CompilerParams(vmem_limit_bytes=LIMIT),
        cost_estimate=cost(3 * t * d * 4 * d),
        name="attn_fwd",
    )(tok, seg.reshape(t // rows, rows // SEQ, SEQ), vecs, wqkv, wo)


def fetch_body(first, up, down, bias, out_o):
    d, half = up.shape
    out_o[0:d] = up[...]
    out_o[d : d + half] = down[...]
    bias = bias[...].astype(F32)
    bias = jnp.where(first[0] == 0, bias[0:1], bias[1:2])
    out_o[d + half :] = jnp.broadcast_to(bias, (16, half)).astype(BF)


def fetch(first, up, down, bias):
    d, f = up.shape
    half = f // 2
    return pl.pallas_call(
        fetch_body,
        grid_spec=pltpu.PrefetchScalarGridSpec(
            num_scalar_prefetch=1,
            grid=(1,),
            in_specs=[
                pl.BlockSpec((d, half), lambda i, at: (0, at[0])),
                pl.BlockSpec((half, d), lambda i, at: (at[0], 0)),
                whole(bias),
            ],
            out_specs=pl.BlockSpec((d + half + 16, half), lambda i, at: (0, 0)),
        ),
        out_shape=shape((d + half + 16, half), BF),
        compiler_params=pltpu.CompilerParams(vmem_limit_bytes=LIMIT),
        cost_estimate=cost(0, 1024 * 1024),
        name="fetch",
    )(first, up, down, bias)


def gate(v, dg, bias):
    v = v + bias
    v2 = v * v
    a = 0.5 + 0.5 * jnp.tanh(v * (C0 + C1 * v2))
    act = v * a
    slope = a + act * (1.0 - a) * (2.0 * C0 + 6.0 * C1 * v2)
    return act.astype(BF), (dg * slope).astype(BF)


def ffn_block(h2, g, up, ub, down, gated_o, dhid, gup, gdn, gub):
    f = up.shape[1]
    side, tile = 256, 64
    units = [(r, c) for r in range(0, h2.shape[0], side) for c in range(0, f, side)]

    def products(r, c):
        return mm(h2[r : r + side, :], up[:, c : c + side]), mm(g[r : r + side, :], down[c : c + side, :], 1, 1)

    ahead = products(*units[0])
    for k, (r, c) in enumerate(units):
        v, dg = ahead
        if k + 1 < len(units):
            ahead = products(*units[k + 1])
        for t in range(0, side, tile):
            act, dh = gate(v[t : t + tile], dg[t : t + tile], ub[:, c : c + side])
            gated_o[r + t : r + t + tile, c : c + side] = act
            dhid[r + t : r + t + tile, c : c + side] = dh
    dh = dhid[...]
    gup[...] += mm(h2[...].T, dh)
    gdn[...] += mm(g[...].T, gated_o[...])
    gub[...] += fold(dh.astype(F32))
    return mm(dh, up[...], 1, 1)


def put_grads(o, gup, gdn, cols):
    n = gup.shape[0] // 2
    for j in range(2):
        o[j] = gup[j * n : (j + 1) * n, cols].astype(BF)
        o[2 + j] = gdn[j * n : (j + 1) * n, cols].astype(BF)


def put_bias(o, gub):
    half = o.shape[1]
    total = jnp.sum(gub[...], axis=0, keepdims=True)
    for j in range(2):
        o[j : j + 1] = total[:, j * half : (j + 1) * half]


def ffn_own_body(core, h2, g, up, vecs, down, gated_o, dh2_o, keep_o, send_o, gub_o, gup, gdn, gub, dhid):
    i = pl.program_id(0)
    half = up.shape[1] // 2

    @pl.when(i == 0)
    def _():
        for a in (gup, gdn, gub):
            a[...] = jnp.zeros_like(a)

    bias = vecs[...].astype(F32)
    bias = jnp.concatenate([bias[8:9], bias[9:10]], axis=1)
    dh2_o[...] = ffn_block(h2, g, up, bias, down, gated_o, dhid, gup, gdn, gub)

    @pl.when(i == pl.num_programs(0) - 1)
    def _():
        put_grads(keep_o, gup, gdn, pl.ds(pl.multiple_of(core[0] * half, 128), half))
        put_grads(send_o, gup, gdn, pl.ds(pl.multiple_of((1 - core[0]) * half, 128), half))
        put_bias(gub_o, gub)


def ffn_scratch(rows, d, f):
    return [pltpu.VMEM((d, f), F32), pltpu.VMEM((d, f), F32), pltpu.VMEM((8, f), F32), pltpu.VMEM((rows, f), BF)]


def ffn_own(core, h2, g, up, vecs, down, rows):
    t, d = h2.shape
    f = up.shape[1]
    half = f // 2
    outs = [in_hbm((t, f), BF), in_hbm((t, d), F32)] + [shape((4, d // 2, half), BF)] * 2 + [shape((2, half), F32)]
    return pl.pallas_call(
        ffn_own_body,
        grid_spec=pltpu.PrefetchScalarGridSpec(
            num_scalar_prefetch=1,
            grid=(t // rows,),
            in_specs=[rows_spec(rows, d), rows_spec(rows, d), once(up), whole(vecs), once(down)],
            out_specs=[rows_spec(rows, f), rows_spec(rows, d)] + [whole(o) for o in outs[2:]],
            scratch_shapes=ffn_scratch(rows, d, f),
        ),
        out_shape=outs,
        compiler_params=pltpu.CompilerParams(vmem_limit_bytes=OWN_LIMIT),
        cost_estimate=cost(2 * 5 * t * d * f),
        name="ffn_own",
    )(core, h2, g, up, vecs, down)


def ffn_other_body(
    h2, g, w_send, w_keep, dh2_p, resid, ctx, wo, vecs,
    gated_o, dattn_o, dctx_o, keep_o, send_o, gub_o, gout_o, vec_o,
    gup, gdn, gub, dhid, up, down, ub, gout, vec,
):
    i = pl.program_id(0)
    d = h2.shape[1]
    half = w_send.shape[1]

    @pl.when(i == 0)
    def _():
        for a in (gup, gdn, gub, gout, vec):
            a[...] = jnp.zeros_like(a)
        for c, w in enumerate((w_send, w_keep)):
            up[:, c * half : (c + 1) * half] = w[0:d, :]
            down[c * half : (c + 1) * half, :] = w[d : d + half, :]
            ub[:, c * half : (c + 1) * half] = w[d + half : d + half + 16, :].astype(F32)[0:8]

    dh = dh2_p[...] + ffn_block(h2, g, up, ub[0:1], down, gated_o, dhid, gup, gdn, gub)
    n2, inv2 = layer_norm(resid[...])
    gf = g[...].astype(F32)
    dattn = (gf + norm_back(dh, n2, inv2, vecs[...].astype(F32)[3:4])).astype(BF)
    dattn_o[...] = dattn
    dctx_o[...] = mm(dattn, wo[...], 1, 1).astype(BF)
    gout[...] += mm(ctx[...].T, dattn)
    for j, v in enumerate((dattn.astype(F32), dh * n2, dh, gf)):
        vec[j] += fold(v)

    @pl.when(i == pl.num_programs(0) - 1)
    def _():
        put_grads(send_o, gup, gdn, slice(0, half))
        put_grads(keep_o, gup, gdn, slice(half, 2 * half))
        gout_o[...] = gout[...].astype(BF)
        put_bias(gub_o, gub)
        for j in range(4):
            vec_o[j : j + 1] = jnp.sum(vec[j], axis=0, keepdims=True)


def ffn_other(h2, g, w_send, w_keep, dh2_p, resid, ctx, wo, vecs, rows):
    t, d = h2.shape
    half = w_send.shape[1]
    f = 2 * half
    outs = [in_hbm((t, f), BF), in_hbm((t, d), BF), in_hbm((t, d), BF)]
    outs += [shape((4, d // 2, half), BF)] * 2 + [shape((2, half), F32), in_hbm((d, d), BF), shape((4, d), F32)]
    return pl.pallas_call(
        ffn_other_body,
        grid_spec=pltpu.PrefetchScalarGridSpec(
            num_scalar_prefetch=0,
            grid=(t // rows,),
            in_specs=[rows_spec(rows, d), rows_spec(rows, d), once(w_send), once(w_keep)]
            + [rows_spec(rows, d)] * 3
            + [once(wo), whole(vecs)],
            out_specs=[rows_spec(rows, f), rows_spec(rows, d), rows_spec(rows, d)] + [whole(o) for o in outs[3:]],
            scratch_shapes=ffn_scratch(rows, d, f)
            + [pltpu.VMEM((d, f), BF), pltpu.VMEM((f, d), BF), pltpu.VMEM((8, f), F32)]
            + [pltpu.VMEM((d, d), F32), pltpu.VMEM((4, 8, d), F32)],
        ),
        out_shape=outs,
        compiler_params=pltpu.CompilerParams(vmem_limit_bytes=OTHER_LIMIT),
        cost_estimate=cost(2 * (5 * t * d * f + 2 * t * d * d)),
        name="ffn_other",
    )(h2, g, w_send, w_keep, dh2_p, resid, ctx, wo, vecs)


def attn_bwd_block(q, k, v, dc, probs, dj_o):
    rows, width = q.shape
    pairs = width // 128
    group = 2
    for s0 in range(0, rows // SEQ, group):
        items = [(slice(s * SEQ, (s + 1) * SEQ), p) for s in range(s0, s0 + group) for p in range(pairs)]
        both = lambda r, p: probs[r, 2 * p * SEQ : 2 * (p + 1) * SEQ]
        qs = [stack_heads(slab(q, r, p) * BF(0.125)) for r, p in items]
        dcs = [stack_heads(slab(dc, r, p)) for r, p in items]
        dprobs = [mm(slab(v, r, p), a, 1, 1) for (r, p), a in zip(items, dcs)]
        dscores = []
        for (r, p), dp in zip(items, dprobs):
            pr = both(r, p).astype(F32)
            dscores.append((pr * (dp - jnp.sum(pr * dp, axis=0, keepdims=True))).astype(BF))
        for (r, p), a in zip(items, dcs):
            dj_o[r, 2 * width + p * 128 : 2 * width + (p + 1) * 128] = mm(both(r, p), a).astype(BF)
        for (r, p), ds, a in zip(items, dscores, qs):
            dj_o[r, width + p * 128 : width + (p + 1) * 128] = mm(ds, a).astype(BF)
        for (r, p), ds in zip(items, dscores):
            tall = jnp.concatenate([ds[:, 0:SEQ], ds[:, SEQ:]], axis=0)
            dq = mm(tall, stack_heads(slab(k, r, p)), 0, 0) * 0.125
            dj_o[r, p * 128 : (p + 1) * 128] = dq.astype(BF)


def ln1_parts(acc, cs, w):
    ones = jnp.ones((8, w.shape[1]), BF)
    gain = mm(ones, (acc * w.astype(F32)).astype(BF), 1, 1)[0:1]
    hi = cs.astype(BF)
    lo = (cs - hi.astype(F32)).astype(BF)
    return gain, jnp.sum(mm(hi, w, 1, 1) + mm(lo, w, 1, 1), axis=0, keepdims=True)


def attn_bwd_body(place, joined, dc, probs, n1t, wqkv, gout, gub_own, gub_oth, vec, dj_o, keep_o, send_o, acc, cs, small):
    i = pl.program_id(0)
    d = n1t.shape[0]
    step = d // 16

    @pl.when(i == 0)
    def _():
        acc[...] = jnp.zeros_like(acc)
        cs[...] = jnp.zeros_like(cs)

    q, k, v = (joined.at[:, j * d : (j + 1) * d] for j in range(3))
    attn_bwd_block(q, k, v, dc, probs, dj_o)
    dj = dj_o[...]
    acc[...] += mm(n1t[...], dj)
    cs[...] += fold(dj.astype(F32))

    @pl.when(i == pl.num_programs(0) - 1)
    def _():
        gain, bias = ln1_parts(acc[...], cs[...], wqkv[...])
        csum = jnp.sum(cs[...], axis=0, keepdims=True)
        y, c = place[0], place[1]
        small[...] = jnp.zeros_like(small)

        def put(at, row):
            n = row.shape[1] // 128
            for j in range(n):
                small[pl.ds(at + j, 1)] = row[:, j * 128 : (j + 1) * 128]

        n = d // 128
        for j in range(4):
            put(j * n, vec[j : j + 1, :])
        for j in range(2):
            put(4 * n + (2 * y + j) * n, gub_own[j : j + 1, :])
        put(4 * n + (2 * (1 - y) + 1 - c) * n, gub_oth[0:1, :])
        put(4 * n + (2 * (1 - y) + c) * n, gub_oth[1:2, :])
        put(8 * n, csum)
        put(11 * n, gain)
        put(12 * n, bias)
        for o, core in ((keep_o, c), (send_o, 1 - c)):
            for b in range(8):
                where = pl.ds(pl.multiple_of((8 * core + b) * step, step), step)
                o[b, :, 0 : 3 * d] = acc[where, :].astype(BF)
                o[b, :, 3 * d : 4 * d] = gout[where, :]
                o[b, :, 4 * d :] = jnp.zeros((step, 128), BF)

        @pl.when(c == 0)
        def _():
            for b in range(2):
                keep_o[b, :, 4 * d :] = small[b * step : (b + 1) * step].astype(BF)

        @pl.when(c == 1)
        def _():
            for b in range(2):
                send_o[b, :, 4 * d :] = small[b * step : (b + 1) * step].astype(BF)


def attn_bwd(place, joined, dctx, probs, n1t, wqkv, gout, gub_own, gub_oth, vec, rows):
    d, t = n1t.shape
    outs = [pltpu.VMEM((t, 3 * d), BF)] + [shape((8, d // 16, 4 * d + 128), BF)] * 2
    rest = (wqkv, gout, gub_own, gub_oth, vec)
    return pl.pallas_call(
        attn_bwd_body,
        grid_spec=pltpu.PrefetchScalarGridSpec(
            num_scalar_prefetch=1,
            grid=(t // rows,),
            in_specs=[
                rows_spec(rows, 3 * d),
                rows_spec(rows, d),
                rows_spec(rows, 2 * d),
                pl.BlockSpec((d, rows), lambda i, *_: (0, i)),
            ]
            + [once(a) for a in rest],
            out_specs=[rows_spec(rows, 3 * d)] + [whole(o) for o in outs[1:]],
            scratch_shapes=[pltpu.VMEM((d, 3 * d), F32), pltpu.VMEM((8, 3 * d), F32), pltpu.VMEM((64, 128), F32)],
        ),
        out_shape=outs,
        compiler_params=pltpu.CompilerParams(vmem_limit_bytes=LIMIT + 8 * 1024 * 1024),
        cost_estimate=cost(8 * t * d * 3 * d),
        name="attn_bwd",
    )(place, joined, dctx, probs, n1t, *rest)


def in_grad_body(dj, tok, dattn, wqkv, vecs, *refs):
    dh1 = mm(dj[...], wqkv[...], 1, 1)
    n1, inv1 = layer_norm(tok[...].astype(F32))
    gain = vecs[...].astype(F32)[0:1]
    refs[-1][...] = (dattn[...].astype(F32) + norm_back(dh1, n1, inv1, gain)).astype(BF)


def in_part(body, rows, first, count, streams, fixed, before, macs, name):
    t, d = streams[1].shape
    spec = lambda w: pl.BlockSpec((rows, w), lambda i: (i + first, 0))
    args = (*streams, *fixed) + (() if before is None else (before,))
    return pl.pallas_call(
        body,
        grid=(count,),
        in_specs=[spec(a.shape[1]) for a in streams]
        + [once(a) for a in fixed]
        + ([] if before is None else [pl.BlockSpec(memory_space=pl.ANY)]),
        out_specs=spec(d),
        out_shape=in_hbm((t, d), BF),
        input_output_aliases={} if before is None else {len(args) - 1: 0},
        compiler_params=pltpu.CompilerParams(vmem_limit_bytes=LIMIT),
        cost_estimate=cost(2 * rows * count * macs),
        name=name,
    )(*args)


def layer_out_body(own, resid, oth, down, w_send, w_keep, vecs, *refs):
    d = resid.shape[1]
    half = w_send.shape[1]
    out = mm(own[...], down[...])
    out += mm(oth[:, 0:half], w_send[d : d + half, :]) + mm(oth[:, half:], w_keep[d : d + half, :])
    refs[-1][...] = (resid[...] + out + vecs[...].astype(F32)[7:8]).astype(BF)


def on_chip(body, outs, at, *args, name):
    return pl.pallas_call(
        body,
        in_specs=[pl.BlockSpec(memory_space=pltpu.SMEM)] + [pl.BlockSpec(memory_space=pltpu.VMEM)] * len(args),
        out_specs=[pl.BlockSpec(memory_space=pltpu.VMEM)] * len(outs),
        out_shape=outs,
        compiler_params=pltpu.CompilerParams(vmem_limit_bytes=24 * 1024 * 1024),
        cost_estimate=cost(0, 4 * 1024 * 1024),
        name=name,
    )(at, *args)


def plus(a, b):
    return (a.astype(F32) + b.astype(F32)).astype(BF)


def split_body(at, own_a, own_b, oth_a, oth_b, keep_o, send_o):
    def total(o, j):
        a, b = (own_a, own_b) if o == 0 else (oth_a, oth_b)
        return plus(a[j], b[j])

    @pl.when(at[0] == 0)
    def _():
        v = at[1]
        for o in range(2):
            for p in range(2):
                keep_o[2 * o + p] = total(o, 2 * v + p)
                send_o[2 * o + p] = total(o, 2 * (1 - v) + p)

    @pl.when(at[0] == 1)
    def _():
        for j in range(4):
            keep_o[j] = total(0, j)
            send_o[j] = total(1, j)


def halve(at, which, a, b):
    n = a.shape[0] // 2

    def body(at, a, b, keep_o, send_o):
        v = at[which]
        for j in range(n):
            keep_o[j] = plus(a[v * n + j], b[v * n + j])
            send_o[j] = plus(a[(1 - v) * n + j], b[(1 - v) * n + j])

    return on_chip(body, [shape((n, *a.shape[1:]), BF)] * 2, at, a, b, name="halve")


def finish_ffn_body(at, *refs):
    up_o, down_o = refs[4:]
    quarter = refs[0].shape[1]
    for c in range(2):

        @pl.when(pl.program_id(0) == c)
        def _(c=c):
            for j in range(2):
                pair = refs[2 * c + j]
                which = at[3 + 2 * c] if j == 0 else 1 - at[3 + 2 * c]
                for i in range(2):
                    part = at[4 + 2 * c] if i == 0 else 1 - at[4 + 2 * c]
                    cols = pl.ds(pl.multiple_of(part * quarter, 128), quarter)

                    @pl.when(which == 0)
                    def _(pair=pair, i=i, cols=cols):
                        up_o[cols, :] = pair[i].astype(F32)

                    @pl.when(which == 1)
                    def _(pair=pair, i=i, cols=cols):
                        down_o[:, cols] = pair[i].astype(F32).T


def finish_ffn(at, *pairs):
    half = pairs[0].shape[2]
    d = 2 * pairs[0].shape[1]
    unit = lambda i, at: jnp.where(i == 0, at[0], 1 - at[0])
    return pl.pallas_call(
        finish_ffn_body,
        grid_spec=pltpu.PrefetchScalarGridSpec(
            num_scalar_prefetch=1,
            grid=(2,),
            in_specs=[whole(a) for a in pairs],
            out_specs=[
                pl.BlockSpec((d, half), lambda i, at: (0, unit(i, at))),
                pl.BlockSpec((half, d), lambda i, at: (unit(i, at), 0)),
            ],
        ),
        out_shape=[shape((d, 2 * half), F32), shape((2 * half, d), F32)],
        compiler_params=pltpu.CompilerParams(vmem_limit_bytes=24 * 1024 * 1024),
        cost_estimate=cost(0, 4 * 1024 * 1024),
        name="finish_ffn",
    )(at, *pairs)


def finish_rest_body(at, columns, *refs):
    qkv_o, qv_o, gout_o, gain1_o, bias1_o, bo_o, gain2_o, bias2_o, gub_o, b2_o, small = refs[4:]
    d = gout_o.shape[1]
    step, n = d // 16, d // 128
    pieces = []
    for c in range(2):
        core = at[0] if c == 0 else 1 - at[0]
        a0, b0, c0 = (at[7 + j] if c == 0 else at[11 + j] for j in range(3))
        for j in range(2):
            for i in range(4):
                bits = (a0 if j == 0 else 1 - a0, b0 if i < 2 else 1 - b0, c0 if i % 2 == 0 else 1 - c0)
                pieces.append((refs[2 * c + j], i, 8 * core + 4 * bits[0] + 2 * bits[1] + bits[2]))
    @pl.when(pl.program_id(0) == 0)
    def _():
        for ref, i, at_ in pieces:

            @pl.when(at_ < 2)
            def _(ref=ref, i=i, at_=at_):
                small[pl.ds(pl.multiple_of(at_ * step, step), step)] = ref[i, :, 4 * d :].astype(F32)

    def row(first, count):
        return jnp.concatenate([small[first + j : first + j + 1] for j in range(count)], axis=1)

    csum = row(8 * n, 3 * n)
    for c in range(2):

        @pl.when(pl.program_id(0) == c)
        def _(c=c):
            for ref, i, at_ in pieces[8 * c : 8 * c + 8]:
                rows = pl.ds(pl.multiple_of(at_ * step, step), step)
                here = pl.ds(pl.multiple_of((at_ % 8) * step, step), step)
                gain, bias = columns[rows, 0:1], columns[rows, 1:2]
                qkv_o[here, :] = ref[i, :, 0 : 3 * d].astype(F32) * gain + bias * csum
                gout_o[here, :] = ref[i, :, 3 * d : 4 * d].astype(F32)

    @pl.when(pl.program_id(0) == 0)
    def _():
        qv_o[0:1] = csum[:, 0:d]
        qv_o[1:2] = csum[:, 2 * d :]
        for o, j in ((bo_o, 0), (gain2_o, 1), (bias2_o, 2), (b2_o, 3)):
            o[...] = row(j * n, n)
        gain1_o[...] = row(11 * n, n)
        bias1_o[...] = row(12 * n, n)
        first = 4 * n + 2 * n * at[10]
        for j in range(2 * n):
            gub_o[:, j * 128 : (j + 1) * 128] = small[pl.ds(first + j, 1)]


def finish_rest(at, columns, *pieces):
    d = columns.shape[0]
    one = shape((1, d), F32)
    outs = [shape((d, 3 * d), F32), shape((2, d), F32), shape((d, d), F32)] + [one] * 5 + [shape((1, 2 * d), F32), one]
    args = (columns, *pieces)
    half = lambda i, at: (jnp.where(i == 0, at[0], 1 - at[0]), 0)
    return pl.pallas_call(
        finish_rest_body,
        grid_spec=pltpu.PrefetchScalarGridSpec(
            num_scalar_prefetch=1,
            grid=(2,),
            in_specs=[whole(a) for a in args],
            out_specs=[pl.BlockSpec((d // 2, 3 * d), half), whole(outs[1]), pl.BlockSpec((d // 2, d), half)]
            + [whole(o) for o in outs[3:]],
            scratch_shapes=[pltpu.VMEM((64, 128), F32)],
        ),
        out_shape=outs,
        compiler_params=pltpu.CompilerParams(vmem_limit_bytes=24 * 1024 * 1024),
        cost_estimate=cost(0, 8 * 1024 * 1024),
        name="finish_rest",
    )(at, *args)


def local(
    n_rows,
    tokens,
    segment_ids,
    ln1_gain,
    ln1_bias,
    qkv_weight,
    qv_bias,
    out_weight,
    out_bias,
    ln2_gain,
    ln2_bias,
    up_weight,
    up_bias,
    down_weight,
    down_bias,
    out_grad,
):
    t, d = tokens.shape
    half = up_weight.shape[1] // 2
    r, y = lax.axis_index("rows"), lax.axis_index("mlp")
    core = r & 1
    up_dims = n_rows.bit_length() - 2

    def flip(dim, row, m):
        if dim == "core":
            return row ^ 1, m
        if dim == "y":
            return row, m ^ 1
        return row ^ (2 << dim), m

    def bit(dim):
        return y if dim == "y" else (r >> (dim + 1)) & 1

    def swap(value, *dims):
        pairs = []
        for row in range(n_rows):
            for m in range(2):
                row2, m2 = flip(dims[0] if row & 1 == 0 else dims[-1], row, m)
                pairs.append((row * 2 + m, row2 * 2 + m2))
        return lax.ppermute(value, BOTH, pairs)

    def by_core(first, second):
        return jnp.where(core == 0, first, second)

    def after(value, *done):
        return lax.optimization_barrier((value, *done))[0]

    u0 = [0, "y"] + list(range(1, up_dims))
    u1 = ["y", 1, 0] + list(range(2, up_dims))
    q0 = ["y", 1, 0, 2] + list(range(3, up_dims))
    q1 = [0, "y", 1, 2] + list(range(3, up_dims))
    at = jnp.stack(
        [core, bit(0), by_core(0, bit(u1[1]))]
        + [by_core(bit(u0[0]), bit(u1[1])), by_core(bit(u0[2]), bit(u1[2]))]
        + [by_core(bit(u1[1]), bit(u0[0])), by_core(bit(u1[2]), bit(u0[2]))]
        + [by_core(bit(a), bit(b)) for a, b in zip(q0[:3], q1[:3])]
        + [y]
        + [by_core(bit(b), bit(a)) for a, b in zip(q0[:3], q1[:3])]
    ).astype(jnp.int32)
    place = jnp.stack([y, core]).astype(jnp.int32)
    core_s = core.reshape(1).astype(jnp.int32)
    hbm = lambda v: pltpu.with_memory_space_constraint(v, pltpu.HBM)
    qkv_free, down_free = qkv_weight, down_weight
    tokens, out_grad, qkv_weight, out_weight, up_weight, down_weight = map(
        hbm, (tokens, out_grad, qkv_weight, out_weight, up_weight, down_weight)
    )

    bias = up_bias.reshape(2, half)
    vecs = jnp.concatenate(
        [
            jnp.stack([ln1_gain, ln1_bias, out_bias, ln2_gain, ln2_bias, qv_bias[0], qv_bias[1], down_bias]),
            bias,
            jnp.zeros((6, d), BF),
        ]
    )
    columns = jnp.stack([ln1_gain, ln1_bias], axis=1).astype(F32)

    w_send = swap(fetch(1 - core_s, up_weight, down_weight, bias), "y")
    joined, ctx, resid, h2, n1t, probs = attn_fwd(tokens, segment_ids, vecs, qkv_weight, out_weight, rows=512)
    gated_own, dh2_own, own_keep, own_send, gub_own = ffn_own(
        core_s, hbm(h2), out_grad, up_weight, vecs, down_weight, rows=512
    )
    w_send = hbm(after(w_send, own_send))
    w_keep = swap(w_send, "core")
    own_recv = swap(own_send, "core")
    gated_oth, dattn, dctx, oth_keep, oth_send, gub_oth, gout, vec = ffn_other(
        hbm(h2), out_grad, w_send, w_keep, hbm(dh2_own), hbm(resid), hbm(ctx), out_weight, vecs, rows=512
    )
    oth_recv = swap(oth_send, "core")
    blocks = t // 512

    def layer_out_part(first, count, before, *ready):
        return in_part(
            layer_out_body, 512, first, count, (hbm(gated_own), hbm(after(resid, *ready)), hbm(gated_oth)),
            (down_weight, w_send, hbm(w_keep), vecs), before, 4 * half * d, "layer_out",
        )

    def in_grad_part(first, count, before, *ready):
        return in_part(
            in_grad_body, 512, first, count, (dj, tokens, hbm(after(dattn, *ready))), (qkv_free, vecs), before,
            3 * d * d, "in_grad",
        )

    block = shape((4, d // 2, half), BF)
    u_keep, u_send = on_chip(split_body, [block] * 2, at, own_keep, own_recv, oth_keep, oth_recv, name="split")
    u_recv = swap(u_send, u0[0], u1[0])
    dj, q_keep, q_send = attn_bwd(
        place, hbm(joined), hbm(after(dctx, u_keep)), hbm(probs), hbm(n1t), qkv_weight, hbm(gout), gub_own, gub_oth, vec,
        rows=512,
    )
    q_recv = swap(q_send, "core")
    u_keep, u_send = halve(at, 2, u_keep, after(u_recv, q_send))
    u_recv = swap(u_send, u0[1], u1[1])
    in_grad = in_grad_part(0, blocks // 2, None, u_keep)
    q_keep, q_send = halve(at, 7, q_keep, after(q_recv, in_grad))
    q_recv = swap(q_send, q0[0], q1[0])
    in_grad = in_grad_part(blocks // 2, blocks // 2, in_grad, q_keep)
    u_keep, u_send = halve(at, 4, u_keep, after(u_recv, in_grad))
    u_recv = swap(u_send, u0[2], u1[2])
    q_keep, q_send = halve(at, 8, q_keep, after(q_recv, u_keep))
    q_recv = swap(q_send, q0[1], q1[1])
    u_one = plus(u_keep, after(u_recv, q_keep))
    u_recv = swap(u_one, u0[3], u1[3])
    q_keep, q_send = halve(at, 9, q_keep, after(q_recv, u_one))
    q_recv = swap(q_send, q0[2], q1[2])
    layer_out = layer_out_part(0, blocks // 2, None, q_keep)
    q_one = plus(q_keep, after(q_recv, layer_out))
    for k in range(3, len(u0)):
        q_recv = swap(q_one, q0[k], q1[k])
        u_one = plus(u_one, after(u_recv, q_one))
        if k + 1 < len(u0):
            u_recv = swap(u_one, u0[k + 1], u1[k + 1])
            q_one = plus(q_one, after(q_recv, u_one))
    u_ag = swap(u_one, u0[2], u1[2])
    q_one = plus(q_one, after(q_recv, u_one))
    q_ag = swap(q_one, q0[2], q1[2])
    u_pair = jnp.concatenate([u_one, after(u_ag, q_one)], axis=0)
    u_far = swap(u_pair, u0[0], u1[1])
    u_pair_c = swap(u_pair, "core")
    q_pair = jnp.concatenate([q_one, after(q_ag, u_pair)], axis=0)
    q_ag = swap(q_pair, q0[1], q1[1])
    q_four = jnp.concatenate([q_pair, after(q_ag, u_pair)], axis=0)
    q_far = swap(q_four, q0[0], q1[0])
    q_four_c = swap(q_four, "core")
    layer_out = layer_out_part(blocks // 2, blocks // 2, layer_out, q_four)
    u_far = after(u_far, layer_out)
    u_far_c = swap(u_far, "core")
    grad_up, grad_down = finish_ffn(at, u_pair, u_far, u_pair_c, u_far_c)
    q_far = after(q_far, grad_up)
    grad_qkv, grad_qv, grad_wo, g1, c1, bo, g2, c2, gub, b2 = finish_rest(
        at, columns, q_four, q_far, q_four_c, swap(q_far, "core")
    )
    flat = lambda v: v.reshape(-1)
    return (
        layer_out, in_grad, flat(g1), flat(c1), grad_qkv, grad_qv, grad_wo, flat(bo), flat(g2), flat(c2),
        grad_up, flat(gub), grad_down, flat(b2),
    )


def solution(mesh):
    placed = (
        P(BOTH, None), P(BOTH, None), P(), P(), P(), P(), P(), P(), P(), P(),
        P(None, "mlp"), P("mlp"), P("mlp", None), P(), P(BOTH, None),
    )
    return jax.shard_map(
        functools.partial(local, mesh.shape["rows"]),
        mesh=mesh,
        in_specs=placed,
        out_specs=(
            P(BOTH, None), P(BOTH, None), P(), P(), P(), P(), P(), P(), P(), P(),
            P(None, "mlp"), P("mlp"), P("mlp", None), P(),
        ),
        check_vma=False,
    )
```

```python
import functools
import math

import jax
import jax.numpy as jnp
from jax import lax
from jax.experimental import pallas as pl
from jax.experimental.pallas import tpu as pltpu
from jax.sharding import PartitionSpec as P

BF, F32 = jnp.bfloat16, jnp.float32
SEQ, HD, FRAME = 128, 64, 4
EPS = 1e-5
C0 = math.sqrt(2.0 / math.pi)
C1 = C0 * 0.044715
LIMIT = 20 * 1024 * 1024
BOTH = ("rows", "mlp")
OWN_LIMIT = 24 * 1024 * 1024
OTHER_LIMIT = 32 * 1024 * 1024


def mm(a, b, ca=1, cb=0):
    return lax.dot_general(a, b, (((ca,), (cb,)), ((), ())), preferred_element_type=F32)


def layer_norm(x):
    c = x - jnp.mean(x, axis=-1, keepdims=True)
    inv = lax.rsqrt(jnp.mean(c * c, axis=-1, keepdims=True) + EPS)
    return c * inv, inv


def norm_back(grad, normed, inv, gain):
    s = grad * gain
    return inv * (
        s
        - jnp.mean(s, axis=-1, keepdims=True)
        - normed * jnp.mean(s * normed, axis=-1, keepdims=True)
    )


def fold(v):
    return jnp.sum(v.reshape(-1, 8, v.shape[-1]), axis=0)


def stack_heads(v):
    low = lax.broadcasted_iota(jnp.int32, v.shape, 1) < HD
    zero = jnp.zeros_like(v)
    return jnp.concatenate([jnp.where(low, v, zero), jnp.where(low, zero, v)], axis=0)


def allowed_of(seg_row, transposed):
    wide = jnp.broadcast_to(seg_row.astype(F32), (SEQ, SEQ))
    same = wide == wide.T
    a = lax.broadcasted_iota(jnp.int32, (SEQ, SEQ), 1 if transposed else 0)
    b = lax.broadcasted_iota(jnp.int32, (SEQ, SEQ), 0 if transposed else 1)
    return same & (a // FRAME >= b // FRAME)


def whole(a):
    zeros = (0,) * len(a.shape)
    return pl.BlockSpec(a.shape, lambda i, *_: zeros)


def once(a):
    zeros = (0,) * len(a.shape)
    return pl.BlockSpec(a.shape, lambda i, *_: zeros, pipeline_mode=pl.Buffered(buffer_count=1))


def rows_spec(r, w):
    return pl.BlockSpec((r, w), lambda i, *_: (i, 0))


def shape(s, dtype):
    return jax.ShapeDtypeStruct(s, dtype)


def in_hbm(s, dtype):
    return pltpu.HBM(s, dtype)


def cost(macs, nbytes=0):
    return pl.CostEstimate(flops=8 * macs, bytes_accessed=1, transcendentals=0)


def slab(ref, r, c):
    return ref[r, c * 128 : (c + 1) * 128]


def attn_fwd_body(tok, seg, vecs, wqkv, wo, joined_o, ctx_o, resid_o, h2_o, n1t_o, probs_o):
    rows, width = tok.shape
    pairs = width // 128
    vec = vecs[...].astype(F32)
    g1, b1, bo, g2, b2, bq, bv = (vec[j : j + 1] for j in range(7))
    x = tok[...].astype(F32)
    n1, _ = layer_norm(x)
    n1t_o[...] = n1.astype(BF).T
    h1 = (n1 * g1 + b1).astype(BF)
    bias = jnp.concatenate([bq, jnp.zeros_like(bq), bv], axis=1)
    joined = (mm(h1, wqkv[...]) + bias).astype(BF)
    joined_o[...] = joined
    group = 4
    done = []
    for s0 in range(0, rows // SEQ, group):
        items = [(s, p) for s in range(s0, s0 + group) for p in range(pairs)]
        allow = {s: allowed_of(seg[0, s : s + 1, :], True) for s in range(s0, s0 + group)}

        def part(s, o, p):
            return joined[s * SEQ : (s + 1) * SEQ, o * width + p * 128 : o * width + (p + 1) * 128]

        scores = [mm(part(s, 1, p), stack_heads(part(s, 0, p) * BF(0.125)), 1, 1) for s, p in items]
        probs = []
        for (s, p), sc in zip(items, scores):
            two = []
            for h in range(2):
                v = jnp.where(allow[s], sc[:, h * SEQ : (h + 1) * SEQ], -1e9)
                e = jnp.exp(v - jnp.max(v, axis=0, keepdims=True))
                two.append((e * (1.0 / jnp.sum(e, axis=0, keepdims=True))).astype(BF))
            probs.append(jnp.concatenate(two, axis=0))
            for h in range(2):
                at = (2 * p + h) * SEQ
                probs_o[s * SEQ : (s + 1) * SEQ, at : at + SEQ] = two[h]
        outs = [mm(pr, stack_heads(part(s, 2, p)), 0, 0).astype(BF) for (s, p), pr in zip(items, probs)]
        for j in range(group):
            done.append(jnp.concatenate(outs[j * pairs : (j + 1) * pairs], axis=1))
    ctx = jnp.concatenate(done, axis=0)
    ctx_o[...] = ctx
    resid = x + mm(ctx, wo[...]) + bo
    resid_o[...] = resid
    n2, _ = layer_norm(resid)
    h2_o[...] = (n2 * g2 + b2).astype(BF)


def attn_fwd(tok, seg, vecs, wqkv, wo, rows):
    t, d = tok.shape
    return pl.pallas_call(
        attn_fwd_body,
        grid=(t // rows,),
        in_specs=[rows_spec(rows, d), pl.BlockSpec((1, rows // SEQ, SEQ), lambda i: (i, 0, 0))]
        + [once(a) for a in (vecs, wqkv, wo)],
        out_specs=[rows_spec(rows, w) for w in (3 * d, d, d, d)] + [pl.BlockSpec((d, rows), lambda i: (0, i)), rows_spec(rows, 2 * d)],
        out_shape=[in_hbm((t, 3 * d), BF), in_hbm((t, d), BF), in_hbm((t, d), F32), pltpu.VMEM((t, d), BF), in_hbm((d, t), BF), in_hbm((t, 2 * d), BF)],
        compiler_params=pltpu.CompilerParams(vmem_limit_bytes=LIMIT),
        cost_estimate=cost(3 * t * d * 4 * d),
        name="attn_fwd",
    )(tok, seg.reshape(t // rows, rows // SEQ, SEQ), vecs, wqkv, wo)


def fetch_body(first, up, down, bias, out_o):
    d, half = up.shape
    out_o[0:d] = up[...]
    out_o[d : d + half] = down[...]
    bias = bias[...].astype(F32)
    bias = jnp.where(first[0] == 0, bias[0:1], bias[1:2])
    out_o[d + half :] = jnp.broadcast_to(bias, (16, half)).astype(BF)


def fetch(first, up, down, bias):
    d, f = up.shape
    half = f // 2
    return pl.pallas_call(
        fetch_body,
        grid_spec=pltpu.PrefetchScalarGridSpec(
            num_scalar_prefetch=1,
            grid=(1,),
            in_specs=[
                pl.BlockSpec((d, half), lambda i, at: (0, at[0])),
                pl.BlockSpec((half, d), lambda i, at: (at[0], 0)),
                whole(bias),
            ],
            out_specs=pl.BlockSpec((d + half + 16, half), lambda i, at: (0, 0)),
        ),
        out_shape=shape((d + half + 16, half), BF),
        compiler_params=pltpu.CompilerParams(vmem_limit_bytes=LIMIT),
        cost_estimate=cost(0, 1024 * 1024),
        name="fetch",
    )(first, up, down, bias)


def gate(v, dg, bias):
    v = v + bias
    v2 = v * v
    a = 0.5 + 0.5 * jnp.tanh(v * (C0 + C1 * v2))
    act = v * a
    slope = a + act * (1.0 - a) * (2.0 * C0 + 6.0 * C1 * v2)
    return act.astype(BF), (dg * slope).astype(BF)


def ffn_block(h2, g, up, ub, down, gated_o, dhid, gup, gdn, gub):
    f = up.shape[1]
    side, tile = 256, 64
    units = [(r, c) for r in range(0, h2.shape[0], side) for c in range(0, f, side)]

    def products(r, c):
        return mm(h2[r : r + side, :], up[:, c : c + side]), mm(g[r : r + side, :], down[c : c + side, :], 1, 1)

    ahead = products(*units[0])
    for k, (r, c) in enumerate(units):
        v, dg = ahead
        if k + 1 < len(units):
            ahead = products(*units[k + 1])
        for t in range(0, side, tile):
            act, dh = gate(v[t : t + tile], dg[t : t + tile], ub[:, c : c + side])
            gated_o[r + t : r + t + tile, c : c + side] = act
            dhid[r + t : r + t + tile, c : c + side] = dh
    dh = dhid[...]
    gup[...] += mm(h2[...].T, dh)
    gdn[...] += mm(g[...].T, gated_o[...])
    gub[...] += fold(dh.astype(F32))
    return mm(dh, up[...], 1, 1)


def put_grads(o, gup, gdn, cols):
    n = gup.shape[0] // 2
    for j in range(2):
        o[j] = gup[j * n : (j + 1) * n, cols].astype(BF)
        o[2 + j] = gdn[j * n : (j + 1) * n, cols].astype(BF)


def put_bias(o, gub):
    half = o.shape[1]
    total = jnp.sum(gub[...], axis=0, keepdims=True)
    for j in range(2):
        o[j : j + 1] = total[:, j * half : (j + 1) * half]


def ffn_own_body(core, h2, g, up, vecs, down, gated_o, dh2_o, keep_o, send_o, gub_o, gup, gdn, gub, dhid):
    i = pl.program_id(0)
    half = up.shape[1] // 2

    @pl.when(i == 0)
    def _():
        for a in (gup, gdn, gub):
            a[...] = jnp.zeros_like(a)

    bias = vecs[...].astype(F32)
    bias = jnp.concatenate([bias[8:9], bias[9:10]], axis=1)
    dh2_o[...] = ffn_block(h2, g, up, bias, down, gated_o, dhid, gup, gdn, gub)

    @pl.when(i == pl.num_programs(0) - 1)
    def _():
        put_grads(keep_o, gup, gdn, pl.ds(pl.multiple_of(core[0] * half, 128), half))
        put_grads(send_o, gup, gdn, pl.ds(pl.multiple_of((1 - core[0]) * half, 128), half))
        put_bias(gub_o, gub)


def ffn_scratch(rows, d, f):
    return [pltpu.VMEM((d, f), F32), pltpu.VMEM((d, f), F32), pltpu.VMEM((8, f), F32), pltpu.VMEM((rows, f), BF)]


def ffn_own(core, h2, g, up, vecs, down, rows):
    t, d = h2.shape
    f = up.shape[1]
    half = f // 2
    outs = [in_hbm((t, f), BF), pltpu.VMEM((t, d), F32)] + [shape((4, d // 2, half), BF)] * 2 + [shape((2, half), F32)]
    return pl.pallas_call(
        ffn_own_body,
        grid_spec=pltpu.PrefetchScalarGridSpec(
            num_scalar_prefetch=1,
            grid=(t // rows,),
            in_specs=[rows_spec(rows, d), rows_spec(rows, d), once(up), whole(vecs), once(down)],
            out_specs=[rows_spec(rows, f), rows_spec(rows, d)] + [whole(o) for o in outs[2:]],
            scratch_shapes=ffn_scratch(rows, d, f),
        ),
        out_shape=outs,
        compiler_params=pltpu.CompilerParams(vmem_limit_bytes=OWN_LIMIT),
        cost_estimate=cost(2 * 5 * t * d * f),
        name="ffn_own",
    )(core, h2, g, up, vecs, down)


def ffn_other_body(
    h2, g, w_send, w_keep, dh2_p, resid, ctx, wo, vecs,
    gated_o, dattn_o, dctx_o, keep_o, send_o, gub_o, gout_o, vec_o,
    gup, gdn, gub, dhid, up, down, ub, gout, vec,
):
    i = pl.program_id(0)
    d = h2.shape[1]
    half = w_send.shape[1]

    @pl.when(i == 0)
    def _():
        for a in (gup, gdn, gub, gout, vec):
            a[...] = jnp.zeros_like(a)
        for c, w in enumerate((w_send, w_keep)):
            up[:, c * half : (c + 1) * half] = w[0:d, :]
            down[c * half : (c + 1) * half, :] = w[d : d + half, :]
            ub[:, c * half : (c + 1) * half] = w[d + half : d + half + 16, :].astype(F32)[0:8]

    dh = dh2_p[...] + ffn_block(h2, g, up, ub[0:1], down, gated_o, dhid, gup, gdn, gub)
    n2, inv2 = layer_norm(resid[...])
    gf = g[...].astype(F32)
    dattn = (gf + norm_back(dh, n2, inv2, vecs[...].astype(F32)[3:4])).astype(BF)
    dattn_o[...] = dattn
    dctx_o[...] = mm(dattn, wo[...], 1, 1).astype(BF)
    gout[...] += mm(ctx[...].T, dattn)
    for j, v in enumerate((dattn.astype(F32), dh * n2, dh, gf)):
        vec[j] += fold(v)

    @pl.when(i == pl.num_programs(0) - 1)
    def _():
        put_grads(send_o, gup, gdn, slice(0, half))
        put_grads(keep_o, gup, gdn, slice(half, 2 * half))
        gout_o[...] = gout[...].astype(BF)
        put_bias(gub_o, gub)
        for j in range(4):
            vec_o[j : j + 1] = jnp.sum(vec[j], axis=0, keepdims=True)


def ffn_other(h2, g, w_send, w_keep, dh2_p, resid, ctx, wo, vecs, rows):
    t, d = h2.shape
    half = w_send.shape[1]
    f = 2 * half
    outs = [in_hbm((t, f), BF), in_hbm((t, d), BF), in_hbm((t, d), BF)]
    outs += [shape((4, d // 2, half), BF)] * 2 + [shape((2, half), F32), in_hbm((d, d), BF), shape((4, d), F32)]
    return pl.pallas_call(
        ffn_other_body,
        grid_spec=pltpu.PrefetchScalarGridSpec(
            num_scalar_prefetch=0,
            grid=(t // rows,),
            in_specs=[rows_spec(rows, d), rows_spec(rows, d), once(w_send), once(w_keep)]
            + [rows_spec(rows, d)] * 3
            + [once(wo), whole(vecs)],
            out_specs=[rows_spec(rows, f), rows_spec(rows, d), rows_spec(rows, d)] + [whole(o) for o in outs[3:]],
            scratch_shapes=ffn_scratch(rows, d, f)
            + [pltpu.VMEM((d, f), BF), pltpu.VMEM((f, d), BF), pltpu.VMEM((8, f), F32)]
            + [pltpu.VMEM((d, d), F32), pltpu.VMEM((4, 8, d), F32)],
        ),
        out_shape=outs,
        compiler_params=pltpu.CompilerParams(vmem_limit_bytes=OTHER_LIMIT),
        cost_estimate=cost(2 * (5 * t * d * f + 2 * t * d * d)),
        name="ffn_other",
    )(h2, g, w_send, w_keep, dh2_p, resid, ctx, wo, vecs)


def attn_bwd_block(q, k, v, dc, probs, dj_o):
    rows, width = q.shape
    pairs = width // 128
    group = 2
    for s0 in range(0, rows // SEQ, group):
        items = [(slice(s * SEQ, (s + 1) * SEQ), p) for s in range(s0, s0 + group) for p in range(pairs)]
        both = lambda r, p: probs[r, 2 * p * SEQ : 2 * (p + 1) * SEQ]
        qs = [stack_heads(slab(q, r, p) * BF(0.125)) for r, p in items]
        dcs = [stack_heads(slab(dc, r, p)) for r, p in items]
        dprobs = [mm(slab(v, r, p), a, 1, 1) for (r, p), a in zip(items, dcs)]
        dscores = []
        for (r, p), dp in zip(items, dprobs):
            pr = both(r, p).astype(F32)
            dscores.append((pr * (dp - jnp.sum(pr * dp, axis=0, keepdims=True))).astype(BF))
        for (r, p), a in zip(items, dcs):
            dj_o[r, 2 * width + p * 128 : 2 * width + (p + 1) * 128] = mm(both(r, p), a).astype(BF)
        for (r, p), ds, a in zip(items, dscores, qs):
            dj_o[r, width + p * 128 : width + (p + 1) * 128] = mm(ds, a).astype(BF)
        for (r, p), ds in zip(items, dscores):
            tall = jnp.concatenate([ds[:, 0:SEQ], ds[:, SEQ:]], axis=0)
            dq = mm(tall, stack_heads(slab(k, r, p)), 0, 0) * 0.125
            dj_o[r, p * 128 : (p + 1) * 128] = dq.astype(BF)


def ln1_parts(acc, cs, w):
    def parts(v):
        hi = v.astype(BF)
        return hi, (v - hi.astype(F32)).astype(BF)

    narrow = sum(acc[:, j : j + 128] * w[:, j : j + 128].astype(F32) for j in range(0, w.shape[1], 128))
    ones = jnp.ones((16, 128), BF)
    gain = sum(mm(ones, v, 1, 1) for v in parts(narrow))[0:1]
    bias = mm(jnp.concatenate(parts(cs), axis=0), w, 1, 1)
    return gain, jnp.sum(bias, axis=0, keepdims=True)


def attn_bwd_body(place, joined, dc, probs, n1t, wqkv, gout, gub_own, gub_oth, vec, dj_o, keep_o, send_o, acc, cs, small):
    i = pl.program_id(0)
    d = n1t.shape[0]
    step = d // 16

    @pl.when(i == 0)
    def _():
        acc[...] = jnp.zeros_like(acc)
        cs[...] = jnp.zeros_like(cs)

    q, k, v = (joined.at[:, j * d : (j + 1) * d] for j in range(3))
    attn_bwd_block(q, k, v, dc, probs, dj_o)
    dj = dj_o[...]
    acc[...] += mm(n1t[...], dj)
    cs[...] += fold(dj.astype(F32))

    @pl.when(i == pl.num_programs(0) - 1)
    def _():
        gain, bias = ln1_parts(acc[...], cs[...], wqkv[...])
        csum = jnp.sum(cs[...], axis=0, keepdims=True)
        y, c = place[0], place[1]
        small[...] = jnp.zeros_like(small)

        def put(at, row):
            n = row.shape[1] // 128
            for j in range(n):
                small[pl.ds(at + j, 1)] = row[:, j * 128 : (j + 1) * 128]

        n = d // 128
        for j in range(4):
            put(j * n, vec[j : j + 1, :])
        for j in range(2):
            put(4 * n + (2 * y + j) * n, gub_own[j : j + 1, :])
        put(4 * n + (2 * (1 - y) + 1 - c) * n, gub_oth[0:1, :])
        put(4 * n + (2 * (1 - y) + c) * n, gub_oth[1:2, :])
        put(8 * n, csum)
        put(11 * n, gain)
        put(12 * n, bias)
        for o, core in ((keep_o, c), (send_o, 1 - c)):
            for b in range(8):
                where = pl.ds(pl.multiple_of((8 * core + b) * step, step), step)
                o[b, :, 0 : 3 * d] = acc[where, :].astype(BF)
                o[b, :, 3 * d : 4 * d] = gout[where, :]
                o[b, :, 4 * d :] = jnp.zeros((step, 128), BF)

        @pl.when(c == 0)
        def _():
            for b in range(2):
                keep_o[b, :, 4 * d :] = small[b * step : (b + 1) * step].astype(BF)

        @pl.when(c == 1)
        def _():
            for b in range(2):
                send_o[b, :, 4 * d :] = small[b * step : (b + 1) * step].astype(BF)


def attn_bwd(place, joined, dctx, probs, n1t, wqkv, gout, gub_own, gub_oth, vec, rows):
    d, t = n1t.shape
    outs = [pltpu.VMEM((t, 3 * d), BF)] + [shape((8, d // 16, 4 * d + 128), BF)] * 2
    rest = (wqkv, gout, gub_own, gub_oth, vec)
    return pl.pallas_call(
        attn_bwd_body,
        grid_spec=pltpu.PrefetchScalarGridSpec(
            num_scalar_prefetch=1,
            grid=(t // rows,),
            in_specs=[
                rows_spec(rows, 3 * d),
                rows_spec(rows, d),
                rows_spec(rows, 2 * d),
                pl.BlockSpec((d, rows), lambda i, *_: (0, i)),
            ]
            + [once(a) for a in rest],
            out_specs=[rows_spec(rows, 3 * d)] + [whole(o) for o in outs[1:]],
            scratch_shapes=[pltpu.VMEM((d, 3 * d), F32), pltpu.VMEM((8, 3 * d), F32), pltpu.VMEM((64, 128), F32)],
        ),
        out_shape=outs,
        compiler_params=pltpu.CompilerParams(vmem_limit_bytes=LIMIT + 8 * 1024 * 1024),
        cost_estimate=cost(8 * t * d * 3 * d),
        name="attn_bwd",
    )(place, joined, dctx, probs, n1t, *rest)


def in_grad_body(dj, tok, dattn, wqkv, vecs, *refs):
    dh1 = mm(dj[...], wqkv[...], 1, 1)
    n1, inv1 = layer_norm(tok[...].astype(F32))
    gain = vecs[...].astype(F32)[0:1]
    refs[-1][...] = (dattn[...].astype(F32) + norm_back(dh1, n1, inv1, gain)).astype(BF)


def in_part(body, rows, first, count, streams, fixed, before, macs, name):
    t, d = streams[1].shape
    spec = lambda w: pl.BlockSpec((rows, w), lambda i: (i + first, 0))
    args = (*streams, *fixed) + (() if before is None else (before,))
    return pl.pallas_call(
        body,
        grid=(count,),
        in_specs=[spec(a.shape[1]) for a in streams]
        + [once(a) for a in fixed]
        + ([] if before is None else [pl.BlockSpec(memory_space=pl.ANY)]),
        out_specs=spec(d),
        out_shape=in_hbm((t, d), BF),
        input_output_aliases={} if before is None else {len(args) - 1: 0},
        compiler_params=pltpu.CompilerParams(vmem_limit_bytes=LIMIT),
        cost_estimate=cost(2 * rows * count * macs),
        name=name,
    )(*args)


def layer_out_body(own, resid, oth, down, w_send, w_keep, vecs, *refs):
    d = resid.shape[1]
    half = w_send.shape[1]
    out = mm(own[...], down[...])
    out += mm(oth[:, 0:half], w_send[d : d + half, :]) + mm(oth[:, half:], w_keep[d : d + half, :])
    refs[-1][...] = (resid[...] + out + vecs[...].astype(F32)[7:8]).astype(BF)


def on_chip(body, outs, at, *args, name):
    return pl.pallas_call(
        body,
        in_specs=[pl.BlockSpec(memory_space=pltpu.SMEM)] + [pl.BlockSpec(memory_space=pltpu.VMEM)] * len(args),
        out_specs=[pl.BlockSpec(memory_space=pltpu.VMEM)] * len(outs),
        out_shape=outs,
        compiler_params=pltpu.CompilerParams(vmem_limit_bytes=24 * 1024 * 1024),
        cost_estimate=cost(0, 4 * 1024 * 1024),
        name=name,
    )(at, *args)


def plus(a, b):
    return (a.astype(F32) + b.astype(F32)).astype(BF)


def split_body(at, own_a, own_b, oth_a, oth_b, keep_o, send_o):
    def total(o, j):
        a, b = (own_a, own_b) if o == 0 else (oth_a, oth_b)
        return plus(a[j], b[j])

    @pl.when(at[0] == 0)
    def _():
        v = at[1]
        for o in range(2):
            for p in range(2):
                keep_o[2 * o + p] = total(o, 2 * v + p)
                send_o[2 * o + p] = total(o, 2 * (1 - v) + p)

    @pl.when(at[0] == 1)
    def _():
        for j in range(4):
            keep_o[j] = total(0, j)
            send_o[j] = total(1, j)


def halve(at, which, a, b):
    n = a.shape[0] // 2

    def body(at, a, b, keep_o, send_o):
        v = at[which]
        for j in range(n):
            keep_o[j] = plus(a[v * n + j], b[v * n + j])
            send_o[j] = plus(a[(1 - v) * n + j], b[(1 - v) * n + j])

    return on_chip(body, [shape((n, *a.shape[1:]), BF)] * 2, at, a, b, name="halve")


def finish_ffn_body(at, *refs):
    up_o, down_o = refs[4:]
    quarter = refs[0].shape[1]
    for c in range(2):

        @pl.when(pl.program_id(0) == c)
        def _(c=c):
            for j in range(2):
                pair = refs[2 * c + j]
                which = at[3 + 2 * c] if j == 0 else 1 - at[3 + 2 * c]
                for i in range(2):
                    part = at[4 + 2 * c] if i == 0 else 1 - at[4 + 2 * c]
                    cols = pl.ds(pl.multiple_of(part * quarter, 128), quarter)

                    @pl.when(which == 0)
                    def _(pair=pair, i=i, cols=cols):
                        up_o[cols, :] = pair[i].astype(F32)

                    @pl.when(which == 1)
                    def _(pair=pair, i=i, cols=cols):
                        down_o[:, cols] = pair[i].astype(F32).T


def finish_ffn(at, *pairs):
    half = pairs[0].shape[2]
    d = 2 * pairs[0].shape[1]
    unit = lambda i, at: jnp.where(i == 0, at[0], 1 - at[0])
    return pl.pallas_call(
        finish_ffn_body,
        grid_spec=pltpu.PrefetchScalarGridSpec(
            num_scalar_prefetch=1,
            grid=(2,),
            in_specs=[whole(a) for a in pairs],
            out_specs=[
                pl.BlockSpec((d, half), lambda i, at: (0, unit(i, at))),
                pl.BlockSpec((half, d), lambda i, at: (unit(i, at), 0)),
            ],
        ),
        out_shape=[shape((d, 2 * half), F32), shape((2 * half, d), F32)],
        compiler_params=pltpu.CompilerParams(vmem_limit_bytes=24 * 1024 * 1024),
        cost_estimate=cost(0, 4 * 1024 * 1024),
        name="finish_ffn",
    )(at, *pairs)


def finish_rest_body(at, columns, *refs):
    qkv_o, qv_o, gout_o, gain1_o, bias1_o, bo_o, gain2_o, bias2_o, gub_o, b2_o, small = refs[4:]
    d = gout_o.shape[1]
    step, n = d // 16, d // 128
    pieces = []
    for c in range(2):
        core = at[0] if c == 0 else 1 - at[0]
        a0, b0, c0 = (at[7 + j] if c == 0 else at[11 + j] for j in range(3))
        for j in range(2):
            for i in range(4):
                bits = (a0 if j == 0 else 1 - a0, b0 if i < 2 else 1 - b0, c0 if i % 2 == 0 else 1 - c0)
                pieces.append((refs[2 * c + j], i, 8 * core + 4 * bits[0] + 2 * bits[1] + bits[2]))
    @pl.when(pl.program_id(0) == 0)
    def _():
        for ref, i, at_ in pieces:

            @pl.when(at_ < 2)
            def _(ref=ref, i=i, at_=at_):
                small[pl.ds(pl.multiple_of(at_ * step, step), step)] = ref[i, :, 4 * d :].astype(F32)

    def row(first, count):
        return jnp.concatenate([small[first + j : first + j + 1] for j in range(count)], axis=1)

    csum = row(8 * n, 3 * n)
    for c in range(2):

        @pl.when(pl.program_id(0) == c)
        def _(c=c):
            for ref, i, at_ in pieces[8 * c : 8 * c + 8]:
                rows = pl.ds(pl.multiple_of(at_ * step, step), step)
                here = pl.ds(pl.multiple_of((at_ % 8) * step, step), step)
                gain, bias = columns[rows, 0:1], columns[rows, 1:2]
                qkv_o[here, :] = ref[i, :, 0 : 3 * d].astype(F32) * gain + bias * csum
                gout_o[here, :] = ref[i, :, 3 * d : 4 * d].astype(F32)

    @pl.when(pl.program_id(0) == 0)
    def _():
        qv_o[0:1] = csum[:, 0:d]
        qv_o[1:2] = csum[:, 2 * d :]
        for o, j in ((bo_o, 0), (gain2_o, 1), (bias2_o, 2), (b2_o, 3)):
            o[...] = row(j * n, n)
        gain1_o[...] = row(11 * n, n)
        bias1_o[...] = row(12 * n, n)
        first = 4 * n + 2 * n * at[10]
        for j in range(2 * n):
            gub_o[:, j * 128 : (j + 1) * 128] = small[pl.ds(first + j, 1)]


def finish_rest(at, columns, *pieces):
    d = columns.shape[0]
    one = shape((1, d), F32)
    outs = [shape((d, 3 * d), F32), shape((2, d), F32), shape((d, d), F32)] + [one] * 5 + [shape((1, 2 * d), F32), one]
    args = (columns, *pieces)
    half = lambda i, at: (jnp.where(i == 0, at[0], 1 - at[0]), 0)
    return pl.pallas_call(
        finish_rest_body,
        grid_spec=pltpu.PrefetchScalarGridSpec(
            num_scalar_prefetch=1,
            grid=(2,),
            in_specs=[whole(a) for a in args],
            out_specs=[pl.BlockSpec((d // 2, 3 * d), half), whole(outs[1]), pl.BlockSpec((d // 2, d), half)]
            + [whole(o) for o in outs[3:]],
            scratch_shapes=[pltpu.VMEM((64, 128), F32)],
        ),
        out_shape=outs,
        compiler_params=pltpu.CompilerParams(vmem_limit_bytes=24 * 1024 * 1024),
        cost_estimate=cost(0, 8 * 1024 * 1024),
        name="finish_rest",
    )(at, *args)


def local(
    n_rows,
    tokens,
    segment_ids,
    ln1_gain,
    ln1_bias,
    qkv_weight,
    qv_bias,
    out_weight,
    out_bias,
    ln2_gain,
    ln2_bias,
    up_weight,
    up_bias,
    down_weight,
    down_bias,
    out_grad,
):
    t, d = tokens.shape
    half = up_weight.shape[1] // 2
    r, y = lax.axis_index("rows"), lax.axis_index("mlp")
    core = r & 1
    up_dims = n_rows.bit_length() - 2

    def flip(dim, row, m):
        if dim == "core":
            return row ^ 1, m
        if dim == "y":
            return row, m ^ 1
        return row ^ (2 << dim), m

    def bit(dim):
        return y if dim == "y" else (r >> (dim + 1)) & 1

    def swap(value, *dims):
        pairs = []
        for row in range(n_rows):
            for m in range(2):
                row2, m2 = flip(dims[0] if row & 1 == 0 else dims[-1], row, m)
                pairs.append((row * 2 + m, row2 * 2 + m2))
        return lax.ppermute(value, BOTH, pairs)

    def by_core(first, second):
        return jnp.where(core == 0, first, second)

    def after(value, *done):
        return lax.optimization_barrier((value, *done))[0]

    u0 = [0, "y"] + list(range(1, up_dims))
    u1 = ["y", 1, 0] + list(range(2, up_dims))
    q0 = ["y", 1, 0, 2] + list(range(3, up_dims))
    q1 = [0, "y", 1, 2] + list(range(3, up_dims))
    at = jnp.stack(
        [core, bit(0), by_core(0, bit(u1[1]))]
        + [by_core(bit(u0[0]), bit(u1[1])), by_core(bit(u0[2]), bit(u1[2]))]
        + [by_core(bit(u1[1]), bit(u0[0])), by_core(bit(u1[2]), bit(u0[2]))]
        + [by_core(bit(a), bit(b)) for a, b in zip(q0[:3], q1[:3])]
        + [y]
        + [by_core(bit(b), bit(a)) for a, b in zip(q0[:3], q1[:3])]
    ).astype(jnp.int32)
    place = jnp.stack([y, core]).astype(jnp.int32)
    core_s = core.reshape(1).astype(jnp.int32)
    hbm = lambda v: pltpu.with_memory_space_constraint(v, pltpu.HBM)
    vmem = lambda v: pltpu.with_memory_space_constraint(v, pltpu.VMEM)
    qkv_free, down_free = qkv_weight, down_weight
    tokens, out_grad, qkv_weight, out_weight, up_weight, down_weight = map(
        hbm, (tokens, out_grad, qkv_weight, out_weight, up_weight, down_weight)
    )

    bias = up_bias.reshape(2, half)
    vecs = jnp.concatenate(
        [
            jnp.stack([ln1_gain, ln1_bias, out_bias, ln2_gain, ln2_bias, qv_bias[0], qv_bias[1], down_bias]),
            bias,
            jnp.zeros((6, d), BF),
        ]
    )
    columns = jnp.stack([ln1_gain, ln1_bias], axis=1).astype(F32)

    w_send = swap(fetch(1 - core_s, up_weight, down_weight, bias), "y")
    joined, ctx, resid, h2, n1t, probs = attn_fwd(tokens, segment_ids, vecs, qkv_weight, out_weight, rows=512)
    gated_own, dh2_own, own_keep, own_send, gub_own = ffn_own(
        core_s, vmem(h2), out_grad, up_weight, vecs, down_weight, rows=512
    )
    w_send = hbm(after(w_send, own_send))
    w_keep = swap(w_send, "core")
    own_recv = swap(own_send, "core")
    gated_oth, dattn, dctx, oth_keep, oth_send, gub_oth, gout, vec = ffn_other(
        vmem(h2), out_grad, w_send, w_keep, vmem(dh2_own), hbm(resid), hbm(ctx), out_weight, vecs, rows=512
    )
    oth_recv = swap(oth_send, "core")
    blocks = t // 512

    def layer_out_part(first, count, before, *ready):
        return in_part(
            layer_out_body, 512, first, count, (hbm(gated_own), hbm(after(resid, *ready)), hbm(gated_oth)),
            (down_weight, w_send, hbm(w_keep), vecs), before, 4 * half * d, "layer_out",
        )

    def in_grad_part(first, count, before, *ready):
        return in_part(
            in_grad_body, 512, first, count, (dj, tokens, hbm(after(dattn, *ready))), (qkv_free, vecs), before,
            3 * d * d, "in_grad",
        )

    block = shape((4, d // 2, half), BF)
    u_keep, u_send = on_chip(split_body, [block] * 2, at, own_keep, own_recv, oth_keep, oth_recv, name="split")
    u_recv = swap(u_send, u0[0], u1[0])
    dj, q_keep, q_send = attn_bwd(
        place, hbm(joined), hbm(after(dctx, u_keep)), hbm(probs), hbm(n1t), qkv_weight, hbm(gout), gub_own, gub_oth, vec,
        rows=512,
    )
    q_recv = swap(q_send, "core")
    u_keep, u_send = halve(at, 2, u_keep, after(u_recv, q_send))
    u_recv = swap(u_send, u0[1], u1[1])
    in_grad = in_grad_part(0, blocks // 2, None, u_keep)
    q_keep, q_send = halve(at, 7, q_keep, after(q_recv, in_grad))
    q_recv = swap(q_send, q0[0], q1[0])
    in_grad = in_grad_part(blocks // 2, blocks // 2, in_grad, q_keep)
    u_keep, u_send = halve(at, 4, u_keep, after(u_recv, in_grad))
    u_recv = swap(u_send, u0[2], u1[2])
    q_keep, q_send = halve(at, 8, q_keep, after(q_recv, u_keep))
    q_recv = swap(q_send, q0[1], q1[1])
    u_one = plus(u_keep, after(u_recv, q_keep))
    u_recv = swap(u_one, u0[3], u1[3])
    q_keep, q_send = halve(at, 9, q_keep, after(q_recv, u_one))
    q_recv = swap(q_send, q0[2], q1[2])
    layer_out = layer_out_part(0, blocks // 2, None, q_keep)
    q_one = plus(q_keep, after(q_recv, layer_out))
    for k in range(3, len(u0)):
        q_recv = swap(q_one, q0[k], q1[k])
        u_one = plus(u_one, after(u_recv, q_one))
        if k + 1 < len(u0):
            u_recv = swap(u_one, u0[k + 1], u1[k + 1])
            q_one = plus(q_one, after(q_recv, u_one))
    u_ag = swap(u_one, u0[2], u1[2])
    q_one = plus(q_one, after(q_recv, u_one))
    q_ag = swap(q_one, q0[2], q1[2])
    u_pair = jnp.concatenate([u_one, after(u_ag, q_one)], axis=0)
    u_far = swap(u_pair, u0[0], u1[1])
    u_pair_c = swap(u_pair, "core")
    q_pair = jnp.concatenate([q_one, after(q_ag, u_pair)], axis=0)
    q_ag = swap(q_pair, q0[1], q1[1])
    q_four = jnp.concatenate([q_pair, after(q_ag, u_pair)], axis=0)
    q_far = swap(q_four, q0[0], q1[0])
    q_four_c = swap(q_four, "core")
    layer_out = layer_out_part(blocks // 2, blocks // 2, layer_out, q_four)
    u_far = after(u_far, layer_out)
    u_far_c = swap(u_far, "core")
    grad_up, grad_down = finish_ffn(at, u_pair, u_far, u_pair_c, u_far_c)
    q_far = after(q_far, grad_up)
    grad_qkv, grad_qv, grad_wo, g1, c1, bo, g2, c2, gub, b2 = finish_rest(
        at, columns, q_four, q_far, q_four_c, swap(q_far, "core")
    )
    flat = lambda v: v.reshape(-1)
    return (
        layer_out, in_grad, flat(g1), flat(c1), grad_qkv, grad_qv, grad_wo, flat(bo), flat(g2), flat(c2),
        grad_up, flat(gub), grad_down, flat(b2),
    )


def solution(mesh):
    placed = (
        P(BOTH, None), P(BOTH, None), P(), P(), P(), P(), P(), P(), P(), P(),
        P(None, "mlp"), P("mlp"), P("mlp", None), P(), P(BOTH, None),
    )
    return jax.shard_map(
        functools.partial(local, mesh.shape["rows"]),
        mesh=mesh,
        in_specs=placed,
        out_specs=(
            P(BOTH, None), P(BOTH, None), P(), P(), P(), P(), P(), P(), P(), P(),
            P(None, "mlp"), P("mlp"), P("mlp", None), P(),
        ),
        check_vma=False,
    )
```

```python
import functools
import math

import jax
import jax.numpy as jnp
from jax import lax
from jax.experimental import pallas as pl
from jax.experimental.pallas import tpu as pltpu
from jax.sharding import PartitionSpec as P

BF, F32 = jnp.bfloat16, jnp.float32
SEQ, HD, FRAME = 128, 64, 4
EPS = 1e-5
C0 = math.sqrt(2.0 / math.pi)
C1 = C0 * 0.044715
LIMIT = 20 * 1024 * 1024
BOTH = ("rows", "mlp")
OWN_LIMIT = 24 * 1024 * 1024
OTHER_LIMIT = 32 * 1024 * 1024


def mm(a, b, ca=1, cb=0):
    return lax.dot_general(a, b, (((ca,), (cb,)), ((), ())), preferred_element_type=F32)


def layer_norm(x):
    c = x - jnp.mean(x, axis=-1, keepdims=True)
    inv = lax.rsqrt(jnp.mean(c * c, axis=-1, keepdims=True) + EPS)
    return c * inv, inv


def norm_back(grad, normed, inv, gain):
    s = grad * gain
    return inv * (
        s
        - jnp.mean(s, axis=-1, keepdims=True)
        - normed * jnp.mean(s * normed, axis=-1, keepdims=True)
    )


def fold(v):
    return jnp.sum(v.reshape(-1, 8, v.shape[-1]), axis=0)


def stack_heads(v):
    low = lax.broadcasted_iota(jnp.int32, v.shape, 1) < HD
    zero = jnp.zeros_like(v)
    return jnp.concatenate([jnp.where(low, v, zero), jnp.where(low, zero, v)], axis=0)


def allowed_of(seg_row, transposed):
    wide = jnp.broadcast_to(seg_row.astype(F32), (SEQ, SEQ))
    same = wide == wide.T
    a = lax.broadcasted_iota(jnp.int32, (SEQ, SEQ), 1 if transposed else 0)
    b = lax.broadcasted_iota(jnp.int32, (SEQ, SEQ), 0 if transposed else 1)
    return same & (a // FRAME >= b // FRAME)


def whole(a):
    zeros = (0,) * len(a.shape)
    return pl.BlockSpec(a.shape, lambda i, *_: zeros)


def once(a):
    zeros = (0,) * len(a.shape)
    return pl.BlockSpec(a.shape, lambda i, *_: zeros, pipeline_mode=pl.Buffered(buffer_count=1))


def rows_spec(r, w):
    return pl.BlockSpec((r, w), lambda i, *_: (i, 0))


def shape(s, dtype):
    return jax.ShapeDtypeStruct(s, dtype)


def in_hbm(s, dtype):
    return pltpu.HBM(s, dtype)


def cost(macs, nbytes=0):
    return pl.CostEstimate(flops=8 * macs, bytes_accessed=1, transcendentals=0)


def slab(ref, r, c):
    return ref[r, c * 128 : (c + 1) * 128]


def attn_fwd_body(tok, seg, vecs, wqkv, wo, joined_o, ctx_o, resid_o, h2_o, n1t_o, probs_o):
    rows, width = tok.shape
    pairs = width // 128
    vec = vecs[...].astype(F32)
    g1, b1, bo, g2, b2, bq, bv = (vec[j : j + 1] for j in range(7))
    x = tok[...].astype(F32)
    n1, _ = layer_norm(x)
    n1t_o[...] = n1.astype(BF).T
    h1 = (n1 * g1 + b1).astype(BF)
    bias = jnp.concatenate([bq, jnp.zeros_like(bq), bv], axis=1)
    joined = (mm(h1, wqkv[...]) + bias).astype(BF)
    joined_o[...] = joined
    group = 4
    done = []
    for s0 in range(0, rows // SEQ, group):
        items = [(s, p) for s in range(s0, s0 + group) for p in range(pairs)]
        allow = {s: allowed_of(seg[0, s : s + 1, :], True) for s in range(s0, s0 + group)}

        def part(s, o, p):
            return joined[s * SEQ : (s + 1) * SEQ, o * width + p * 128 : o * width + (p + 1) * 128]

        scores = [mm(part(s, 1, p), stack_heads(part(s, 0, p) * BF(0.125)), 1, 1) for s, p in items]
        probs = []
        for (s, p), sc in zip(items, scores):
            two = []
            for h in range(2):
                v = jnp.where(allow[s], sc[:, h * SEQ : (h + 1) * SEQ], -1e9)
                e = jnp.exp(v - jnp.max(v, axis=0, keepdims=True))
                two.append((e * (1.0 / jnp.sum(e, axis=0, keepdims=True))).astype(BF))
            probs.append(jnp.concatenate(two, axis=0))
            for h in range(2):
                at = (2 * p + h) * SEQ
                probs_o[s * SEQ : (s + 1) * SEQ, at : at + SEQ] = two[h]
        outs = [mm(pr, stack_heads(part(s, 2, p)), 0, 0).astype(BF) for (s, p), pr in zip(items, probs)]
        for j in range(group):
            done.append(jnp.concatenate(outs[j * pairs : (j + 1) * pairs], axis=1))
    ctx = jnp.concatenate(done, axis=0)
    ctx_o[...] = ctx
    resid = x + mm(ctx, wo[...]) + bo
    resid_o[...] = resid
    n2, _ = layer_norm(resid)
    h2_o[...] = (n2 * g2 + b2).astype(BF)


def attn_fwd(tok, seg, vecs, wqkv, wo, rows):
    t, d = tok.shape
    return pl.pallas_call(
        attn_fwd_body,
        grid=(t // rows,),
        in_specs=[rows_spec(rows, d), pl.BlockSpec((1, rows // SEQ, SEQ), lambda i: (i, 0, 0))]
        + [once(a) for a in (vecs, wqkv, wo)],
        out_specs=[rows_spec(rows, w) for w in (3 * d, d, d, d)] + [pl.BlockSpec((d, rows), lambda i: (0, i)), rows_spec(rows, 2 * d)],
        out_shape=[in_hbm((t, 3 * d), BF), in_hbm((t, d), BF), in_hbm((t, d), F32), pltpu.VMEM((t, d), BF), in_hbm((d, t), BF), in_hbm((t, 2 * d), BF)],
        compiler_params=pltpu.CompilerParams(vmem_limit_bytes=LIMIT),
        cost_estimate=cost(3 * t * d * 4 * d),
        name="attn_fwd",
    )(tok, seg.reshape(t // rows, rows // SEQ, SEQ), vecs, wqkv, wo)


def fetch_body(first, up, down, bias, out_o):
    d, half = up.shape
    out_o[0:d] = up[...]
    out_o[d : d + half] = down[...]
    bias = bias[...].astype(F32)
    bias = jnp.where(first[0] == 0, bias[0:1], bias[1:2])
    out_o[d + half :] = jnp.broadcast_to(bias, (16, half)).astype(BF)


def fetch(first, up, down, bias):
    d, f = up.shape
    half = f // 2
    return pl.pallas_call(
        fetch_body,
        grid_spec=pltpu.PrefetchScalarGridSpec(
            num_scalar_prefetch=1,
            grid=(1,),
            in_specs=[
                pl.BlockSpec((d, half), lambda i, at: (0, at[0])),
                pl.BlockSpec((half, d), lambda i, at: (at[0], 0)),
                whole(bias),
            ],
            out_specs=pl.BlockSpec((d + half + 16, half), lambda i, at: (0, 0)),
        ),
        out_shape=shape((d + half + 16, half), BF),
        compiler_params=pltpu.CompilerParams(vmem_limit_bytes=LIMIT),
        cost_estimate=cost(0, 1024 * 1024),
        name="fetch",
    )(first, up, down, bias)


def gate(v, dg, bias):
    v = v + bias
    v2 = v * v
    a = 0.5 + 0.5 * jnp.tanh(v * (C0 + C1 * v2))
    act = v * a
    slope = a + act * (1.0 - a) * (2.0 * C0 + 6.0 * C1 * v2)
    return act.astype(BF), (dg * slope).astype(BF)


def ffn_block(h2, g, up, ub, down, gated_o, dhid, gup, gdn, gub):
    f = up.shape[1]
    side, tile = 256, 64
    units = [(r, c) for r in range(0, h2.shape[0], side) for c in range(0, f, side)]

    def products(r, c):
        return mm(h2[r : r + side, :], up[:, c : c + side]), mm(g[r : r + side, :], down[c : c + side, :], 1, 1)

    ahead = products(*units[0])
    for k, (r, c) in enumerate(units):
        v, dg = ahead
        if k + 1 < len(units):
            ahead = products(*units[k + 1])
        for t in range(0, side, tile):
            act, dh = gate(v[t : t + tile], dg[t : t + tile], ub[:, c : c + side])
            gated_o[r + t : r + t + tile, c : c + side] = act
            dhid[r + t : r + t + tile, c : c + side] = dh
    dh = dhid[...]
    gup[...] += mm(h2[...].T, dh)
    gdn[...] += mm(g[...].T, gated_o[...])
    gub[...] += fold(dh.astype(F32))
    return mm(dh, up[...], 1, 1)


def put_grads(o, gup, gdn, cols):
    n = gup.shape[0] // 2
    for j in range(2):
        o[j] = gup[j * n : (j + 1) * n, cols].astype(BF)
        o[2 + j] = gdn[j * n : (j + 1) * n, cols].astype(BF)


def put_bias(o, gub):
    half = o.shape[1]
    total = jnp.sum(gub[...], axis=0, keepdims=True)
    for j in range(2):
        o[j : j + 1] = total[:, j * half : (j + 1) * half]


def ffn_own_body(core, h2, g, up, vecs, down, gated_o, dh2_o, keep_o, send_o, gub_o, gup, gdn, gub, dhid):
    i = pl.program_id(0)
    half = up.shape[1] // 2

    @pl.when(i == 0)
    def _():
        for a in (gup, gdn, gub):
            a[...] = jnp.zeros_like(a)

    bias = vecs[...].astype(F32)
    bias = jnp.concatenate([bias[8:9], bias[9:10]], axis=1)
    dh2_o[...] = ffn_block(h2, g, up, bias, down, gated_o, dhid, gup, gdn, gub)

    @pl.when(i == pl.num_programs(0) - 1)
    def _():
        put_grads(keep_o, gup, gdn, pl.ds(pl.multiple_of(core[0] * half, 128), half))
        put_grads(send_o, gup, gdn, pl.ds(pl.multiple_of((1 - core[0]) * half, 128), half))
        put_bias(gub_o, gub)


def ffn_scratch(rows, d, f):
    return [pltpu.VMEM((d, f), F32), pltpu.VMEM((d, f), F32), pltpu.VMEM((8, f), F32), pltpu.VMEM((rows, f), BF)]


def ffn_own(core, h2, g, up, vecs, down, rows):
    t, d = h2.shape
    f = up.shape[1]
    half = f // 2
    outs = [in_hbm((t, f), BF), pltpu.VMEM((t, d), F32)] + [shape((4, d // 2, half), BF)] * 2 + [shape((2, half), F32)]
    return pl.pallas_call(
        ffn_own_body,
        grid_spec=pltpu.PrefetchScalarGridSpec(
            num_scalar_prefetch=1,
            grid=(t // rows,),
            in_specs=[rows_spec(rows, d), rows_spec(rows, d), once(up), whole(vecs), once(down)],
            out_specs=[rows_spec(rows, f), rows_spec(rows, d)] + [whole(o) for o in outs[2:]],
            scratch_shapes=ffn_scratch(rows, d, f),
        ),
        out_shape=outs,
        compiler_params=pltpu.CompilerParams(vmem_limit_bytes=OWN_LIMIT),
        cost_estimate=cost(2 * 5 * t * d * f),
        name="ffn_own",
    )(core, h2, g, up, vecs, down)


def ffn_other_body(
    h2, g, w_send, w_keep, dh2_p, resid, ctx, wo, vecs,
    gated_o, dattn_o, dctx_o, keep_o, send_o, gub_o, gout_o, vec_o,
    gup, gdn, gub, dhid, up, down, ub, gout, vec,
):
    i = pl.program_id(0)
    d = h2.shape[1]
    half = w_send.shape[1]

    @pl.when(i == 0)
    def _():
        for a in (gup, gdn, gub, gout, vec):
            a[...] = jnp.zeros_like(a)
        for c, w in enumerate((w_send, w_keep)):
            up[:, c * half : (c + 1) * half] = w[0:d, :]
            down[c * half : (c + 1) * half, :] = w[d : d + half, :]
            ub[:, c * half : (c + 1) * half] = w[d + half : d + half + 16, :].astype(F32)[0:8]

    dh = dh2_p[...] + ffn_block(h2, g, up, ub[0:1], down, gated_o, dhid, gup, gdn, gub)
    n2, inv2 = layer_norm(resid[...])
    gf = g[...].astype(F32)
    dattn = (gf + norm_back(dh, n2, inv2, vecs[...].astype(F32)[3:4])).astype(BF)
    dattn_o[...] = dattn
    dctx_o[...] = mm(dattn, wo[...], 1, 1).astype(BF)
    gout[...] += mm(ctx[...].T, dattn)
    for j, v in enumerate((dattn.astype(F32), dh * n2, dh, gf)):
        vec[j] += fold(v)

    @pl.when(i == pl.num_programs(0) - 1)
    def _():
        put_grads(send_o, gup, gdn, slice(0, half))
        put_grads(keep_o, gup, gdn, slice(half, 2 * half))
        gout_o[...] = gout[...].astype(BF)
        put_bias(gub_o, gub)
        for j in range(4):
            vec_o[j : j + 1] = jnp.sum(vec[j], axis=0, keepdims=True)


def ffn_other(h2, g, w_send, w_keep, dh2_p, resid, ctx, wo, vecs, rows):
    t, d = h2.shape
    half = w_send.shape[1]
    f = 2 * half
    outs = [in_hbm((t, f), BF), in_hbm((t, d), BF), in_hbm((t, d), BF)]
    outs += [shape((4, d // 2, half), BF)] * 2 + [shape((2, half), F32), in_hbm((d, d), BF), shape((4, d), F32)]
    return pl.pallas_call(
        ffn_other_body,
        grid_spec=pltpu.PrefetchScalarGridSpec(
            num_scalar_prefetch=0,
            grid=(t // rows,),
            in_specs=[rows_spec(rows, d), rows_spec(rows, d), once(w_send), once(w_keep)]
            + [rows_spec(rows, d)] * 3
            + [once(wo), whole(vecs)],
            out_specs=[rows_spec(rows, f), rows_spec(rows, d), rows_spec(rows, d)] + [whole(o) for o in outs[3:]],
            scratch_shapes=ffn_scratch(rows, d, f)
            + [pltpu.VMEM((d, f), BF), pltpu.VMEM((f, d), BF), pltpu.VMEM((8, f), F32)]
            + [pltpu.VMEM((d, d), F32), pltpu.VMEM((4, 8, d), F32)],
        ),
        out_shape=outs,
        compiler_params=pltpu.CompilerParams(vmem_limit_bytes=OTHER_LIMIT),
        cost_estimate=cost(2 * (5 * t * d * f + 2 * t * d * d)),
        name="ffn_other",
    )(h2, g, w_send, w_keep, dh2_p, resid, ctx, wo, vecs)


def attn_bwd_block(q, k, v, dc, probs, dj_o):
    rows, width = q.shape
    pairs = width // 128
    group = 2
    for s0 in range(0, rows // SEQ, group):
        items = [(slice(s * SEQ, (s + 1) * SEQ), p) for s in range(s0, s0 + group) for p in range(pairs)]
        both = lambda r, p: probs[r, 2 * p * SEQ : 2 * (p + 1) * SEQ]
        qs = [stack_heads(slab(q, r, p) * BF(0.125)) for r, p in items]
        dcs = [stack_heads(slab(dc, r, p)) for r, p in items]
        dprobs = [mm(slab(v, r, p), a, 1, 1) for (r, p), a in zip(items, dcs)]
        dscores = []
        for (r, p), dp in zip(items, dprobs):
            pr = both(r, p).astype(F32)
            dscores.append((pr * (dp - jnp.sum(pr * dp, axis=0, keepdims=True))).astype(BF))
        for (r, p), a in zip(items, dcs):
            dj_o[r, 2 * width + p * 128 : 2 * width + (p + 1) * 128] = mm(both(r, p), a).astype(BF)
        for (r, p), ds, a in zip(items, dscores, qs):
            dj_o[r, width + p * 128 : width + (p + 1) * 128] = mm(ds, a).astype(BF)
        for (r, p), ds in zip(items, dscores):
            tall = jnp.concatenate([ds[:, 0:SEQ], ds[:, SEQ:]], axis=0)
            dq = mm(tall, stack_heads(slab(k, r, p)), 0, 0) * 0.125
            dj_o[r, p * 128 : (p + 1) * 128] = dq.astype(BF)


def ln1_parts(acc, cs, w):
    def parts(v):
        hi = v.astype(BF)
        return hi, (v - hi.astype(F32)).astype(BF)

    narrow = sum(acc[:, j : j + 128] * w[:, j : j + 128].astype(F32) for j in range(0, w.shape[1], 128))
    ones = jnp.ones((16, 128), BF)
    gain = sum(mm(ones, v, 1, 1) for v in parts(narrow))[0:1]
    bias = mm(jnp.concatenate(parts(cs), axis=0), w, 1, 1)
    return gain, jnp.sum(bias, axis=0, keepdims=True)


def attn_bwd_body(place, joined, dc, probs, n1t, wqkv, gout, gub_own, gub_oth, vec, dj_o, keep_o, send_o, acc, cs, small):
    i = pl.program_id(0)
    d = n1t.shape[0]
    step = d // 16

    @pl.when(i == 0)
    def _():
        acc[...] = jnp.zeros_like(acc)
        cs[...] = jnp.zeros_like(cs)

    q, k, v = (joined.at[:, j * d : (j + 1) * d] for j in range(3))
    attn_bwd_block(q, k, v, dc, probs, dj_o)
    dj = dj_o[...]
    acc[...] += mm(n1t[...], dj)
    cs[...] += fold(dj.astype(F32))

    @pl.when(i == pl.num_programs(0) - 1)
    def _():
        gain, bias = ln1_parts(acc[...], cs[...], wqkv[...])
        csum = jnp.sum(cs[...], axis=0, keepdims=True)
        y, c = place[0], place[1]
        small[...] = jnp.zeros_like(small)

        def put(at, row):
            n = row.shape[1] // 128
            for j in range(n):
                small[pl.ds(at + j, 1)] = row[:, j * 128 : (j + 1) * 128]

        n = d // 128
        for j in range(4):
            put(j * n, vec[j : j + 1, :])
        for j in range(2):
            put(4 * n + (2 * y + j) * n, gub_own[j : j + 1, :])
        put(4 * n + (2 * (1 - y) + 1 - c) * n, gub_oth[0:1, :])
        put(4 * n + (2 * (1 - y) + c) * n, gub_oth[1:2, :])
        put(8 * n, csum)
        put(11 * n, gain)
        put(12 * n, bias)
        for o, core in ((keep_o, c), (send_o, 1 - c)):
            for b in range(8):
                where = pl.ds(pl.multiple_of((8 * core + b) * step, step), step)
                o[b, :, 0 : 3 * d] = acc[where, :].astype(BF)
                o[b, :, 3 * d : 4 * d] = gout[where, :]
                o[b, :, 4 * d :] = jnp.zeros((step, 128), BF)

        @pl.when(c == 0)
        def _():
            for b in range(2):
                keep_o[b, :, 4 * d :] = small[b * step : (b + 1) * step].astype(BF)

        @pl.when(c == 1)
        def _():
            for b in range(2):
                send_o[b, :, 4 * d :] = small[b * step : (b + 1) * step].astype(BF)


def attn_bwd(place, joined, dctx, probs, n1t, wqkv, gout, gub_own, gub_oth, vec, rows):
    d, t = n1t.shape
    outs = [pltpu.VMEM((t, 3 * d), BF)] + [shape((8, d // 16, 4 * d + 128), BF)] * 2
    rest = (wqkv, gout, gub_own, gub_oth, vec)
    return pl.pallas_call(
        attn_bwd_body,
        grid_spec=pltpu.PrefetchScalarGridSpec(
            num_scalar_prefetch=1,
            grid=(t // rows,),
            in_specs=[
                rows_spec(rows, 3 * d),
                rows_spec(rows, d),
                rows_spec(rows, 2 * d),
                pl.BlockSpec((d, rows), lambda i, *_: (0, i)),
            ]
            + [once(a) for a in rest],
            out_specs=[rows_spec(rows, 3 * d)] + [whole(o) for o in outs[1:]],
            scratch_shapes=[pltpu.VMEM((d, 3 * d), F32), pltpu.VMEM((8, 3 * d), F32), pltpu.VMEM((64, 128), F32)],
        ),
        out_shape=outs,
        compiler_params=pltpu.CompilerParams(vmem_limit_bytes=LIMIT + 8 * 1024 * 1024),
        cost_estimate=cost(8 * t * d * 3 * d),
        name="attn_bwd",
    )(place, joined, dctx, probs, n1t, *rest)


def in_grad_body(dj, tok, dattn, wqkv, vecs, *refs):
    dh1 = mm(dj[...], wqkv[...], 1, 1)
    n1, inv1 = layer_norm(tok[...].astype(F32))
    gain = vecs[...].astype(F32)[0:1]
    refs[-1][...] = (dattn[...].astype(F32) + norm_back(dh1, n1, inv1, gain)).astype(BF)


def in_part(body, rows, first, count, streams, fixed, before, macs, name):
    t, d = streams[1].shape
    spec = lambda w: pl.BlockSpec((rows, w), lambda i: (i + first, 0))
    args = (*streams, *fixed) + (() if before is None else (before,))
    return pl.pallas_call(
        body,
        grid=(count,),
        in_specs=[spec(a.shape[1]) for a in streams]
        + [once(a) for a in fixed]
        + ([] if before is None else [pl.BlockSpec(memory_space=pl.ANY)]),
        out_specs=spec(d),
        out_shape=in_hbm((t, d), BF),
        input_output_aliases={} if before is None else {len(args) - 1: 0},
        compiler_params=pltpu.CompilerParams(vmem_limit_bytes=LIMIT),
        cost_estimate=cost(2 * rows * count * macs),
        name=name,
    )(*args)


def layer_out_body(own, resid, oth, down, down_oth, vecs, *refs):
    out = mm(own[...], down[...]) + mm(oth[...], down_oth[...])
    refs[-1][...] = (resid[...] + out + vecs[...].astype(F32)[7:8]).astype(BF)


def on_chip(body, outs, at, *args, name):
    return pl.pallas_call(
        body,
        in_specs=[pl.BlockSpec(memory_space=pltpu.SMEM)] + [pl.BlockSpec(memory_space=pltpu.VMEM)] * len(args),
        out_specs=[pl.BlockSpec(memory_space=pltpu.VMEM)] * len(outs),
        out_shape=outs,
        compiler_params=pltpu.CompilerParams(vmem_limit_bytes=24 * 1024 * 1024),
        cost_estimate=cost(0, 4 * 1024 * 1024),
        name=name,
    )(at, *args)


def plus(a, b):
    return (a.astype(F32) + b.astype(F32)).astype(BF)


def split_body(at, own_a, own_b, oth_a, oth_b, keep_o, send_o):
    def total(o, j):
        a, b = (own_a, own_b) if o == 0 else (oth_a, oth_b)
        return plus(a[j], b[j])

    @pl.when(at[0] == 0)
    def _():
        v = at[1]
        for o in range(2):
            for p in range(2):
                keep_o[2 * o + p] = total(o, 2 * v + p)
                send_o[2 * o + p] = total(o, 2 * (1 - v) + p)

    @pl.when(at[0] == 1)
    def _():
        for j in range(4):
            keep_o[j] = total(0, j)
            send_o[j] = total(1, j)


def halve(at, which, a, b):
    n = a.shape[0] // 2

    def body(at, a, b, keep_o, send_o):
        v = at[which]
        for j in range(n):
            keep_o[j] = plus(a[v * n + j], b[v * n + j])
            send_o[j] = plus(a[(1 - v) * n + j], b[(1 - v) * n + j])

    return on_chip(body, [shape((n, *a.shape[1:]), BF)] * 2, at, a, b, name="halve")


def finish_ffn_body(at, *refs):
    up_o, down_o = refs[4:]
    quarter = refs[0].shape[1]
    for c in range(2):

        @pl.when(pl.program_id(0) == c)
        def _(c=c):
            for j in range(2):
                pair = refs[2 * c + j]
                which = at[3 + 2 * c] if j == 0 else 1 - at[3 + 2 * c]
                for i in range(2):
                    part = at[4 + 2 * c] if i == 0 else 1 - at[4 + 2 * c]
                    cols = pl.ds(pl.multiple_of(part * quarter, 128), quarter)

                    @pl.when(which == 0)
                    def _(pair=pair, i=i, cols=cols):
                        up_o[cols, :] = pair[i].astype(F32)

                    @pl.when(which == 1)
                    def _(pair=pair, i=i, cols=cols):
                        down_o[:, cols] = pair[i].astype(F32).T


def finish_ffn(at, *pairs):
    half = pairs[0].shape[2]
    d = 2 * pairs[0].shape[1]
    unit = lambda i, at: jnp.where(i == 0, at[0], 1 - at[0])
    return pl.pallas_call(
        finish_ffn_body,
        grid_spec=pltpu.PrefetchScalarGridSpec(
            num_scalar_prefetch=1,
            grid=(2,),
            in_specs=[whole(a) for a in pairs],
            out_specs=[
                pl.BlockSpec((d, half), lambda i, at: (0, unit(i, at))),
                pl.BlockSpec((half, d), lambda i, at: (unit(i, at), 0)),
            ],
        ),
        out_shape=[shape((d, 2 * half), F32), shape((2 * half, d), F32)],
        compiler_params=pltpu.CompilerParams(vmem_limit_bytes=24 * 1024 * 1024),
        cost_estimate=cost(0, 4 * 1024 * 1024),
        name="finish_ffn",
    )(at, *pairs)


def finish_rest_body(at, columns, *refs):
    qkv_o, qv_o, gout_o, gain1_o, bias1_o, bo_o, gain2_o, bias2_o, gub_o, b2_o, small = refs[4:]
    d = gout_o.shape[1]
    step, n = d // 16, d // 128
    pieces = []
    for c in range(2):
        core = at[0] if c == 0 else 1 - at[0]
        a0, b0, c0 = (at[7 + j] if c == 0 else at[11 + j] for j in range(3))
        for j in range(2):
            for i in range(4):
                bits = (a0 if j == 0 else 1 - a0, b0 if i < 2 else 1 - b0, c0 if i % 2 == 0 else 1 - c0)
                pieces.append((refs[2 * c + j], i, 8 * core + 4 * bits[0] + 2 * bits[1] + bits[2]))
    @pl.when(pl.program_id(0) == 0)
    def _():
        for ref, i, at_ in pieces:

            @pl.when(at_ < 2)
            def _(ref=ref, i=i, at_=at_):
                small[pl.ds(pl.multiple_of(at_ * step, step), step)] = ref[i, :, 4 * d :].astype(F32)

    def row(first, count):
        return jnp.concatenate([small[first + j : first + j + 1] for j in range(count)], axis=1)

    csum = row(8 * n, 3 * n)
    for c in range(2):

        @pl.when(pl.program_id(0) == c)
        def _(c=c):
            for ref, i, at_ in pieces[8 * c : 8 * c + 8]:
                rows = pl.ds(pl.multiple_of(at_ * step, step), step)
                here = pl.ds(pl.multiple_of((at_ % 8) * step, step), step)
                gain, bias = columns[rows, 0:1], columns[rows, 1:2]
                qkv_o[here, :] = ref[i, :, 0 : 3 * d].astype(F32) * gain + bias * csum
                gout_o[here, :] = ref[i, :, 3 * d : 4 * d].astype(F32)

    @pl.when(pl.program_id(0) == 0)
    def _():
        qv_o[0:1] = csum[:, 0:d]
        qv_o[1:2] = csum[:, 2 * d :]
        for o, j in ((bo_o, 0), (gain2_o, 1), (bias2_o, 2), (b2_o, 3)):
            o[...] = row(j * n, n)
        gain1_o[...] = row(11 * n, n)
        bias1_o[...] = row(12 * n, n)
        first = 4 * n + 2 * n * at[10]
        for j in range(2 * n):
            gub_o[:, j * 128 : (j + 1) * 128] = small[pl.ds(first + j, 1)]


def finish_rest(at, columns, *pieces):
    d = columns.shape[0]
    one = shape((1, d), F32)
    outs = [shape((d, 3 * d), F32), shape((2, d), F32), shape((d, d), F32)] + [one] * 5 + [shape((1, 2 * d), F32), one]
    args = (columns, *pieces)
    half = lambda i, at: (jnp.where(i == 0, at[0], 1 - at[0]), 0)
    return pl.pallas_call(
        finish_rest_body,
        grid_spec=pltpu.PrefetchScalarGridSpec(
            num_scalar_prefetch=1,
            grid=(2,),
            in_specs=[whole(a) for a in args],
            out_specs=[pl.BlockSpec((d // 2, 3 * d), half), whole(outs[1]), pl.BlockSpec((d // 2, d), half)]
            + [whole(o) for o in outs[3:]],
            scratch_shapes=[pltpu.VMEM((64, 128), F32)],
        ),
        out_shape=outs,
        compiler_params=pltpu.CompilerParams(vmem_limit_bytes=24 * 1024 * 1024),
        cost_estimate=cost(0, 8 * 1024 * 1024),
        name="finish_rest",
    )(at, *args)


def local(
    n_rows,
    tokens,
    segment_ids,
    ln1_gain,
    ln1_bias,
    qkv_weight,
    qv_bias,
    out_weight,
    out_bias,
    ln2_gain,
    ln2_bias,
    up_weight,
    up_bias,
    down_weight,
    down_bias,
    out_grad,
):
    t, d = tokens.shape
    half = up_weight.shape[1] // 2
    r, y = lax.axis_index("rows"), lax.axis_index("mlp")
    core = r & 1
    up_dims = n_rows.bit_length() - 2

    def flip(dim, row, m):
        if dim == "core":
            return row ^ 1, m
        if dim == "y":
            return row, m ^ 1
        return row ^ (2 << dim), m

    def bit(dim):
        return y if dim == "y" else (r >> (dim + 1)) & 1

    def swap(value, *dims):
        pairs = []
        for row in range(n_rows):
            for m in range(2):
                row2, m2 = flip(dims[0] if row & 1 == 0 else dims[-1], row, m)
                pairs.append((row * 2 + m, row2 * 2 + m2))
        return lax.ppermute(value, BOTH, pairs)

    def by_core(first, second):
        return jnp.where(core == 0, first, second)

    def after(value, *done):
        return lax.optimization_barrier((value, *done))[0]

    u0 = [0, "y"] + list(range(1, up_dims))
    u1 = ["y", 1, 0] + list(range(2, up_dims))
    q0 = ["y", 1, 0, 2] + list(range(3, up_dims))
    q1 = [0, "y", 1, 2] + list(range(3, up_dims))
    at = jnp.stack(
        [core, bit(0), by_core(0, bit(u1[1]))]
        + [by_core(bit(u0[0]), bit(u1[1])), by_core(bit(u0[2]), bit(u1[2]))]
        + [by_core(bit(u1[1]), bit(u0[0])), by_core(bit(u1[2]), bit(u0[2]))]
        + [by_core(bit(a), bit(b)) for a, b in zip(q0[:3], q1[:3])]
        + [y]
        + [by_core(bit(b), bit(a)) for a, b in zip(q0[:3], q1[:3])]
    ).astype(jnp.int32)
    place = jnp.stack([y, core]).astype(jnp.int32)
    core_s = core.reshape(1).astype(jnp.int32)
    hbm = lambda v: pltpu.with_memory_space_constraint(v, pltpu.HBM)
    vmem = lambda v: pltpu.with_memory_space_constraint(v, pltpu.VMEM)
    qkv_free, down_free = qkv_weight, down_weight
    tokens, out_grad, qkv_weight, out_weight, up_weight, down_weight = map(
        hbm, (tokens, out_grad, qkv_weight, out_weight, up_weight, down_weight)
    )

    bias = up_bias.reshape(2, half)
    vecs = jnp.concatenate(
        [
            jnp.stack([ln1_gain, ln1_bias, out_bias, ln2_gain, ln2_bias, qv_bias[0], qv_bias[1], down_bias]),
            bias,
            jnp.zeros((6, d), BF),
        ]
    )
    columns = jnp.stack([ln1_gain, ln1_bias], axis=1).astype(F32)

    w_send = swap(fetch(1 - core_s, up_weight, down_weight, bias), "y")
    joined, ctx, resid, h2, n1t, probs = attn_fwd(tokens, segment_ids, vecs, qkv_weight, out_weight, rows=512)
    gated_own, dh2_own, own_keep, own_send, gub_own = ffn_own(
        core_s, vmem(h2), out_grad, up_weight, vecs, down_weight, rows=512
    )
    w_send = after(w_send, own_send)
    w_keep = swap(w_send, "core")
    own_recv = swap(own_send, "core")
    gated_oth, dattn, dctx, oth_keep, oth_send, gub_oth, gout, vec = ffn_other(
        vmem(h2), out_grad, hbm(w_send), w_keep, vmem(dh2_own), hbm(resid), hbm(ctx), out_weight, vecs, rows=512
    )
    oth_recv = swap(oth_send, "core")
    down_oth = jnp.concatenate([w[d : d + half] for w in lax.optimization_barrier((w_send, w_keep, oth_send))[:2]])
    blocks = t // 512

    def layer_out_part(first, count, before, *ready):
        return in_part(
            layer_out_body, 512, first, count, (hbm(gated_own), hbm(after(resid, *ready)), hbm(gated_oth)),
            (down_weight, hbm(down_oth), vecs), before, 4 * half * d, "layer_out",
        )

    def in_grad_part(first, count, before, *ready):
        return in_part(
            in_grad_body, 512, first, count, (dj, tokens, hbm(after(dattn, *ready))), (qkv_free, vecs), before,
            3 * d * d, "in_grad",
        )

    block = shape((4, d // 2, half), BF)
    u_keep, u_send = on_chip(split_body, [block] * 2, at, own_keep, own_recv, oth_keep, oth_recv, name="split")
    u_recv = swap(u_send, u0[0], u1[0])
    dj, q_keep, q_send = attn_bwd(
        place, hbm(joined), hbm(after(dctx, u_keep)), hbm(probs), hbm(n1t), qkv_weight, hbm(gout), gub_own, gub_oth, vec,
        rows=512,
    )
    q_recv = swap(q_send, "core")
    u_keep, u_send = halve(at, 2, u_keep, after(u_recv, q_send))
    u_recv = swap(u_send, u0[1], u1[1])
    in_grad = in_grad_part(0, blocks // 2, None, u_keep)
    q_keep, q_send = halve(at, 7, q_keep, after(q_recv, in_grad))
    q_recv = swap(q_send, q0[0], q1[0])
    in_grad = in_grad_part(blocks // 2, blocks // 2, in_grad, q_keep)
    u_keep, u_send = halve(at, 4, u_keep, after(u_recv, in_grad))
    u_recv = swap(u_send, u0[2], u1[2])
    q_keep, q_send = halve(at, 8, q_keep, after(q_recv, u_keep))
    q_recv = swap(q_send, q0[1], q1[1])
    u_one = plus(u_keep, after(u_recv, q_keep))
    u_recv = swap(u_one, u0[3], u1[3])
    q_keep, q_send = halve(at, 9, q_keep, after(q_recv, u_one))
    q_recv = swap(q_send, q0[2], q1[2])
    layer_out = layer_out_part(0, blocks // 2, None, q_keep)
    q_one = plus(q_keep, after(q_recv, layer_out))
    for k in range(3, len(u0)):
        q_recv = swap(q_one, q0[k], q1[k])
        u_one = plus(u_one, after(u_recv, q_one))
        if k + 1 < len(u0):
            u_recv = swap(u_one, u0[k + 1], u1[k + 1])
            q_one = plus(q_one, after(q_recv, u_one))
    u_ag = swap(u_one, u0[2], u1[2])
    q_one = plus(q_one, after(q_recv, u_one))
    q_ag = swap(q_one, q0[2], q1[2])
    u_pair = jnp.concatenate([u_one, after(u_ag, q_one)], axis=0)
    u_far = swap(u_pair, u0[0], u1[1])
    u_pair_c = swap(u_pair, "core")
    q_pair = jnp.concatenate([q_one, after(q_ag, u_pair)], axis=0)
    q_ag = swap(q_pair, q0[1], q1[1])
    q_four = jnp.concatenate([q_pair, after(q_ag, u_pair)], axis=0)
    q_far = swap(q_four, q0[0], q1[0])
    q_four_c = swap(q_four, "core")
    layer_out = layer_out_part(blocks // 2, blocks // 2, layer_out, q_four)
    u_far = after(u_far, layer_out)
    u_far_c = swap(u_far, "core")
    grad_up, grad_down = finish_ffn(at, u_pair, u_far, u_pair_c, u_far_c)
    q_far = after(q_far, grad_up)
    grad_qkv, grad_qv, grad_wo, g1, c1, bo, g2, c2, gub, b2 = finish_rest(
        at, columns, q_four, q_far, q_four_c, swap(q_far, "core")
    )
    flat = lambda v: v.reshape(-1)
    return (
        layer_out, in_grad, flat(g1), flat(c1), grad_qkv, grad_qv, grad_wo, flat(bo), flat(g2), flat(c2),
        grad_up, flat(gub), grad_down, flat(b2),
    )


def solution(mesh):
    placed = (
        P(BOTH, None), P(BOTH, None), P(), P(), P(), P(), P(), P(), P(), P(),
        P(None, "mlp"), P("mlp"), P("mlp", None), P(), P(BOTH, None),
    )
    return jax.shard_map(
        functools.partial(local, mesh.shape["rows"]),
        mesh=mesh,
        in_specs=placed,
        out_specs=(
            P(BOTH, None), P(BOTH, None), P(), P(), P(), P(), P(), P(), P(), P(),
            P(None, "mlp"), P("mlp"), P("mlp", None), P(),
        ),
        check_vma=False,
    )
```

```python
import functools
import math

import jax
import jax.numpy as jnp
from jax import lax
from jax.experimental import pallas as pl
from jax.experimental.pallas import tpu as pltpu
from jax.sharding import PartitionSpec as P

BF, F32 = jnp.bfloat16, jnp.float32
SEQ, HD, FRAME = 128, 64, 4
EPS = 1e-5
C0 = math.sqrt(2.0 / math.pi)
C1 = C0 * 0.044715
LIMIT = 20 * 1024 * 1024
BOTH = ("rows", "mlp")
OWN_LIMIT = 24 * 1024 * 1024
OTHER_LIMIT = 32 * 1024 * 1024


def mm(a, b, ca=1, cb=0):
    return lax.dot_general(a, b, (((ca,), (cb,)), ((), ())), preferred_element_type=F32)


def layer_norm(x):
    c = x - jnp.mean(x, axis=-1, keepdims=True)
    inv = lax.rsqrt(jnp.mean(c * c, axis=-1, keepdims=True) + EPS)
    return c * inv, inv


def norm_back(grad, normed, inv, gain):
    s = grad * gain
    return inv * (
        s
        - jnp.mean(s, axis=-1, keepdims=True)
        - normed * jnp.mean(s * normed, axis=-1, keepdims=True)
    )


def fold(v):
    return jnp.sum(v.reshape(-1, 8, v.shape[-1]), axis=0)


def stack_heads(v):
    low = lax.broadcasted_iota(jnp.int32, v.shape, 1) < HD
    zero = jnp.zeros_like(v)
    return jnp.concatenate([jnp.where(low, v, zero), jnp.where(low, zero, v)], axis=0)


def allowed_of(seg_row, transposed):
    wide = jnp.broadcast_to(seg_row.astype(F32), (SEQ, SEQ))
    same = wide == wide.T
    a = lax.broadcasted_iota(jnp.int32, (SEQ, SEQ), 1 if transposed else 0)
    b = lax.broadcasted_iota(jnp.int32, (SEQ, SEQ), 0 if transposed else 1)
    return same & (a // FRAME >= b // FRAME)


def whole(a):
    zeros = (0,) * len(a.shape)
    return pl.BlockSpec(a.shape, lambda i, *_: zeros)


def once(a):
    zeros = (0,) * len(a.shape)
    return pl.BlockSpec(a.shape, lambda i, *_: zeros, pipeline_mode=pl.Buffered(buffer_count=1))


def rows_spec(r, w):
    return pl.BlockSpec((r, w), lambda i, *_: (i, 0))


def shape(s, dtype):
    return jax.ShapeDtypeStruct(s, dtype)


def in_hbm(s, dtype):
    return pltpu.HBM(s, dtype)


def cost(macs, nbytes=0):
    return pl.CostEstimate(flops=8 * macs, bytes_accessed=1, transcendentals=0)


def slab(ref, r, c):
    return ref[r, c * 128 : (c + 1) * 128]


def attn_fwd_body(tok, seg, vecs, wqkv, wo, joined_o, ctx_o, resid_o, h2_o, n1t_o, probs_o):
    rows, width = tok.shape
    pairs = width // 128
    vec = vecs[...].astype(F32)
    g1, b1, bo, g2, b2, bq, bv = (vec[j : j + 1] for j in range(7))
    x = tok[...].astype(F32)
    n1, _ = layer_norm(x)
    n1t_o[...] = n1.astype(BF).T
    h1 = (n1 * g1 + b1).astype(BF)
    bias = jnp.concatenate([bq, jnp.zeros_like(bq), bv], axis=1)
    joined = (mm(h1, wqkv[...]) + bias).astype(BF)
    joined_o[...] = joined
    group = 4
    done = []
    for s0 in range(0, rows // SEQ, group):
        items = [(s, p) for s in range(s0, s0 + group) for p in range(pairs)]
        allow = {s: allowed_of(seg[0, s : s + 1, :], True) for s in range(s0, s0 + group)}

        def part(s, o, p):
            return joined[s * SEQ : (s + 1) * SEQ, o * width + p * 128 : o * width + (p + 1) * 128]

        scores = [mm(part(s, 1, p), stack_heads(part(s, 0, p) * BF(0.125)), 1, 1) for s, p in items]
        probs = []
        for (s, p), sc in zip(items, scores):
            two = []
            for h in range(2):
                v = jnp.where(allow[s], sc[:, h * SEQ : (h + 1) * SEQ], -1e9)
                e = jnp.exp(v - jnp.max(v, axis=0, keepdims=True))
                two.append((e * (1.0 / jnp.sum(e, axis=0, keepdims=True))).astype(BF))
            probs.append(jnp.concatenate(two, axis=0))
            for h in range(2):
                at = (2 * p + h) * SEQ
                probs_o[s * SEQ : (s + 1) * SEQ, at : at + SEQ] = two[h]
        outs = [mm(pr, stack_heads(part(s, 2, p)), 0, 0).astype(BF) for (s, p), pr in zip(items, probs)]
        for j in range(group):
            done.append(jnp.concatenate(outs[j * pairs : (j + 1) * pairs], axis=1))
    ctx = jnp.concatenate(done, axis=0)
    ctx_o[...] = ctx
    resid = x + mm(ctx, wo[...]) + bo
    resid_o[...] = resid
    n2, _ = layer_norm(resid)
    h2_o[...] = (n2 * g2 + b2).astype(BF)


def attn_fwd(tok, seg, vecs, wqkv, wo, rows):
    t, d = tok.shape
    return pl.pallas_call(
        attn_fwd_body,
        grid=(t // rows,),
        in_specs=[rows_spec(rows, d), pl.BlockSpec((1, rows // SEQ, SEQ), lambda i: (i, 0, 0))]
        + [once(a) for a in (vecs, wqkv, wo)],
        out_specs=[rows_spec(rows, w) for w in (3 * d, d, d, d)] + [pl.BlockSpec((d, rows), lambda i: (0, i)), rows_spec(rows, 2 * d)],
        out_shape=[in_hbm((t, 3 * d), BF), in_hbm((t, d), BF), in_hbm((t, d), F32), pltpu.VMEM((t, d), BF), in_hbm((d, t), BF), in_hbm((t, 2 * d), BF)],
        compiler_params=pltpu.CompilerParams(vmem_limit_bytes=LIMIT),
        cost_estimate=cost(3 * t * d * 4 * d),
        name="attn_fwd",
    )(tok, seg.reshape(t // rows, rows // SEQ, SEQ), vecs, wqkv, wo)


def fetch_body(first, up, down, bias, out_o):
    d, half = up.shape
    out_o[0:d] = up[...]
    out_o[d : d + half] = down[...]
    bias = bias[...].astype(F32)
    bias = jnp.where(first[0] == 0, bias[0:1], bias[1:2])
    out_o[d + half :] = jnp.broadcast_to(bias, (16, half)).astype(BF)


def fetch(first, up, down, bias):
    d, f = up.shape
    half = f // 2
    return pl.pallas_call(
        fetch_body,
        grid_spec=pltpu.PrefetchScalarGridSpec(
            num_scalar_prefetch=1,
            grid=(1,),
            in_specs=[
                pl.BlockSpec((d, half), lambda i, at: (0, at[0])),
                pl.BlockSpec((half, d), lambda i, at: (at[0], 0)),
                whole(bias),
            ],
            out_specs=pl.BlockSpec((d + half + 16, half), lambda i, at: (0, 0)),
        ),
        out_shape=shape((d + half + 16, half), BF),
        compiler_params=pltpu.CompilerParams(vmem_limit_bytes=LIMIT),
        cost_estimate=cost(0, 1024 * 1024),
        name="fetch",
    )(first, up, down, bias)


def gate(v, dg, bias):
    v = v + bias
    v2 = v * v
    a = 0.5 + 0.5 * jnp.tanh(v * (C0 + C1 * v2))
    act = v * a
    slope = a + act * (1.0 - a) * (2.0 * C0 + 6.0 * C1 * v2)
    return act.astype(BF), (dg * slope).astype(BF)


def ffn_block(h2, g, up, ub, down, gated_o, dhid, gup, gdn, gub):
    f = up.shape[1]
    side, tile = 256, 64
    units = [(r, c) for r in range(0, h2.shape[0], side) for c in range(0, f, side)]

    def products(r, c):
        return mm(h2[r : r + side, :], up[:, c : c + side]), mm(g[r : r + side, :], down[c : c + side, :], 1, 1)

    ahead = products(*units[0])
    for k, (r, c) in enumerate(units):
        v, dg = ahead
        if k + 1 < len(units):
            ahead = products(*units[k + 1])
        for t in range(0, side, tile):
            act, dh = gate(v[t : t + tile], dg[t : t + tile], ub[:, c : c + side])
            gated_o[r + t : r + t + tile, c : c + side] = act
            dhid[r + t : r + t + tile, c : c + side] = dh
    dh = dhid[...]
    gup[...] += mm(h2[...].T, dh)
    gdn[...] += mm(g[...].T, gated_o[...])
    gub[...] += fold(dh.astype(F32))
    return mm(dh, up[...], 1, 1)


def put_grads(o, gup, gdn, cols):
    n = gup.shape[0] // 2
    for j in range(2):
        o[j] = gup[j * n : (j + 1) * n, cols].astype(BF)
        o[2 + j] = gdn[j * n : (j + 1) * n, cols].astype(BF)


def put_bias(o, gub):
    half = o.shape[1]
    total = jnp.sum(gub[...], axis=0, keepdims=True)
    for j in range(2):
        o[j : j + 1] = total[:, j * half : (j + 1) * half]


def ffn_own_body(core, h2, g, up, vecs, down, gated_o, dh2_o, keep_o, send_o, gub_o, gup, gdn, gub, dhid):
    i = pl.program_id(0)
    half = up.shape[1] // 2

    @pl.when(i == 0)
    def _():
        for a in (gup, gdn, gub):
            a[...] = jnp.zeros_like(a)

    bias = vecs[...].astype(F32)
    bias = jnp.concatenate([bias[8:9], bias[9:10]], axis=1)
    dh2_o[...] = ffn_block(h2, g, up, bias, down, gated_o, dhid, gup, gdn, gub)

    @pl.when(i == pl.num_programs(0) - 1)
    def _():
        put_grads(keep_o, gup, gdn, pl.ds(pl.multiple_of(core[0] * half, 128), half))
        put_grads(send_o, gup, gdn, pl.ds(pl.multiple_of((1 - core[0]) * half, 128), half))
        put_bias(gub_o, gub)


def ffn_scratch(rows, d, f):
    return [pltpu.VMEM((d, f), F32), pltpu.VMEM((d, f), F32), pltpu.VMEM((8, f), F32), pltpu.VMEM((rows, f), BF)]


def ffn_own(core, h2, g, up, vecs, down, rows):
    t, d = h2.shape
    f = up.shape[1]
    half = f // 2
    outs = [in_hbm((t, f), BF), pltpu.VMEM((t, d), F32)] + [shape((4, d // 2, half), BF)] * 2 + [shape((2, half), F32)]
    return pl.pallas_call(
        ffn_own_body,
        grid_spec=pltpu.PrefetchScalarGridSpec(
            num_scalar_prefetch=1,
            grid=(t // rows,),
            in_specs=[rows_spec(rows, d), rows_spec(rows, d), once(up), whole(vecs), once(down)],
            out_specs=[rows_spec(rows, f), rows_spec(rows, d)] + [whole(o) for o in outs[2:]],
            scratch_shapes=ffn_scratch(rows, d, f),
        ),
        out_shape=outs,
        compiler_params=pltpu.CompilerParams(vmem_limit_bytes=OWN_LIMIT),
        cost_estimate=cost(2 * 5 * t * d * f),
        name="ffn_own",
    )(core, h2, g, up, vecs, down)


def ffn_other_body(
    h2, g, w_send, w_keep, dh2_p, resid, ctx, wo, vecs,
    gated_o, dattn_o, dctx_o, keep_o, send_o, gub_o, gout_o, vec_o,
    gup, gdn, gub, dhid, up, down, ub, gout, vec,
):
    i = pl.program_id(0)
    d = h2.shape[1]
    half = w_send.shape[1]

    @pl.when(i == 0)
    def _():
        for a in (gup, gdn, gub, gout, vec):
            a[...] = jnp.zeros_like(a)
        for c, w in enumerate((w_send, w_keep)):
            up[:, c * half : (c + 1) * half] = w[0:d, :]
            down[c * half : (c + 1) * half, :] = w[d : d + half, :]
            ub[:, c * half : (c + 1) * half] = w[d + half : d + half + 16, :].astype(F32)[0:8]

    dh = dh2_p[...] + ffn_block(h2, g, up, ub[0:1], down, gated_o, dhid, gup, gdn, gub)
    n2, inv2 = layer_norm(resid[...])
    gf = g[...].astype(F32)
    dattn = (gf + norm_back(dh, n2, inv2, vecs[...].astype(F32)[3:4])).astype(BF)
    dattn_o[...] = dattn
    dctx_o[...] = mm(dattn, wo[...], 1, 1).astype(BF)
    gout[...] += mm(ctx[...].T, dattn)
    for j, v in enumerate((dattn.astype(F32), dh * n2, dh, gf)):
        vec[j] += fold(v)

    @pl.when(i == pl.num_programs(0) - 1)
    def _():
        put_grads(send_o, gup, gdn, slice(0, half))
        put_grads(keep_o, gup, gdn, slice(half, 2 * half))
        gout_o[...] = gout[...].astype(BF)
        put_bias(gub_o, gub)
        for j in range(4):
            vec_o[j : j + 1] = jnp.sum(vec[j], axis=0, keepdims=True)


def ffn_other(h2, g, w_send, w_keep, dh2_p, resid, ctx, wo, vecs, rows):
    t, d = h2.shape
    half = w_send.shape[1]
    f = 2 * half
    outs = [in_hbm((t, f), BF), in_hbm((t, d), BF), in_hbm((t, d), BF)]
    outs += [shape((4, d // 2, half), BF)] * 2 + [shape((2, half), F32), in_hbm((d, d), BF), shape((4, d), F32)]
    return pl.pallas_call(
        ffn_other_body,
        grid_spec=pltpu.PrefetchScalarGridSpec(
            num_scalar_prefetch=0,
            grid=(t // rows,),
            in_specs=[rows_spec(rows, d), rows_spec(rows, d), once(w_send), once(w_keep)]
            + [rows_spec(rows, d)] * 3
            + [once(wo), whole(vecs)],
            out_specs=[rows_spec(rows, f), rows_spec(rows, d), rows_spec(rows, d)] + [whole(o) for o in outs[3:]],
            scratch_shapes=ffn_scratch(rows, d, f)
            + [pltpu.VMEM((d, f), BF), pltpu.VMEM((f, d), BF), pltpu.VMEM((8, f), F32)]
            + [pltpu.VMEM((d, d), F32), pltpu.VMEM((4, 8, d), F32)],
        ),
        out_shape=outs,
        compiler_params=pltpu.CompilerParams(vmem_limit_bytes=OTHER_LIMIT),
        cost_estimate=cost(2 * (5 * t * d * f + 2 * t * d * d)),
        name="ffn_other",
    )(h2, g, w_send, w_keep, dh2_p, resid, ctx, wo, vecs)


def attn_bwd_block(q, k, v, dc, probs, dj_o):
    rows, width = q.shape
    pairs = width // 128
    group = 2
    for s0 in range(0, rows // SEQ, group):
        items = [(slice(s * SEQ, (s + 1) * SEQ), p) for s in range(s0, s0 + group) for p in range(pairs)]
        both = lambda r, p: probs[r, 2 * p * SEQ : 2 * (p + 1) * SEQ]
        qs = [stack_heads(slab(q, r, p) * BF(0.125)) for r, p in items]
        dcs = [stack_heads(slab(dc, r, p)) for r, p in items]
        dprobs = [mm(slab(v, r, p), a, 1, 1) for (r, p), a in zip(items, dcs)]
        dscores = []
        for (r, p), dp in zip(items, dprobs):
            pr = both(r, p).astype(F32)
            dscores.append((pr * (dp - jnp.sum(pr * dp, axis=0, keepdims=True))).astype(BF))
        for (r, p), a in zip(items, dcs):
            dj_o[r, 2 * width + p * 128 : 2 * width + (p + 1) * 128] = mm(both(r, p), a).astype(BF)
        for (r, p), ds, a in zip(items, dscores, qs):
            dj_o[r, width + p * 128 : width + (p + 1) * 128] = mm(ds, a).astype(BF)
        for (r, p), ds in zip(items, dscores):
            tall = jnp.concatenate([ds[:, 0:SEQ], ds[:, SEQ:]], axis=0)
            dq = mm(tall, stack_heads(slab(k, r, p)), 0, 0) * 0.125
            dj_o[r, p * 128 : (p + 1) * 128] = dq.astype(BF)


def ln1_parts(acc, cs, w):
    def parts(v):
        hi = v.astype(BF)
        return hi, (v - hi.astype(F32)).astype(BF)

    narrow = sum(acc[:, j : j + 128] * w[:, j : j + 128].astype(F32) for j in range(0, w.shape[1], 128))
    ones = jnp.ones((16, 128), BF)
    gain = sum(mm(ones, v, 1, 1) for v in parts(narrow))[0:1]
    bias = mm(jnp.concatenate(parts(cs), axis=0), w, 1, 1)
    return gain, jnp.sum(bias, axis=0, keepdims=True)


def attn_bwd_body(place, joined, dc, probs, n1t, wqkv, gout, gub_own, gub_oth, vec, dj_o, keep_o, send_o, acc, cs, small):
    i = pl.program_id(0)
    d = n1t.shape[0]
    step = d // 16

    @pl.when(i == 0)
    def _():
        acc[...] = jnp.zeros_like(acc)
        cs[...] = jnp.zeros_like(cs)

    q, k, v = (joined.at[:, j * d : (j + 1) * d] for j in range(3))
    attn_bwd_block(q, k, v, dc, probs, dj_o)
    dj = dj_o[...]
    acc[...] += mm(n1t[...], dj)
    cs[...] += fold(dj.astype(F32))

    @pl.when(i == pl.num_programs(0) - 1)
    def _():
        gain, bias = ln1_parts(acc[...], cs[...], wqkv[...])
        csum = jnp.sum(cs[...], axis=0, keepdims=True)
        y, c = place[0], place[1]
        small[...] = jnp.zeros_like(small)

        def put(at, row):
            n = row.shape[1] // 128
            for j in range(n):
                small[pl.ds(at + j, 1)] = row[:, j * 128 : (j + 1) * 128]

        n = d // 128
        for j in range(4):
            put(j * n, vec[j : j + 1, :])
        for j in range(2):
            put(4 * n + (2 * y + j) * n, gub_own[j : j + 1, :])
        put(4 * n + (2 * (1 - y) + 1 - c) * n, gub_oth[0:1, :])
        put(4 * n + (2 * (1 - y) + c) * n, gub_oth[1:2, :])
        put(8 * n, csum)
        put(11 * n, gain)
        put(12 * n, bias)
        for o, core in ((keep_o, c), (send_o, 1 - c)):
            for b in range(8):
                where = pl.ds(pl.multiple_of((8 * core + b) * step, step), step)
                o[b, :, 0 : 3 * d] = acc[where, :].astype(BF)
                o[b, :, 3 * d : 4 * d] = gout[where, :]
                o[b, :, 4 * d :] = jnp.zeros((step, 128), BF)

        @pl.when(c == 0)
        def _():
            for b in range(2):
                keep_o[b, :, 4 * d :] = small[b * step : (b + 1) * step].astype(BF)

        @pl.when(c == 1)
        def _():
            for b in range(2):
                send_o[b, :, 4 * d :] = small[b * step : (b + 1) * step].astype(BF)


def attn_bwd(place, joined, dctx, probs, n1t, wqkv, gout, gub_own, gub_oth, vec, rows):
    d, t = n1t.shape
    outs = [pltpu.VMEM((t, 3 * d), BF)] + [shape((8, d // 16, 4 * d + 128), BF)] * 2
    rest = (wqkv, gout, gub_own, gub_oth, vec)
    return pl.pallas_call(
        attn_bwd_body,
        grid_spec=pltpu.PrefetchScalarGridSpec(
            num_scalar_prefetch=1,
            grid=(t // rows,),
            in_specs=[
                rows_spec(rows, 3 * d),
                rows_spec(rows, d),
                rows_spec(rows, 2 * d),
                pl.BlockSpec((d, rows), lambda i, *_: (0, i)),
            ]
            + [once(a) for a in rest],
            out_specs=[rows_spec(rows, 3 * d)] + [whole(o) for o in outs[1:]],
            scratch_shapes=[pltpu.VMEM((d, 3 * d), F32), pltpu.VMEM((8, 3 * d), F32), pltpu.VMEM((64, 128), F32)],
        ),
        out_shape=outs,
        compiler_params=pltpu.CompilerParams(vmem_limit_bytes=LIMIT + 8 * 1024 * 1024),
        cost_estimate=cost(8 * t * d * 3 * d),
        name="attn_bwd",
    )(place, joined, dctx, probs, n1t, *rest)


def in_grad_body(dj, tok, dattn, wqkv, vecs, *refs):
    dh1 = mm(dj[...], wqkv[...], 1, 1)
    n1, inv1 = layer_norm(tok[...].astype(F32))
    gain = vecs[...].astype(F32)[0:1]
    refs[-1][...] = (dattn[...].astype(F32) + norm_back(dh1, n1, inv1, gain)).astype(BF)


def in_part(body, rows, first, count, streams, fixed, before, macs, name):
    t, d = streams[1].shape
    spec = lambda w: pl.BlockSpec((rows, w), lambda i: (i + first, 0))
    args = (*streams, *fixed) + (() if before is None else (before,))
    return pl.pallas_call(
        body,
        grid=(count,),
        in_specs=[spec(a.shape[1]) for a in streams]
        + [once(a) for a in fixed]
        + ([] if before is None else [pl.BlockSpec(memory_space=pl.ANY)]),
        out_specs=spec(d),
        out_shape=in_hbm((t, d), BF),
        input_output_aliases={} if before is None else {len(args) - 1: 0},
        compiler_params=pltpu.CompilerParams(vmem_limit_bytes=LIMIT),
        cost_estimate=cost(2 * rows * count * macs),
        name=name,
    )(*args)


def layer_out_body(own, resid, oth, down, down_oth, vecs, *refs):
    out = mm(own[...], down[...]) + mm(oth[...], down_oth[...])
    refs[-1][...] = (resid[...] + out + vecs[...].astype(F32)[7:8]).astype(BF)


def on_chip(body, outs, at, *args, name):
    return pl.pallas_call(
        body,
        in_specs=[pl.BlockSpec(memory_space=pltpu.SMEM)] + [pl.BlockSpec(memory_space=pltpu.VMEM)] * len(args),
        out_specs=[pl.BlockSpec(memory_space=pltpu.VMEM)] * len(outs),
        out_shape=outs,
        compiler_params=pltpu.CompilerParams(vmem_limit_bytes=24 * 1024 * 1024),
        cost_estimate=cost(0, 4 * 1024 * 1024),
        name=name,
    )(at, *args)


def plus(a, b):
    return (a.astype(F32) + b.astype(F32)).astype(BF)


def split_body(at, own_a, own_b, oth_a, oth_b, keep_o, send_o):
    def total(o, j):
        a, b = (own_a, own_b) if o == 0 else (oth_a, oth_b)
        return plus(a[j], b[j])

    @pl.when(at[0] == 0)
    def _():
        v = at[1]
        for o in range(2):
            for p in range(2):
                keep_o[2 * o + p] = total(o, 2 * v + p)
                send_o[2 * o + p] = total(o, 2 * (1 - v) + p)

    @pl.when(at[0] == 1)
    def _():
        for j in range(4):
            keep_o[j] = total(0, j)
            send_o[j] = total(1, j)


def halve(at, which, a, b):
    n = a.shape[0] // 2

    def body(at, a, b, keep_o, send_o):
        v = at[which]
        for j in range(n):
            keep_o[j] = plus(a[v * n + j], b[v * n + j])
            send_o[j] = plus(a[(1 - v) * n + j], b[(1 - v) * n + j])

    return on_chip(body, [shape((n, *a.shape[1:]), BF)] * 2, at, a, b, name="halve")


def finish_ffn_body(at, *refs):
    up_o, down_o = refs[4:]
    quarter = refs[0].shape[1]
    for c in range(2):

        @pl.when(pl.program_id(0) == c)
        def _(c=c):
            for j in range(2):
                pair = refs[2 * c + j]
                which = at[3 + 2 * c] if j == 0 else 1 - at[3 + 2 * c]
                for i in range(2):
                    part = at[4 + 2 * c] if i == 0 else 1 - at[4 + 2 * c]
                    cols = pl.ds(pl.multiple_of(part * quarter, 128), quarter)

                    @pl.when(which == 0)
                    def _(pair=pair, i=i, cols=cols):
                        up_o[cols, :] = pair[i].astype(F32)

                    @pl.when(which == 1)
                    def _(pair=pair, i=i, cols=cols):
                        down_o[:, cols] = pair[i].astype(F32).T


def finish_ffn(at, *pairs):
    half = pairs[0].shape[2]
    d = 2 * pairs[0].shape[1]
    unit = lambda i, at: jnp.where(i == 0, at[0], 1 - at[0])
    return pl.pallas_call(
        finish_ffn_body,
        grid_spec=pltpu.PrefetchScalarGridSpec(
            num_scalar_prefetch=1,
            grid=(2,),
            in_specs=[whole(a) for a in pairs],
            out_specs=[
                pl.BlockSpec((d, half), lambda i, at: (0, unit(i, at))),
                pl.BlockSpec((half, d), lambda i, at: (unit(i, at), 0)),
            ],
        ),
        out_shape=[shape((d, 2 * half), F32), shape((2 * half, d), F32)],
        compiler_params=pltpu.CompilerParams(vmem_limit_bytes=24 * 1024 * 1024),
        cost_estimate=cost(0, 4 * 1024 * 1024),
        name="finish_ffn",
    )(at, *pairs)


def finish_rest_body(at, columns, *refs):
    qkv_o, qv_o, gout_o, gain1_o, bias1_o, bo_o, gain2_o, bias2_o, gub_o, b2_o, small = refs[4:]
    d = gout_o.shape[1]
    step, n = d // 16, d // 128
    pieces = []
    for c in range(2):
        core = at[0] if c == 0 else 1 - at[0]
        a0, b0, c0 = (at[7 + j] if c == 0 else at[11 + j] for j in range(3))
        for j in range(2):
            for i in range(4):
                bits = (a0 if j == 0 else 1 - a0, b0 if i < 2 else 1 - b0, c0 if i % 2 == 0 else 1 - c0)
                pieces.append((refs[2 * c + j], i, 8 * core + 4 * bits[0] + 2 * bits[1] + bits[2]))
    @pl.when(pl.program_id(0) == 0)
    def _():
        for ref, i, at_ in pieces:

            @pl.when(at_ < 2)
            def _(ref=ref, i=i, at_=at_):
                small[pl.ds(pl.multiple_of(at_ * step, step), step)] = ref[i, :, 4 * d :].astype(F32)

    def row(first, count):
        return jnp.concatenate([small[first + j : first + j + 1] for j in range(count)], axis=1)

    csum = row(8 * n, 3 * n)
    for c in range(2):

        @pl.when(pl.program_id(0) == c)
        def _(c=c):
            for ref, i, at_ in pieces[8 * c : 8 * c + 8]:
                rows = pl.ds(pl.multiple_of(at_ * step, step), step)
                here = pl.ds(pl.multiple_of((at_ % 8) * step, step), step)
                gain, bias = columns[rows, 0:1], columns[rows, 1:2]
                qkv_o[here, :] = ref[i, :, 0 : 3 * d].astype(F32) * gain + bias * csum
                gout_o[here, :] = ref[i, :, 3 * d : 4 * d].astype(F32)

    @pl.when(pl.program_id(0) == 0)
    def _():
        qv_o[0:1] = csum[:, 0:d]
        qv_o[1:2] = csum[:, 2 * d :]
        for o, j in ((bo_o, 0), (gain2_o, 1), (bias2_o, 2), (b2_o, 3)):
            o[...] = row(j * n, n)
        gain1_o[...] = row(11 * n, n)
        bias1_o[...] = row(12 * n, n)
        first = 4 * n + 2 * n * at[10]
        for j in range(2 * n):
            gub_o[:, j * 128 : (j + 1) * 128] = small[pl.ds(first + j, 1)]


def finish_rest(at, columns, *pieces):
    d = columns.shape[0]
    one = shape((1, d), F32)
    outs = [shape((d, 3 * d), F32), shape((2, d), F32), shape((d, d), F32)] + [one] * 5 + [shape((1, 2 * d), F32), one]
    args = (columns, *pieces)
    half = lambda i, at: (jnp.where(i == 0, at[0], 1 - at[0]), 0)
    return pl.pallas_call(
        finish_rest_body,
        grid_spec=pltpu.PrefetchScalarGridSpec(
            num_scalar_prefetch=1,
            grid=(2,),
            in_specs=[whole(a) for a in args],
            out_specs=[pl.BlockSpec((d // 2, 3 * d), half), whole(outs[1]), pl.BlockSpec((d // 2, d), half)]
            + [whole(o) for o in outs[3:]],
            scratch_shapes=[pltpu.VMEM((64, 128), F32)],
        ),
        out_shape=outs,
        compiler_params=pltpu.CompilerParams(vmem_limit_bytes=24 * 1024 * 1024),
        cost_estimate=cost(0, 8 * 1024 * 1024),
        name="finish_rest",
    )(at, *args)


def local(
    n_rows,
    tokens,
    segment_ids,
    ln1_gain,
    ln1_bias,
    qkv_weight,
    qv_bias,
    out_weight,
    out_bias,
    ln2_gain,
    ln2_bias,
    up_weight,
    up_bias,
    down_weight,
    down_bias,
    out_grad,
):
    t, d = tokens.shape
    half = up_weight.shape[1] // 2
    r, y = lax.axis_index("rows"), lax.axis_index("mlp")
    core = r & 1
    up_dims = n_rows.bit_length() - 2

    def flip(dim, row, m):
        if dim == "core":
            return row ^ 1, m
        if dim == "y":
            return row, m ^ 1
        return row ^ (2 << dim), m

    def bit(dim):
        return y if dim == "y" else (r >> (dim + 1)) & 1

    def swap(value, *dims):
        pairs = []
        for row in range(n_rows):
            for m in range(2):
                row2, m2 = flip(dims[0] if row & 1 == 0 else dims[-1], row, m)
                pairs.append((row * 2 + m, row2 * 2 + m2))
        return lax.ppermute(value, BOTH, pairs)

    def by_core(first, second):
        return jnp.where(core == 0, first, second)

    def after(value, *done):
        return lax.optimization_barrier((value, *done))[0]

    u0 = [0, "y"] + list(range(1, up_dims))
    u1 = ["y", 1, 0] + list(range(2, up_dims))
    q0 = ["y", 1, 0, 2] + list(range(3, up_dims))
    q1 = [0, "y", 2, 1] + list(range(3, up_dims))
    at = jnp.stack(
        [core, bit(0), by_core(0, bit(u1[1]))]
        + [by_core(bit(u0[0]), bit(u1[1])), by_core(bit(u0[2]), bit(u1[2]))]
        + [by_core(bit(u1[1]), bit(u0[0])), by_core(bit(u1[2]), bit(u0[2]))]
        + [by_core(bit(a), bit(b)) for a, b in zip(q0[:3], q1[:3])]
        + [y]
        + [by_core(bit(b), bit(a)) for a, b in zip(q0[:3], q1[:3])]
    ).astype(jnp.int32)
    place = jnp.stack([y, core]).astype(jnp.int32)
    core_s = core.reshape(1).astype(jnp.int32)
    hbm = lambda v: pltpu.with_memory_space_constraint(v, pltpu.HBM)
    vmem = lambda v: pltpu.with_memory_space_constraint(v, pltpu.VMEM)
    qkv_free, down_free = qkv_weight, down_weight
    tokens, out_grad, qkv_weight, out_weight, up_weight, down_weight = map(
        hbm, (tokens, out_grad, qkv_weight, out_weight, up_weight, down_weight)
    )

    bias = up_bias.reshape(2, half)
    vecs = jnp.concatenate(
        [
            jnp.stack([ln1_gain, ln1_bias, out_bias, ln2_gain, ln2_bias, qv_bias[0], qv_bias[1], down_bias]),
            bias,
            jnp.zeros((6, d), BF),
        ]
    )
    columns = jnp.stack([ln1_gain, ln1_bias], axis=1).astype(F32)

    w_send = swap(fetch(1 - core_s, up_weight, down_weight, bias), "y")
    joined, ctx, resid, h2, n1t, probs = attn_fwd(tokens, segment_ids, vecs, qkv_weight, out_weight, rows=512)
    gated_own, dh2_own, own_keep, own_send, gub_own = ffn_own(
        core_s, vmem(h2), out_grad, up_weight, vecs, down_weight, rows=512
    )
    w_send = after(w_send, own_send)
    w_keep = swap(w_send, "core")
    own_recv = swap(own_send, "core")
    gated_oth, dattn, dctx, oth_keep, oth_send, gub_oth, gout, vec = ffn_other(
        vmem(h2), out_grad, hbm(w_send), w_keep, vmem(dh2_own), hbm(resid), hbm(ctx), out_weight, vecs, rows=512
    )
    oth_recv = swap(oth_send, "core")
    down_oth = jnp.concatenate([w[d : d + half] for w in lax.optimization_barrier((w_send, w_keep, oth_send))[:2]])
    blocks = t // 512

    def layer_out_part(first, count, before, *ready):
        return in_part(
            layer_out_body, 512, first, count, (hbm(gated_own), hbm(after(resid, *ready)), hbm(gated_oth)),
            (down_weight, hbm(down_oth), vecs), before, 4 * half * d, "layer_out",
        )

    def in_grad_part(first, count, before, *ready):
        return in_part(
            in_grad_body, 512, first, count, (dj, tokens, hbm(after(dattn, *ready))), (qkv_free, vecs), before,
            3 * d * d, "in_grad",
        )

    block = shape((4, d // 2, half), BF)
    u_keep, u_send = on_chip(split_body, [block] * 2, at, own_keep, own_recv, oth_keep, oth_recv, name="split")
    u_recv = swap(u_send, u0[0], u1[0])
    dj, q_keep, q_send = attn_bwd(
        place, hbm(joined), hbm(after(dctx, u_keep)), hbm(probs), hbm(n1t), qkv_weight, hbm(gout), gub_own, gub_oth, vec,
        rows=512,
    )
    q_recv = swap(q_send, "core")
    u_keep, u_send = halve(at, 2, u_keep, after(u_recv, q_send))
    u_recv = swap(u_send, u0[1], u1[1])
    in_grad = in_grad_part(0, blocks // 2, None, u_keep)
    q_keep, q_send = halve(at, 7, q_keep, after(q_recv, in_grad))
    q_recv = swap(q_send, q0[0], q1[0])
    in_grad = in_grad_part(blocks // 2, blocks // 2, in_grad, q_keep)
    u_keep, u_send = halve(at, 4, u_keep, after(u_recv, in_grad))
    u_recv = swap(u_send, u0[2], u1[2])
    q_keep, q_send = halve(at, 8, q_keep, after(q_recv, u_keep))
    q_recv = swap(q_send, q0[1], q1[1])
    u_one = plus(u_keep, after(u_recv, q_keep))
    u_recv = swap(u_one, u0[3], u1[3])
    q_keep, q_send = halve(at, 9, q_keep, after(q_recv, u_one))
    q_recv = swap(q_send, q0[2], q1[2])
    layer_out = layer_out_part(0, blocks // 2, None, q_keep)
    q_one = plus(q_keep, after(q_recv, layer_out))
    for k in range(3, len(u0)):
        q_recv = swap(q_one, q0[k], q1[k])
        u_one = plus(u_one, after(u_recv, q_one))
        if k + 1 < len(u0):
            u_recv = swap(u_one, u0[k + 1], u1[k + 1])
            q_one = plus(q_one, after(q_recv, u_one))
    u_ag = swap(u_one, u0[2], u1[2])
    q_one = plus(q_one, after(q_recv, u_one))
    q_ag = swap(q_one, q0[2], q1[2])
    u_pair = jnp.concatenate([u_one, after(u_ag, q_one)], axis=0)
    u_far = swap(u_pair, u0[0], u1[1])
    u_pair_c = swap(u_pair, "core")
    q_pair = jnp.concatenate([q_one, after(q_ag, u_pair)], axis=0)
    q_ag = swap(q_pair, q0[1], q1[1])
    q_four = jnp.concatenate([q_pair, after(q_ag, u_pair)], axis=0)
    q_far = swap(q_four, q0[0], q1[0])
    q_four_c = swap(q_four, "core")
    layer_out = layer_out_part(blocks // 2, blocks // 2, layer_out, q_four)
    u_far = after(u_far, layer_out)
    u_far_c = swap(u_far, "core")
    grad_up, grad_down = finish_ffn(at, u_pair, u_far, u_pair_c, u_far_c)
    q_far = after(q_far, grad_up)
    grad_qkv, grad_qv, grad_wo, g1, c1, bo, g2, c2, gub, b2 = finish_rest(
        at, columns, q_four, q_far, q_four_c, swap(q_far, "core")
    )
    flat = lambda v: v.reshape(-1)
    return (
        layer_out, in_grad, flat(g1), flat(c1), grad_qkv, grad_qv, grad_wo, flat(bo), flat(g2), flat(c2),
        grad_up, flat(gub), grad_down, flat(b2),
    )


def solution(mesh):
    placed = (
        P(BOTH, None), P(BOTH, None), P(), P(), P(), P(), P(), P(), P(), P(),
        P(None, "mlp"), P("mlp"), P("mlp", None), P(), P(BOTH, None),
    )
    return jax.shard_map(
        functools.partial(local, mesh.shape["rows"]),
        mesh=mesh,
        in_specs=placed,
        out_specs=(
            P(BOTH, None), P(BOTH, None), P(), P(), P(), P(), P(), P(), P(), P(),
            P(None, "mlp"), P("mlp"), P("mlp", None), P(),
        ),
        check_vma=False,
    )
```
